32 devices in a mesh: batch: 8 (over z, y), tm: 4 (over x, core).
Axes of the slice: x: 2, y: 2, z: 4, core: 2. Of those that a mesh axis runs over, the one named last changes fastest.
Arguments:
- patches: bfloat16 [32, 1024, 768], P('batch', 'tm'), may hold values from -6 to 6
- segment_ids: int32 [32, 1024], P('batch', 'tm'), may hold values from 0 to 4, as said below
- mask_flags: int32 [32, 1024], P('batch', 'tm'), may hold values 0 or 1
- cotangent: bfloat16 [32, 1024, 768], P('batch', 'tm'), may hold values from -6 to 6
- mask_embed: float32 [768], P(('batch', 'tm')), may hold values from -6 to 6
- norm_gain: float32 [2, 768], P(None, ('batch', 'tm')), may hold values from 0.1 to 1.9
- norm_shift: float32 [2, 768], P(None, ('batch', 'tm')), may hold values from -3 to 3
- qkv_weight: float32 [768, 2304], P(('batch', 'tm')), may hold values from -0.3125 to 0.3125
- qv_bias: float32 [2, 768], P(None, ('batch', 'tm')), may hold values from -3 to 3
- out_weight: float32 [768, 768], P(('batch', 'tm')), may hold values from -1.75 to 1.75
- branch_bias: float32 [2, 768], P(None, ('batch', 'tm')), may hold values from -3 to 3
- up_weight: float32 [768, 3072], P(('batch', 'tm')), may hold values from -0.21875 to 0.21875
- up_bias: float32 [3072], P(('batch', 'tm')), may hold values from -3 to 3
- down_weight: float32 [3072, 768], P(('batch', 'tm')), may hold values from -0.109375 to 0.109375
Outputs:
- output: float32 [32, 1024, 768], P('batch', 'tm')
- patch_grad: float32 [32, 1024, 768], P('batch', 'tm')
- mask_embed_grad: float32 [768], P(('batch', 'tm'))
- norm_gain_grad: float32 [2, 768], P(None, ('batch', 'tm'))
- norm_shift_grad: float32 [2, 768], P(None, ('batch', 'tm'))
- qkv_weight_grad: float32 [768, 2304], P(('batch', 'tm'))
- qv_bias_grad: float32 [2, 768], P(None, ('batch', 'tm'))
- out_weight_grad: float32 [768, 768], P(('batch', 'tm'))
- branch_bias_grad: float32 [2, 768], P(None, ('batch', 'tm'))
- up_weight_grad: float32 [768, 3072], P(('batch', 'tm'))
- up_bias_grad: float32 [3072], P(('batch', 'tm'))
- down_weight_grad: float32 [3072, 768], P(('batch', 'tm'))
The draws below stay inside these ranges and needn't reach their ends.
Inputs may be any that keep to these rules, and one draw needn't show every extreme that they name: `segment_ids`: in each row the ids run 1, 2, 3, 4 in that order, the runs of 1 and 2 possibly empty, followed by 1 to 128 positions of id 0 (padding).
All inputs are finite; a program needn't handle non-finite values. No bound on the sum of `mask_flags` on one device may be relied on, other than what follows from the above.
Results may differ from the reference program's by a relative error of at most 0.017.
The reference program's roundings to bfloat16 on the way count: a program that leaves them out, or rounds other values in their place, can miss the bound.
Values may be sent and summed in bfloat16 or wider, within the bound.
A program may use at most 320 MiB of HBM per device.

```python
import math
import jax
import jax.numpy as jnp
from jax import lax

D = 768
HEADS = 12
FF = 3072
SEQ = 1024
ROWS = 32
SPAN = 256


def draw_segment_ids(key, part):
    key = jax.random.fold_in(key, 11)
    keys = jax.random.split(key, 4)
    start = jax.random.randint(keys[0], (ROWS, 1), 1, SPAN)
    padding = jax.random.randint(keys[1], (ROWS, 1), 1, SPAN // 2 + 1)
    finish = jax.random.randint(keys[2], (ROWS, 1), 3 * SPAN + 1, SEQ - padding)
    cut = jax.random.randint(keys[3], (ROWS, 1), 0, start + 1)
    places = jnp.arange(SEQ, dtype=jnp.int32)[None, :]
    ids = jnp.where(places < cut, 1, jnp.where(places < start, 2, jnp.where(places < finish, 3, jnp.where(places < SEQ - padding, 4, 0))))
    return ids.astype(jnp.int32)


def place_ends(values, stream_key, low, top_value):
    longest = values.shape.index(max(values.shape))
    spots = []
    for shift in (0, 1):
        where = [jax.random.randint(jax.random.fold_in(stream_key, axis), (), 0, length) for axis, length in enumerate(values.shape)]
        where[longest] = (where[longest] + shift) % values.shape[longest]
        spots.append(tuple(where))
    return values.at[spots[0]].set(low).at[spots[1]].set(top_value)


def steps_of(rng, dims, cuts, smallest, high):
    factor_of = 1.0
    for axis_at, shards_of in cuts:
        draws = jax.random.uniform(jax.random.fold_in(jax.random.fold_in(rng, 6), axis_at), (shards_of,), jnp.float32, smallest / len(cuts), high / len(cuts))
        factor_of = factor_of * jnp.repeat(jnp.exp(draws), dims[axis_at] // shards_of).reshape((-1,) + (1,) * (len(dims) - 1 - axis_at))
    return factor_of


def noise(own_key, extent, width, limit, cuts=(), kind=jnp.bfloat16):
    array = width * jax.random.normal(own_key, extent, jnp.float32)
    if cuts:
        array = array * steps_of(own_key, extent, cuts, -0.22, 0.18)
    return jnp.clip(array, -limit, limit).astype(kind)


def setup_inputs(seed: int = 0) -> dict:
    key_of = jax.random.split(jax.random.key(seed), 15)
    return {
        "patches": noise(key_of[0], (ROWS, SEQ, D), 1.0, 6.0, ((0, 8), (1, 4))),
        "segment_ids": draw_segment_ids(jax.random.fold_in(key_of[14], 71), 0),
        "mask_flags": place_ends((jax.random.randint(key_of[2], (ROWS, SEQ), 0, 5) < 1).astype(jnp.int32), jax.random.fold_in(key_of[2], 1), 0, 1),
        "cotangent": noise(key_of[3], (ROWS, SEQ, D), 1.0, 6.0, ((0, 8), (1, 4))),
        "mask_embed": noise(key_of[4], (D,), 1.0, 6.0, ((0, 32),), jnp.float32),
        "norm_gain": jnp.clip(1.0 + 0.18 * jax.random.normal(key_of[5], (2, D), jnp.float32), 0.1, 1.9),
        "norm_shift": noise(key_of[6], (2, D), 0.3, 3.0, ((1, 32),), jnp.float32),
        "qkv_weight": noise(key_of[7], (D, 3 * D), (D // 2) ** -0.5, 0.3125, ((0, 32),), jnp.float32),
        "qv_bias": noise(key_of[8], (2, D), 0.3, 3.0, ((1, 32),), jnp.float32),
        "out_weight": noise(key_of[9], (D, D), (D // 64) ** -0.5, 1.75, ((0, 32),), jnp.float32),
        "branch_bias": noise(key_of[10], (2, D), 0.3, 3.0, ((1, 32),), jnp.float32),
        "up_weight": noise(key_of[11], (D, FF), D ** -0.5, 0.21875, ((0, 32),), jnp.float32),
        "up_bias": noise(key_of[12], (FF,), 0.3, 3.0, ((0, 32),), jnp.float32),
        "down_weight": noise(key_of[13], (FF, D), FF ** -0.5, 0.109375, ((0, 32),), jnp.float32),
    }


@jax.custom_vjp
def low(v):
    return lax.optimization_barrier(v.astype(jnp.bfloat16)).astype(jnp.float32)

@jax.custom_vjp
def low_back(v):
    return v

def low_keep(v):
    return (low(v), None)

def low_pass(kept, grad):
    return (grad,)

def back_keep(v):
    return (v, None)

def back_low(kept, grad):
    return (low(grad),)
low.defvjp(low_keep, low_pass)
low_back.defvjp(back_keep, back_low)
EPS = 1e-06
NEGATIVE = -1e+30

def layer_norm(hidden, gain, shift):
    center = hidden - lax.optimization_barrier(jnp.mean(hidden, -1, keepdims=True))
    spread = lax.optimization_barrier(jnp.mean(center * center, -1, keepdims=True))
    return center * lax.rsqrt(spread + EPS) * gain + shift

def gelu_exact(values):
    return jax.nn.gelu(values, approximate=False)

def attend_row(items):
    queries, keys, values, segments = items
    head_dim = D // HEADS
    scale = 1.0 / math.sqrt(head_dim)
    query_heads = queries.reshape(SEQ, HEADS, head_dim)
    key_heads = keys.reshape(SEQ, HEADS, head_dim)
    value_heads = values.reshape(SEQ, HEADS, head_dim)
    scores = jnp.einsum('qhd,khd->hqk', query_heads, key_heads, precision=lax.Precision.HIGHEST) * scale
    scores = low_back(scores)
    allowed = (segments[:, None] == segments[None, :])[None]
    scores = jnp.where(allowed, scores, NEGATIVE)
    probs = low(jax.nn.softmax(scores, axis=-1))
    mixed = jnp.einsum('hqk,khd->qhd', probs, value_heads, precision=lax.Precision.HIGHEST)
    return mixed.reshape(SEQ, D)

def forward(inputs, params, segments, flags):
    mask_embed, norm_gain, norm_shift, qkv_weight, qv_bias, out_weight, branch_bias, up_weight, up_bias, down_weight = [low(item) for item in params]
    highest = lax.Precision.HIGHEST
    start = jnp.where((flags == 1)[..., None], mask_embed, inputs)
    first_in = low(layer_norm(start, norm_gain[0], norm_shift[0]))
    projected = jnp.einsum('gsd,de->gse', first_in, qkv_weight, precision=highest)
    queries = low_back(low(projected[..., :D] + qv_bias[0]))
    keys = low_back(low(projected[..., D:2 * D]))
    values = low_back(low(projected[..., 2 * D:] + qv_bias[1]))
    mixed = lax.map(jax.checkpoint(attend_row), (queries, keys, values, segments))
    mixed = low_back(low(mixed))
    branch = low_back(jnp.einsum('gsd,de->gse', mixed, out_weight, precision=highest) + branch_bias[0])
    middle = start + branch
    second_in = low(layer_norm(middle, norm_gain[1], norm_shift[1]))
    hidden_pre = low_back(jnp.einsum('gsd,df->gsf', second_in, up_weight, precision=highest) + up_bias)
    hidden_act = low_back(low(gelu_exact(hidden_pre)))
    result = low_back(jnp.einsum('gsf,fd->gsd', hidden_act, down_weight, precision=highest) + branch_bias[1])
    return middle + result

def reference(patches, segment_ids, mask_flags, cotangent, mask_embed, norm_gain, norm_shift, qkv_weight, qv_bias, out_weight, branch_bias, up_weight, up_bias, down_weight):
    params = (mask_embed, norm_gain, norm_shift, qkv_weight, qv_bias, out_weight, branch_bias, up_weight, up_bias, down_weight)
    groups = ROWS // 4
    patch_groups = patches.astype(jnp.float32).reshape(groups, 4, SEQ, D)
    segment_groups = segment_ids.reshape(groups, 4, SEQ)
    flag_groups = mask_flags.reshape(groups, 4, SEQ)
    cotangent_groups = cotangent.astype(jnp.float32).reshape(groups, 4, SEQ, D)

    def step(totals, items):
        inputs, segments, flags, upstream = items

        def local(inputs_now, params_now):
            return forward(inputs_now, params_now, segments, flags)
        result, pull = jax.vjp(local, inputs, params)
        input_grad, param_grads = pull(upstream)
        totals = tuple((total + grad for total, grad in zip(totals, param_grads)))
        return (totals, (result, input_grad))
    zeros = tuple((jnp.zeros_like(item) for item in params))
    totals, (results, input_grads) = lax.scan(step, zeros, (patch_groups, segment_groups, flag_groups, cotangent_groups))
    embed_grad, gain_grad, shift_grad, qkv_grad, qv_grad, out_grad, branch_grad, up_grad, up_bias_grad, down_grad = totals
    return (results.reshape(ROWS, SEQ, D), input_grads.reshape(ROWS, SEQ, D), embed_grad, gain_grad, shift_grad, qkv_grad, qv_grad, out_grad, branch_grad, up_grad, up_bias_grad, down_grad)
```

```python
import functools
import math

import jax
import jax.numpy as jnp
from jax import lax
from jax.experimental import pallas as pl
from jax.experimental.pallas import tpu as pltpu
from jax.sharding import PartitionSpec as P

HEADS = 12
EPS = 1e-06
FAR = -1e30
LOG2E = math.log2(math.e)
BF = jnp.bfloat16
F32 = jnp.float32
MESH = pl.DeviceIdType.MESH
HBM = pl.BlockSpec(memory_space=pl.ANY)
SLOPE = 0.36
TAIL = (
    0.14371305209487725,
    0.14177235930704382,
    0.1397197719471602,
    0.026547986328787306,
    0.18095585464885458,
    -0.1797659534284226,
    0.04705662553510592,
)


def nn(left, right):
    return jnp.dot(left, right, preferred_element_type=F32)


def nt(left, right):
    return lax.dot_general(left, right, (((1,), (1,)), ((), ())), preferred_element_type=F32)


def tn(left, right):
    return lax.dot_general(left, right, (((0,), (0,)), ((), ())), preferred_element_type=F32)


def gelu_and_slope(pre):
    size = jnp.abs(pre)
    t = 1.0 / (1.0 + SLOPE * size)
    poly = jnp.full_like(t, TAIL[-1])
    for term in TAIL[-2::-1]:
        poly = poly * t + term
    bell = jnp.exp2(pre * pre * (-0.5 * LOG2E))
    lower = poly * t * bell
    cdf = jnp.where(pre >= 0, 1.0 - lower, lower)
    return pre * cdf, cdf + pre * bell * (1.0 / math.sqrt(2.0 * math.pi))


def moments(hidden):
    center = hidden - jnp.mean(hidden, -1, keepdims=True)
    return center, lax.rsqrt(jnp.mean(center * center, -1, keepdims=True) + EPS)


def norm_back(normed, rate, gain, grad):
    scaled = grad * gain
    shared = jnp.mean(scaled * normed, -1, keepdims=True)
    return rate * (scaled - jnp.mean(scaled, -1, keepdims=True) - normed * shared)


def column_sum(values):
    return jnp.sum(values, 0, keepdims=True)


class Place:
    def __init__(self, deep):
        batch, tm = lax.axis_index("batch"), lax.axis_index("tm")
        self.deep = deep
        self.batch, self.tm = batch, tm
        self.z, self.y = batch // 2, batch % 2
        self.x, self.c = tm // 2, tm % 2

    def device(self, z=None, y=None, x=None, c=None):
        z = self.z if z is None else z
        y = self.y if y is None else y
        x = self.x if x is None else x
        c = self.c if c is None else c
        return (z * 2 + y, x * 2 + c)

    def mate(self, k):
        return (self.x + k // 2) % 2 * 2 + (self.c + k % 2) % 2

    def enter(self):
        barrier = pltpu.get_barrier_semaphore()
        others = [self.device(c=1 - self.c), self.device(x=1 - self.x), self.device(y=1 - self.y)]
        others.append(self.device(x=1 - self.x, c=1 - self.c))
        others += [self.device(z=(self.z + d) % self.deep) for d in range(1, self.deep)]
        for other in others:
            pl.semaphore_signal(barrier, inc=1, device_id=other, device_id_type=MESH)
        pl.semaphore_wait(barrier, len(others))


def remote(src, dst, send, recv, device):
    return pltpu.make_async_remote_copy(
        src_ref=src, dst_ref=dst, send_sem=send, recv_sem=recv, device_id=device, device_id_type=MESH
    )


class Route:
    def __init__(self, place, order, crossed):
        self.place, self.order, self.crossed = place, order, crossed
        c = place.c
        self.own = {
            "z": place.z,
            "p": c * place.y + (1 - c) * place.x if crossed else place.x,
            "q": c * place.x + (1 - c) * place.y if crossed else place.y,
        }
        self.size = {"z": place.deep, "p": 2, "q": 2}
        self.sizes = [self.size[axis] for axis in order]

    def shifted(self, shifts):
        at = {a: (self.own[a] + s % self.size[a]) % self.size[a] for a, s in zip(self.order, shifts)}
        c = self.place.c
        if self.crossed:
            return at["z"], c * at["p"] + (1 - c) * at["q"], c * at["q"] + (1 - c) * at["p"]
        return at["z"], at["q"], at["p"]

    def device(self, shifts):
        z, y, x = self.shifted(shifts)
        return self.place.device(z=z, y=y, x=x)

    def chip(self, shifts):
        z, y, x = self.shifted(shifts)
        return (z * 2 + y) * 2 + x

    def offsets(self, upto):
        found = [()]
        for stage, size in enumerate(self.sizes):
            found = [f + (o,) for f in found for o in range(size if stage < upto else 1)]
        return found

    def index(self, offset):
        flat = 0
        for o, size in zip(offset, self.sizes):
            flat = flat * size + o
        return flat


class Gather:
    def __init__(self, place, route, shard, joined, full, local, sends, recvs):
        self.place, self.route = place, route
        self.shard, self.joined, self.full = shard, joined, full
        self.local, self.sends, self.recvs = local, sends, recvs
        self.rows = shard.shape[0]
        self.half = shard.shape[1] // 2
        self.sent = []
        self.count = 0

    def columns(self, c):
        return pl.ds(pl.multiple_of(c * self.half, 128), self.half)

    def region(self, chip, c):
        rows = 2 * self.rows
        return self.full.at[pl.ds(pl.multiple_of(chip * rows, 16), rows), self.columns(c)]

    def ship(self, src, dst, recv, device):
        copy = remote(src, dst, self.sends.at[self.count], recv, device)
        copy.start()
        self.count += 1
        self.sent.append(copy)

    def join(self):
        place = self.place
        own = pl.ds(pl.multiple_of(place.c * self.rows, 8), self.rows)
        self.mine = pltpu.make_async_copy(
            self.shard.at[:, self.columns(place.c)], self.joined.at[own], self.local
        )
        self.mine.start()
        self.pair = self.recvs.at[0]
        self.ship(
            self.shard.at[:, self.columns(1 - place.c)],
            self.joined.at[own],
            self.recvs.at[0],
            place.device(c=1 - place.c),
        )

    def arrive(self, offset, stage):
        route, place = self.route, self.place
        chip = route.chip([-o for o in offset])
        block = self.region(chip, place.c)
        for later in range(stage + 1, 3):
            for d in range(1, route.sizes[later]):
                shifts = [0, 0, 0]
                shifts[later] = d
                seen = list(offset)
                seen[later] = d
                self.ship(block, block, self.recvs.at[1 + route.index(seen)], route.device(shifts))
        total = math.prod(route.sizes)
        self.ship(
            block,
            block,
            self.recvs.at[1 + total + route.index(offset)],
            place.device(c=1 - place.c),
        )

    def first(self):
        place = self.place
        self.mine.wait()
        own = pl.ds(pl.multiple_of((1 - place.c) * self.rows, 8), self.rows)
        self.sent[0].wait_send()
        remote(
            self.joined.at[own], self.joined.at[own], self.sends.at[0], self.recvs.at[0], place.device(c=1 - place.c)
        ).wait_recv()
        chip = self.route.chip([0, 0, 0])
        self.region(chip, place.c)[...] = self.joined[...].astype(BF)
        self.arrive((0, 0, 0), -1)

    def stage(self, stage):
        route = self.route
        for offset in route.offsets(stage + 1):
            if offset[stage] == 0:
                continue
            block = self.region(route.chip([-o for o in offset]), self.place.c)
            remote(
                block, block, self.sends.at[0], self.recvs.at[1 + route.index(offset)], self.place.device()
            ).wait_recv()
            self.arrive(offset, stage)

    def finish(self):
        route = self.route
        total = math.prod(route.sizes)
        for offset in route.offsets(3):
            block = self.region(route.chip([-o for o in offset]), 1 - self.place.c)
            remote(
                block,
                block,
                self.sends.at[0],
                self.recvs.at[1 + total + route.index(offset)],
                self.place.device(),
            ).wait_recv()

    def drain(self):
        for copy in self.sent[1:]:
            copy.wait_send()


def sum_vectors(place, held, slots, sends, recvs):
    stages = [
        [place.device(c=1 - place.c)],
        [place.device(x=1 - place.x)],
        [place.device(y=1 - place.y)],
        [place.device(z=(place.z + d) % place.deep) for d in range(1, place.deep)],
    ]
    slot = 0
    for stage, others in enumerate(stages):
        copies = []
        for other in others:
            copies.append(remote(held.at[stage], slots.at[slot], sends.at[slot], recvs.at[slot], other))
            copies[-1].start()
            slot += 1
        total = held[stage]
        for copy in copies:
            copy.wait()
        for back in range(len(others)):
            total = total + slots[slot - len(others) + back]
        held[stage + 1] = total


def code_columns(code, source):
    turned = jnp.transpose(code[source])
    flags = jnp.concatenate([turned[:, 0:1], turned[:, 1:2]], 0)
    clips = jnp.concatenate([turned[:, 2:3], turned[:, 3:4]], 0)
    return flags, clips


def forward_kernel(
    deep,
    patches,
    cotangent,
    code_in,
    small_in,
    shard_qkv,
    shard_out,
    shard_up,
    shard_down,
    o_qkv,
    o_out,
    o_up,
    o_down,
    o_small,
    o_x,
    o_cot,
    o_code,
    o_first,
    o_q,
    o_k,
    o_v,
    o_mixed,
    o_second,
    o_rate,
    o_middle,
    o_act,
    o_slope,
    o_expon,
    o_result,
    w_qkv,
    w_out,
    w_up,
    w_down,
    j_qkv,
    j_out,
    j_up,
    j_down,
    small,
    small_slots,
    x,
    code,
    first,
    q,
    k,
    v,
    mixed,
    second,
    rate,
    middle,
    expon,
    act,
    slope,
    result,
    q_code,
    k_code,
    join_sems,
    gather_sends,
    gather_recvs,
    small_sends,
    small_recvs,
    row_sends,
    row_recvs,
    local_sems,
    expon_sems,
    act_sems,
):
    place = Place(deep)
    span, width = patches.shape[1:]
    rows = x.shape[0]
    sources = rows // span
    half = width // HEADS
    pairs = HEADS // 2
    inner = w_up.shape[1]
    chunks = inner // width

    near = pltpu.make_async_copy(small_in, small.at[0], local_sems.at[0])
    near.start()
    place.enter()

    kinds = ((patches, x), (code_in, code), (cotangent, o_cot))

    def own_part(kind):
        src, dst = kinds[kind]
        to = dst.at[pl.ds(pl.multiple_of(place.tm * span, span), span)] if kind != 1 else dst.at[place.tm]
        return pltpu.make_async_copy(src.at[place.tm], to, local_sems.at[1 + kind])

    def row_copy(kind, step, to):
        src, dst = kinds[kind]
        here = dst.at[pl.ds(pl.multiple_of(place.tm * span, span), span)] if kind != 1 else dst.at[place.tm]
        return remote(
            src.at[to], here, row_sends.at[kind, step], row_recvs.at[kind, step], (place.batch, to)
        )

    def row_wait(kind, step):
        src, dst = kinds[kind]
        source = place.mate(step)
        there = dst.at[pl.ds(pl.multiple_of(source * span, span), span)] if kind != 1 else dst.at[source]
        remote(
            there, there, row_sends.at[kind, step], row_recvs.at[kind, step], (place.batch, source)
        ).wait_recv()

    zpq = Route(place, "zpq", True)
    pzq = Route(place, "pzq", False)
    gathers = [
        Gather(place, route, shard, joined, full, join_sems.at[i], gather_sends.at[i], gather_recvs.at[i])
        for i, (route, shard, joined, full) in enumerate(
            (
                (zpq, shard_qkv, j_qkv, w_qkv),
                (zpq, shard_out, j_out, w_out),
                (zpq, shard_up, j_up, w_up),
                (pzq, shard_down, j_down, w_down),
            )
        )
    ]
    for gather in gathers:
        gather.join()
    gathers[0].first()
    for kind in (1, 0):
        own_part(kind).start()
        for step in range(1, sources):
            row_copy(kind, step, place.mate(step)).start()
    near.wait()
    sum_vectors(place, small, small_slots, small_sends, small_recvs)
    gathers[0].stage(0)
    gathers[0].stage(1)
    for gather in gathers[1:]:
        gather.first()
    own_part(2).start()
    for step in range(1, sources):
        row_copy(2, step, place.mate(step)).start()
    gathers[0].stage(2)
    gathers[0].finish()

    vectors = small.at[4]
    lane = lax.broadcasted_iota(jnp.int32, (1, 2 * half), 1)
    low = lane < half
    own_lanes = [low.astype(F32), 1.0 - low.astype(F32)]

    for kind in (1, 0):
        own_part(kind).wait()

    @pl.loop(0, sources)
    def _(step):
        @pl.when(step > 0)
        def _():
            row_wait(1, step)
            row_wait(0, step)

        source = place.mate(step)
        at = pl.ds(pl.multiple_of(source * span, span), span)
        flags, clips = code_columns(code, source)
        start = jnp.where(flags == 1.0, vectors[0:1, :], x[at, :].astype(F32))
        middle[at, :] = start
        center, speed = moments(start)
        normed = (center * speed * vectors[1:2, :] + vectors[3:4, :]).astype(BF)
        first[at, :] = normed
        q[at, :] = (nn(normed, w_qkv[:, 0:width]) + vectors[5:6, :]).astype(BF) * (1.0 / math.sqrt(half))
        k[at, :] = nn(normed, w_qkv[:, width : 2 * width]).astype(BF)
        v[at, :] = (nn(normed, w_qkv[:, 2 * width :]) + vectors[6:7, :]).astype(BF)
        clip_lane = lax.broadcasted_iota(jnp.int32, (span, 2 * half), 1).astype(F32)
        for h in range(2):
            base = float(half * (1 - h))
            same = clip_lane - base == clips
            named = jnp.logical_and(clip_lane >= base, clip_lane < base + 5.0)
            q_code[h, at, :] = jnp.where(same, 1.0, 0.0).astype(BF)
            k_code[h, at, :] = jnp.where(jnp.logical_and(named, jnp.logical_not(same)), FAR, 0.0).astype(BF)

    for gather in gathers[1:]:
        gather.stage(0)
    block = min(rows, 512)

    def expon_copy(p):
        return pltpu.make_async_copy(expon.at[p % 2], o_expon.at[pl.ds(2 * p, 2)], expon_sems.at[p % 2])

    def attend(p):
        lanes = pl.ds(pl.multiple_of(p * 2 * half, 128), 2 * half)

        @pl.when(p >= 2)
        def _():
            expon_copy(p - 2).wait()

        slot = p % 2
        keys, values = [], []
        for h in range(2):
            mask = own_lanes[h].astype(BF)
            keys.append(k[:, lanes] * mask + k_code[h])
            values.append(v[:, lanes] * mask + own_lanes[1 - h].astype(BF))
        for part in range(rows // block):
            at = pl.ds(part * block, block)
            mixes = []
            for h in range(2):
                query = q[at, lanes] * own_lanes[h].astype(BF) + q_code[h, at, :]
                scores = nt(query, keys[h])
                peak = jnp.max(scores, -1, keepdims=True)
                weights = jnp.exp2((scores - peak) * LOG2E).astype(BF)
                expon[slot, h, at, :] = weights
                mixes.append(nn(weights, values[h]))
            top = jnp.where(low, mixes[0], mixes[1])
            totals = pltpu.roll(jnp.where(low, mixes[1], mixes[0]), half, 1)
            speed = 1.0 / totals
            rate[at, lanes] = speed
            mixed[at, lanes] = (top * speed).astype(BF)
        expon_copy(p).start()

    pl.loop(0, pairs)(attend)
    for stage in (1, 2):
        for gather in gathers[1:]:
            gather.stage(stage)
    for gather in gathers[1:]:
        gather.finish()

    def act_copies(step, j, at):
        slot = step % 2
        return (
            pltpu.make_async_copy(act.at[slot, j], o_act.at[j, at], act_sems.at[0, slot, j]),
            pltpu.make_async_copy(slope.at[slot, j], o_slope.at[j, at], act_sems.at[1, slot, j]),
        )

    def feed(step):
        source = place.mate(sources - 1 - step)
        at = pl.ds(pl.multiple_of(source * span, span), span)
        hidden = middle[at, :] + nn(mixed[at, :], w_out[...]) + vectors[7:8, :]
        middle[at, :] = hidden
        center, speed = moments(hidden)
        normed = (center * speed * vectors[2:3, :] + vectors[4:5, :]).astype(BF)
        second[at, :] = normed
        total = hidden + vectors[8:9, :]
        for j in range(chunks):

            @pl.when(step >= 2)
            def _():
                for copy in act_copies(step - 2, j, at):
                    copy.wait()

            columns = pl.ds(j * width, width)
            pre = nn(normed, w_up[:, columns]) + vectors[9 + j : 10 + j, :]
            value, steep = gelu_and_slope(pre)
            value = value.astype(BF)
            act[step % 2, j] = value
            slope[step % 2, j] = steep.astype(BF)
            for copy in act_copies(step, j, at):
                copy.start()
            total = total + nn(value, w_down[columns, :])
        result[step] = total.astype(BF)

        @pl.when(step < sources - 1)
        def _():
            remote(
                result.at[step],
                o_result.at[place.tm],
                row_sends.at[3, sources - 1 - step],
                row_recvs.at[3, sources - 1 - step],
                (place.batch, source),
            ).start()

    pl.loop(0, sources)(feed)
    own_result = pltpu.make_async_copy(result.at[sources - 1], o_result.at[place.tm], local_sems.at[0])
    own_result.start()
    kept = [
        (w_qkv, o_qkv),
        (w_out, o_out),
        (w_up, o_up),
        (w_down, o_down),
        (vectors, o_small),
        (x, o_x),
        (code, o_code),
        (first, o_first),
        (q, o_q),
        (k, o_k),
        (v, o_v),
        (mixed, o_mixed),
        (second, o_second),
        (rate, o_rate),
        (middle, o_middle),
    ]
    copies = [pltpu.make_async_copy(src, dst, local_sems.at[4 + i]) for i, (src, dst) in enumerate(kept)]
    for copy in copies:
        copy.start()
    own_result.wait()
    own_part(2).wait()
    for p in (pairs - 2, pairs - 1):
        expon_copy(p).wait()
    for step in (sources - 2, sources - 1):
        source = place.mate(sources - 1 - step)
        at = pl.ds(pl.multiple_of(source * span, span), span)
        for j in range(chunks):
            for copy in act_copies(step, j, at):
                copy.wait()
    for step in range(1, sources):
        row_wait(2, step)
        remote(
            result.at[0],
            o_result.at[place.mate(step)],
            row_sends.at[3, step],
            row_recvs.at[3, step],
            place.device(),
        ).wait_recv()
        for kind in (0, 1, 2):
            row_copy(kind, step, place.mate(step)).wait_send()
        remote(
            result.at[0], o_result.at[place.tm], row_sends.at[3, step], row_recvs.at[3, step], place.device()
        ).wait_send()
    for copy in copies:
        copy.wait()
    for gather in gathers:
        gather.drain()


def forward(deep, patches, cotangent, code, small, qkv, out, up, down):
    sources, span, width = patches.shape
    rows = sources * span
    chips = deep * 4
    inner = up.shape[1]
    chunks = inner // width
    shape = jax.ShapeDtypeStruct
    shards = (qkv, out, up, down)
    fulls = [(2 * chips * s.shape[0], s.shape[1]) for s in shards]
    plane = (rows, width)
    outs = [shape(f, BF) for f in fulls]
    outs += [shape(small.shape, F32), shape(plane, BF), shape(plane, BF), shape(code.shape, F32)]
    outs += [shape(plane, BF)] * 6 + [shape(plane, F32)] * 2
    outs += [shape((chunks, rows, width), BF)] * 2
    outs += [shape((HEADS, rows, rows), BF), shape(patches.shape, BF)]
    scratch = [pltpu.VMEM(f, BF) for f in fulls]
    scratch += [pltpu.VMEM((2 * s.shape[0], s.shape[1] // 2), F32) for s in shards]
    scratch += [
        pltpu.VMEM((5,) + small.shape, F32),
        pltpu.VMEM((2 + deep,) + small.shape, F32),
        pltpu.VMEM(plane, BF),
        pltpu.VMEM(code.shape, F32),
    ]
    scratch += [pltpu.VMEM(plane, BF)] * 6 + [pltpu.VMEM(plane, F32)] * 2
    scratch += [
        pltpu.VMEM((2, 2, rows, rows), BF),
        pltpu.VMEM((2, chunks, span, width), BF),
        pltpu.VMEM((2, chunks, span, width), BF),
        pltpu.VMEM((sources, span, width), BF),
        pltpu.VMEM((2, rows, 128), BF),
        pltpu.VMEM((2, rows, 128), BF),
    ]
    dma = pltpu.SemaphoreType.DMA
    scratch += [
        dma((4,)),
        dma((4, 1 + 2 * chips)),
        dma((4, 1 + 2 * chips)),
        dma((2 + deep,)),
        dma((2 + deep,)),
        dma((4, sources)),
        dma((4, sources)),
        dma((20,)),
        dma((2,)),
        dma((2, 2, chunks)),
    ]
    return pl.pallas_call(
        functools.partial(forward_kernel, deep),
        out_shape=outs,
        in_specs=[HBM] * 8,
        out_specs=[HBM] * len(outs),
        scratch_shapes=scratch,
        compiler_params=pltpu.CompilerParams(
            collective_id=0, has_side_effects=True, vmem_limit_bytes=62 * 2**20
        ),
        name="forward",
    )(patches, cotangent, code, small, qkv, out, up, down)


class Scatter:
    def __init__(self, place, route, held, slots, final, sends, recvs):
        self.place, self.route = place, route
        self.held, self.slots, self.final = held, slots, final
        self.sends, self.recvs = sends, recvs
        self.rows = slots.shape[1]
        self.sent = []

    def region(self, shifts):
        return pl.ds(pl.multiple_of(self.route.chip(shifts) * self.rows, 16), self.rows)

    def parts(self, stage):
        route = self.route
        for d in range(1, route.sizes[stage]):
            for earlier in route.offsets(stage):
                offset = list(earlier)
                offset[stage] = d
                back = [-o for o in earlier]
                yield d, back, route.index(offset) - 1

    def send(self, stage):
        for d, back, slot in self.parts(stage):
            shifts = list(back)
            shifts[stage] = d
            to = [0, 0, 0]
            to[stage] = d
            copy = remote(
                self.held.at[self.region(shifts)],
                self.slots.at[slot],
                self.sends.at[slot],
                self.recvs.at[slot],
                self.route.device(to),
            )
            copy.start()
            self.sent.append(copy)

    def add(self, stage):
        found = {}
        for _, back, slot in self.parts(stage):
            remote(
                self.slots.at[slot],
                self.slots.at[slot],
                self.sends.at[slot],
                self.recvs.at[slot],
                self.place.device(),
            ).wait_recv()
            found.setdefault(tuple(back), []).append(slot)
        for back, slots in found.items():
            at = self.region(back)
            total = self.held[at, :].astype(F32)
            for slot in slots:
                total = total + self.slots[slot].astype(F32)
            if stage == 0:
                self.final[...] = total
            else:
                self.held[at, :] = total.astype(BF)

    def drain(self):
        for copy in self.sent:
            copy.wait_send()


def backward_kernel(
    deep,
    i_qkv,
    i_out,
    i_up,
    i_down,
    i_small,
    i_x,
    i_cot,
    i_code,
    i_first,
    i_q,
    i_k,
    i_v,
    i_mixed,
    i_second,
    i_rate,
    i_middle,
    i_act,
    i_slope,
    i_expon,
    o_qkv,
    o_out,
    o_up,
    o_down,
    o_small,
    o_patch,
    w_qkv,
    w_out,
    w_up,
    w_down,
    upstream,
    second,
    gathered,
    middle,
    expon,
    score_grad,
    trio,
    rate,
    mixed,
    staged,
    h_qkv,
    h_out,
    h_up,
    h_down,
    s_qkv,
    s_out,
    s_up,
    s_down,
    f_qkv,
    f_out,
    f_up,
    f_down,
    vectors,
    code,
    small,
    small_slots,
    patch,
    load_sems,
    chunk_sems,
    pair_sems,
    hand_sends,
    hand_recvs,
    scatter_sends,
    scatter_recvs,
    final_sends,
    final_recvs,
    small_sends,
    small_recvs,
    row_sends,
    row_recvs,
    local_sems,
):
    place = Place(deep)
    rows, width = upstream.shape
    sources, span = patch.shape[:2]
    half = width // HEADS
    pairs = HEADS // 2
    chunks = i_act.shape[0]
    part = width // 2
    first = second
    mixed_grad = upstream
    first_grad = gathered

    loads = [
        pltpu.make_async_copy(src, dst, load_sems.at[i])
        for i, (src, dst) in enumerate(
            (
                (i_cot, upstream),
                (i_second, second),
                (i_middle, middle),
                (i_small, vectors),
                (i_code, code),
                (i_out, w_out),
                (i_qkv, w_qkv),
            )
        )
    ]

    def chunk_loads(j):
        slot = j % 2
        columns = pl.ds(pl.multiple_of(j * width, 128), width)
        moves = (
            (i_down.at[columns], w_down.at[slot]),
            (i_up.at[:, columns], w_up.at[slot]),
            (i_act.at[j], expon.at[slot, 0, :, pl.ds(0, width)]),
            (i_slope.at[j], expon.at[slot, 1, :, pl.ds(0, width)]),
        )
        return [pltpu.make_async_copy(src, dst, chunk_sems.at[slot, n]) for n, (src, dst) in enumerate(moves)]

    def pair_loads(p):
        slot = p % 2
        lanes = pl.ds(pl.multiple_of(p * 2 * half, 128), 2 * half)
        moves = (
            (i_expon.at[pl.ds(2 * p, 2)], expon.at[slot]),
            (i_q.at[:, lanes], trio.at[slot, 0]),
            (i_k.at[:, lanes], trio.at[slot, 1]),
            (i_v.at[:, lanes], trio.at[slot, 2]),
            (i_rate.at[:, lanes], rate.at[slot]),
            (i_mixed.at[:, lanes], mixed.at[slot]),
        )
        return [pltpu.make_async_copy(src, dst, pair_sems.at[slot, n]) for n, (src, dst) in enumerate(moves)]

    for copy in loads[:2] + chunk_loads(0) + loads[2:]:
        copy.start()
    place.enter()

    zpq = Route(place, "zpq", True)
    pzq = Route(place, "pzq", False)
    scatters = [
        Scatter(place, route, held, slots, final, scatter_sends.at[i], scatter_recvs.at[i])
        for i, (route, held, slots, final) in enumerate(
            (
                (zpq, h_qkv, s_qkv, f_qkv),
                (zpq, h_out, s_out, f_out),
                (zpq, h_up, s_up, f_up),
                (pzq, h_down, s_down, f_down),
            )
        )
    ]
    by_qkv, by_out, by_up, by_down = scatters

    def columns(c):
        return pl.ds(pl.multiple_of(c * part, 128), part)

    def hand(slot, held, n):
        return remote(
            staged.at[slot, :, columns(1 - place.c)],
            held,
            hand_sends.at[n],
            hand_recvs.at[n],
            place.device(c=1 - place.c),
        )

    def settle(slot, held, n):
        copy = hand(slot, held, n)
        copy.wait_recv()
        held[...] = (held[...].astype(F32) + staged[slot, :, columns(place.c)].astype(F32)).astype(BF)
        copy.wait_send()

    def down_chunk(j):
        return (2 * (j % 2), h_down.at[pl.ds(pl.multiple_of(j * width, 128), width)], j)

    def up_chunk(j):
        return (2 * (j % 2) + 1, h_up.at[:, pl.ds(pl.multiple_of(j * part, 128), part)], chunks + j)

    def qkv_chunk(i):
        return (1 + i, h_qkv.at[:, pl.ds(pl.multiple_of(i * part, 128), part)], 2 * chunks + 1 + i)

    out_chunk = (0, h_out, 2 * chunks)

    for copy in loads[:2]:
        copy.wait()

    def feed(j):
        @pl.when(j < chunks - 1)
        def _():
            for copy in chunk_loads(j + 1):
                copy.start()

        for copy in chunk_loads(j):
            copy.wait()
        slot = j % 2
        act_grad = nt(upstream[...], w_down[slot]).astype(BF).astype(F32)
        pre_grad = (act_grad * expon[slot, 1, :, 0:width].astype(F32)).astype(BF)
        small[0, pl.ds(9 + j, 1), :] = column_sum(pre_grad.astype(F32))
        staged[down_chunk(j)[0]] = tn(expon[slot, 0, :, 0:width], upstream[...]).astype(BF)
        hand(*down_chunk(j)).start()
        staged[up_chunk(j)[0]] = tn(second[...], pre_grad).astype(BF)
        hand(*up_chunk(j)).start()
        grown = nt(pre_grad, w_up[slot])

        @pl.when(j == 0)
        def _():
            gathered[...] = grown

        @pl.when(j > 0)
        def _():
            gathered[...] = gathered[...] + grown
            settle(*down_chunk(j - 1))
            settle(*up_chunk(j - 1))

    pl.loop(0, chunks)(feed)
    whole_mixed = pltpu.make_async_copy(i_mixed, expon.at[1, 1, :, pl.ds(0, width)], local_sems.at[0])
    whole_mixed.start()
    for copy in pair_loads(0):
        copy.start()
    load_first = pltpu.make_async_copy(i_first, first, local_sems.at[1])
    load_first.start()
    for copy in loads[2:]:
        copy.wait()
    settle(*down_chunk(chunks - 1))
    settle(*up_chunk(chunks - 1))
    by_down.send(2)
    by_up.send(2)

    for row in (0, 1, 2, 3, 4, 5, 6, 7, 8, 13, 14, 15):
        small[0, row : row + 1, :] = jnp.zeros((1, width), F32)

    def bend(n):
        at = pl.ds(pl.multiple_of(n * span, span), span)
        center, speed = moments(middle[at, :])
        normed = center * speed
        grad = gathered[at, :]
        small[0, 2:3, :] = small[0, 2:3, :] + column_sum(grad * normed)
        small[0, 4:5, :] = small[0, 4:5, :] + column_sum(grad)
        above = upstream[at, :].astype(F32)
        small[0, 8:9, :] = small[0, 8:9, :] + column_sum(above)
        total = above + norm_back(normed, speed, vectors[2:3, :], grad)
        middle[at, :] = total
        low_total = total.astype(BF)
        small[0, 7:8, :] = small[0, 7:8, :] + column_sum(low_total.astype(F32))
        mixed_grad[at, :] = nt(low_total, w_out[...]).astype(BF)

    pl.loop(0, sources)(bend)
    whole_mixed.wait()
    staged[0] = tn(expon[1, 1, :, 0:width], middle[...].astype(BF)).astype(BF)
    hand(*out_chunk).start()
    load_first.wait()

    lane = lax.broadcasted_iota(jnp.int32, (1, 2 * half), 1)
    low = lane < half
    own_lanes = [low.astype(F32), 1.0 - low.astype(F32)]
    block = min(rows, 512)

    def attend(p):
        slot = p % 2
        lanes = pl.ds(pl.multiple_of(p * 2 * half, 128), 2 * half)

        @pl.when(p < pairs - 1)
        def _():
            for copy in pair_loads(p + 1):
                copy.start()

        for copy in pair_loads(p):
            copy.wait()
        scaled = (mixed_grad[:, lanes].astype(F32) * rate[slot]).astype(BF)
        product = scaled.astype(F32) * mixed[slot].astype(F32)
        query, key, value = trio[slot, 0], trio[slot, 1], trio[slot, 2]
        key_grads, value_grads, query_grads = [], [], []
        for h in range(2):
            inner = jnp.sum(product * own_lanes[h], -1, keepdims=True)
            lone = scaled * own_lanes[h].astype(BF)
            query_parts = []
            for n in range(rows // block):
                at = slice(n * block, (n + 1) * block)
                grad = nt(lone[at], value)
                weights = expon[slot, h, at, :].astype(F32)
                grad = (weights * (grad - inner[at])).astype(BF)
                score_grad[h, at, :] = grad
                query_parts.append(nn(grad, key))
            query_grads.append(jnp.concatenate(query_parts, 0))
            key_grads.append(tn(query, score_grad[h]))
            value_grads.append(tn(scaled, expon[slot, h]))
        query_grad = (jnp.where(low, query_grads[0], query_grads[1]) * (1.0 / math.sqrt(half))).astype(BF)
        key_grad = jnp.concatenate([key_grads[0][:half], key_grads[1][half:]], 0).T.astype(BF)
        value_grad = jnp.concatenate([value_grads[0][:half], value_grads[1][half:]], 0).T.astype(BF)
        small[0, 5:6, lanes] = column_sum(query_grad.astype(F32))
        small[0, 6:7, lanes] = column_sum(value_grad.astype(F32))
        grads = jnp.concatenate([query_grad, key_grad, value_grad], 1)
        where = pl.ds(pl.multiple_of(slot * part, 128), part)
        staged[1 + p // 2, :, where] = tn(first[...], grads).astype(BF)
        weight = jnp.concatenate(
            [w_qkv[:, pl.ds(pl.multiple_of(p * 2 * half + n * width, 128), 2 * half)] for n in range(3)], 1
        )
        grown = nt(grads, weight)

        @pl.when(p == 0)
        def _():
            first_grad[...] = grown

        @pl.when(p > 0)
        def _():
            first_grad[...] = first_grad[...] + grown

        @pl.when(p % 2 == 1)
        def _():
            hand(*qkv_chunk(p // 2)).start()

    pl.loop(0, pairs)(attend)
    load_x = pltpu.make_async_copy(i_x, expon.at[0, 0, :, pl.ds(0, width)], local_sems.at[2])
    load_x.start()
    load_x.wait()
    settle(*out_chunk)
    for i in range(3):
        settle(*qkv_chunk(i))
    by_out.send(2)
    by_qkv.send(2)

    def close(step):
        source = place.mate(sources - 1 - step)
        at = pl.ds(pl.multiple_of(source * span, span), span)
        turned = jnp.transpose(code[source])
        flags = jnp.concatenate([turned[:, 0:1], turned[:, 1:2]], 0) == 1.0
        start = jnp.where(flags, vectors[0:1, :], expon[0, 0, at, 0:width].astype(F32))
        center, speed = moments(start)
        normed = center * speed
        grad = first_grad[at, :]
        small[0, 1:2, :] = small[0, 1:2, :] + column_sum(grad * normed)
        small[0, 3:4, :] = small[0, 3:4, :] + column_sum(grad)
        total = middle[at, :] + norm_back(normed, speed, vectors[1:2, :], grad)
        small[0, 0:1, :] = small[0, 0:1, :] + column_sum(jnp.where(flags, total, 0.0))
        patch[step] = jnp.where(flags, 0.0, total).astype(BF)

        @pl.when(step < sources - 1)
        def _():
            remote(
                patch.at[step],
                o_patch.at[place.tm],
                row_sends.at[sources - 1 - step],
                row_recvs.at[sources - 1 - step],
                (place.batch, source),
            ).start()

    pl.loop(0, sources)(close)
    own_patch = pltpu.make_async_copy(patch.at[sources - 1], o_patch.at[place.tm], local_sems.at[3])
    own_patch.start()
    sum_vectors(place, small, small_slots, small_sends, small_recvs)
    own_small = pltpu.make_async_copy(small.at[4], o_small, local_sems.at[4])
    own_small.start()
    for stage in (2, 1, 0):
        for scatter in scatters:
            scatter.add(stage)
        if stage > 0:
            for scatter in scatters:
                scatter.send(stage - 1)

    moves = []

    def deliver(final, target, pieces):
        shard = target.shape[0]
        for near, far, jump, size in pieces:
            to = pl.ds(pl.multiple_of(far + place.c * jump, 128), size)
            mine = pl.ds(pl.multiple_of(place.c * shard, 8), shard)
            theirs = pl.ds(pl.multiple_of((1 - place.c) * shard, 8), shard)
            n = len(moves) // 2
            moves.append(
                pltpu.make_async_copy(final.at[mine, pl.ds(near, size)], target.at[:, to], local_sems.at[5 + n])
            )
            moves.append(
                remote(
                    final.at[theirs, pl.ds(near, size)],
                    target.at[:, to],
                    final_sends.at[n],
                    final_recvs.at[n],
                    place.device(c=1 - place.c),
                )
            )
            moves[-2].start()
            moves[-1].start()

    deliver(f_down, o_down, [(0, 0, part, part)])
    deliver(f_up, o_up, [(j * part, j * width, part, part) for j in range(chunks)])
    deliver(f_out, o_out, [(0, 0, part, part)])
    deliver(
        f_qkv,
        o_qkv,
        [
            (i * part + n * 2 * half, n * width + i * 4 * half, 2 * half, 2 * half)
            for i in range(3)
            for n in range(3)
        ],
    )
    for move in moves:
        move.wait()
    for step in range(1, sources):
        copy = remote(
            patch.at[0], o_patch.at[place.mate(step)], row_sends.at[step], row_recvs.at[step], place.device()
        )
        copy.wait_recv()
        copy.wait_send()
    own_patch.wait()
    own_small.wait()
    for scatter in scatters:
        scatter.drain()


def backward(deep, saved, shards, patches):
    sources, span, width = patches.shape
    rows = sources * span
    chips = deep * 4
    chunks = shards[2].shape[1] // width
    shape = jax.ShapeDtypeStruct
    plane = (rows, width)
    small = saved[4]
    code = saved[7]
    halves = [(2 * chips * s.shape[0], s.shape[1] // 2) for s in shards]
    outs = [shape(s.shape, F32) for s in shards] + [shape(small.shape, F32), shape(patches.shape, BF)]
    scratch = [
        pltpu.VMEM(saved[0].shape, BF),
        pltpu.VMEM(saved[1].shape, BF),
        pltpu.VMEM((2, width, width), BF),
        pltpu.VMEM((2, width, width), BF),
        pltpu.VMEM(plane, BF),
        pltpu.VMEM(plane, BF),
        pltpu.VMEM(plane, F32),
        pltpu.VMEM(plane, F32),
        pltpu.VMEM((2, 2, rows, rows), BF),
        pltpu.VMEM((2, rows, rows), BF),
        pltpu.VMEM((2, 3, rows, 2 * width // HEADS), BF),
        pltpu.VMEM((2, rows, 2 * width // HEADS), F32),
        pltpu.VMEM((2, rows, 2 * width // HEADS), BF),
        pltpu.VMEM((4, width, width), BF),
    ]
    scratch += [pltpu.VMEM(h, BF) for h in halves]
    scratch += [pltpu.VMEM((chips - 1, 2 * s.shape[0], s.shape[1] // 2), BF) for s in shards]
    scratch += [pltpu.VMEM((2 * s.shape[0], s.shape[1] // 2), F32) for s in shards]
    scratch += [
        pltpu.VMEM(small.shape, F32),
        pltpu.VMEM(code.shape, F32),
        pltpu.VMEM((5,) + small.shape, F32),
        pltpu.VMEM((2 + deep,) + small.shape, F32),
        pltpu.VMEM(patches.shape, BF),
    ]
    dma = pltpu.SemaphoreType.DMA
    scratch += [
        dma((7,)),
        dma((2, 4)),
        dma((2, 6)),
        dma((2 * chunks + 4,)),
        dma((2 * chunks + 4,)),
        dma((4, chips - 1)),
        dma((4, chips - 1)),
        dma((11 + chunks,)),
        dma((11 + chunks,)),
        dma((2 + deep,)),
        dma((2 + deep,)),
        dma((sources,)),
        dma((sources,)),
        dma((16 + chunks,)),
    ]
    return pl.pallas_call(
        functools.partial(backward_kernel, deep),
        out_shape=outs,
        in_specs=[HBM] * len(saved),
        out_specs=[HBM] * len(outs),
        scratch_shapes=scratch,
        compiler_params=pltpu.CompilerParams(
            collective_id=1, has_side_effects=True, vmem_limit_bytes=63 * 2**20
        ),
        name="backward",
    )(*saved)


def pack(deep, mask_embed, norm_gain, norm_shift, qv_bias, branch_bias, up_bias, width):
    device = lax.axis_index("batch") * 4 + lax.axis_index("tm")
    lines = jnp.concatenate([mask_embed[None], norm_gain, norm_shift, qv_bias, branch_bias], 0)
    lines = lines.astype(BF).astype(F32)
    top = lax.dynamic_update_slice(jnp.zeros((9, width), F32), lines, (0, device * lines.shape[1]))
    flat = lax.dynamic_update_slice(
        jnp.zeros((7 * width,), F32), up_bias.astype(BF).astype(F32), (device * up_bias.shape[0],)
    )
    return jnp.concatenate([top, flat.reshape(7, width)], 0)


def by_rows(
    deep,
    patches,
    segment_ids,
    mask_flags,
    cotangent,
    mask_embed,
    norm_gain,
    norm_shift,
    qkv_weight,
    qv_bias,
    out_weight,
    branch_bias,
    up_weight,
    up_bias,
    down_weight,
):
    sources, span, width = patches.shape
    shards = (qkv_weight, out_weight, up_weight, down_weight)
    lane = 128
    code = jnp.concatenate([mask_flags.reshape(sources, -1, lane), segment_ids.reshape(sources, -1, lane)], 1)
    code = jnp.pad(code.astype(F32), ((0, 0), (0, 8 - code.shape[1]), (0, 0)))
    small = pack(deep, mask_embed, norm_gain, norm_shift, qv_bias, branch_bias, up_bias, width)
    *saved, result = forward(deep, patches, cotangent, code, small, *shards)
    *grads, sums, patch_grad = backward(deep, saved, shards, patches)
    device = lax.axis_index("batch") * 4 + lax.axis_index("tm")
    piece = mask_embed.shape[0]
    own = lax.dynamic_slice(sums, (0, device * piece), (9, piece))
    up_sum = lax.dynamic_slice(sums[9:].reshape(-1), (device * up_bias.shape[0],), up_bias.shape)
    return (
        result.astype(F32),
        patch_grad.astype(F32),
        own[0],
        own[1:3],
        own[3:5],
        grads[0],
        own[5:7],
        grads[1],
        own[7:9],
        grads[2],
        up_sum,
        grads[3],
    )


def layer_norm(hidden, gain, shift):
    center = hidden - jnp.mean(hidden, -1, keepdims=True)
    spread = jnp.mean(center * center, -1, keepdims=True)
    return center * lax.rsqrt(spread + EPS) * gain + shift


def gelu_exact(values):
    return jax.nn.gelu(values, approximate=False)


def outer_sum(left, right):
    return lax.dot_general(
        left, right, (((0,), (0,)), ((), ())), preferred_element_type=jnp.float32
    )


def back_product(grad, weight):
    return lax.dot_general(
        grad, weight, (((1,), (1,)), ((), ())), preferred_element_type=jnp.float32
    )


def by_patches(
    patches,
    segment_ids,
    mask_flags,
    cotangent,
    mask_embed,
    norm_gain,
    norm_shift,
    qkv_weight,
    qv_bias,
    out_weight,
    branch_bias,
    up_weight,
    up_bias,
    down_weight,
):
    rows, span, width = patches.shape
    head_dim = width // HEADS
    scale = 1.0 / math.sqrt(head_dim)
    count = rows * span
    block = min(rows, max(1, 512 // span))
    groups = rows // block
    (
        whole_embed,
        whole_gain,
        whole_shift,
        whole_qkv,
        whole_qvbias,
        whole_out,
        whole_bias,
        whole_up,
        whole_upbias,
        whole_down,
    ) = (
        lax.all_gather(mask_embed.astype(jnp.bfloat16), ("batch", "tm"), axis=0, tiled=True),
        lax.all_gather(norm_gain.astype(jnp.bfloat16), ("batch", "tm"), axis=1, tiled=True),
        lax.all_gather(norm_shift.astype(jnp.bfloat16), ("batch", "tm"), axis=1, tiled=True),
        lax.all_gather(qkv_weight.astype(jnp.bfloat16), ("batch", "tm"), axis=0, tiled=True),
        lax.all_gather(qv_bias.astype(jnp.bfloat16), ("batch", "tm"), axis=1, tiled=True),
        lax.all_gather(out_weight.astype(jnp.bfloat16), ("batch", "tm"), axis=0, tiled=True),
        lax.all_gather(branch_bias.astype(jnp.bfloat16), ("batch", "tm"), axis=1, tiled=True),
        lax.all_gather(up_weight.astype(jnp.bfloat16), ("batch", "tm"), axis=0, tiled=True),
        lax.all_gather(up_bias.astype(jnp.bfloat16), ("batch", "tm"), axis=0, tiled=True),
        lax.all_gather(down_weight.astype(jnp.bfloat16), ("batch", "tm"), axis=0, tiled=True),
    )
    gains = whole_gain.astype(jnp.float32)
    shifts = whole_shift.astype(jnp.float32)
    biases = whole_bias.astype(jnp.float32)
    qv_terms = whole_qvbias.astype(jnp.float32)
    masked = (mask_flags == 1)[..., None]
    start = jnp.where(masked, whole_embed.astype(jnp.float32), patches.astype(jnp.float32))
    first_in = layer_norm(start, gains[0], shifts[0]).astype(jnp.bfloat16).reshape(count, width)
    projected = jnp.dot(first_in, whole_qkv, preferred_element_type=jnp.float32)
    queries = (projected[:, :width] + qv_terms[0]).astype(jnp.bfloat16)
    keys_local = projected[:, width : 2 * width].astype(jnp.bfloat16)
    values_local = (projected[:, 2 * width :] + qv_terms[1]).astype(jnp.bfloat16)
    pairs = jnp.concatenate([keys_local, values_local], 1).reshape(rows, span, 2 * width)
    all_pairs, all_segments = (
        lax.all_gather(pairs, "tm", axis=1, tiled=True),
        lax.all_gather(segment_ids, "tm", axis=1, tiled=True),
    )
    total_keys = all_pairs.shape[1]
    query_blocks = queries.reshape(groups, block, span, width)
    pair_blocks = all_pairs.reshape(groups, block, total_keys, 2 * width)
    own_segments = segment_ids.reshape(groups, block, span)
    far_segments = all_segments.reshape(groups, block, total_keys)

    def masked_scores(query_blk, key_blk, query_seg, key_seg):
        lead = query_blk.shape[1]
        trail = key_blk.shape[1]
        query_heads = query_blk.reshape(block, lead, HEADS, head_dim)
        key_heads = key_blk.reshape(block, trail, HEADS, head_dim)
        scores = (
            jnp.einsum(
                "bqhd,bkhd->bhqk", query_heads, key_heads, preferred_element_type=jnp.float32
            )
            * scale
        )
        allowed = (query_seg[:, :, None] == key_seg[:, None, :])[:, None]
        return jnp.where(allowed, scores, FAR)

    def attend(items):
        query_blk, pair_blk, own_seg, far_seg = items
        scores = masked_scores(query_blk, pair_blk[..., :width], own_seg, far_seg)
        peak = jnp.max(scores, -1, keepdims=True)
        expon = jnp.exp(scores - peak)
        totals = jnp.sum(expon, -1, keepdims=True)
        probs_low = (expon / totals).astype(jnp.bfloat16)
        value_heads = pair_blk[..., width:].reshape(block, total_keys, HEADS, head_dim)
        mixed_blk = jnp.einsum(
            "bhqk,bkhd->bqhd", probs_low, value_heads, preferred_element_type=jnp.float32
        )
        return (mixed_blk.reshape(block, span, width), peak + jnp.log(totals))

    mixed, log_totals = lax.map(attend, (query_blocks, pair_blocks, own_segments, far_segments))
    mixed_low = mixed.reshape(count, width).astype(jnp.bfloat16)
    branch = jnp.dot(mixed_low, whole_out, preferred_element_type=jnp.float32) + biases[0]
    middle = start + branch.reshape(rows, span, width)
    second_in = layer_norm(middle, gains[1], shifts[1]).astype(jnp.bfloat16).reshape(count, width)
    hidden_pre = jnp.dot(
        second_in, whole_up, preferred_element_type=jnp.float32
    ) + whole_upbias.astype(jnp.float32)
    hidden_act = gelu_exact(hidden_pre).astype(jnp.bfloat16)
    result = jnp.dot(hidden_act, whole_down, preferred_element_type=jnp.float32) + biases[1]
    output = middle + result.reshape(rows, span, width)
    back_qkv, back_out, back_up, back_down = (
        lax.all_gather(qkv_weight.astype(jnp.bfloat16), ("batch", "tm"), axis=0, tiled=True),
        lax.all_gather(out_weight.astype(jnp.bfloat16), ("batch", "tm"), axis=0, tiled=True),
        lax.all_gather(up_weight.astype(jnp.bfloat16), ("batch", "tm"), axis=0, tiled=True),
        lax.all_gather(down_weight.astype(jnp.bfloat16), ("batch", "tm"), axis=0, tiled=True),
    )
    upstream = cotangent.astype(jnp.float32)
    result_grad = upstream.reshape(count, width).astype(jnp.bfloat16)
    down_bias_grad = jnp.sum(result_grad.astype(jnp.float32), 0)
    down_weight_grad = outer_sum(hidden_act, result_grad)
    act_grad = back_product(result_grad, back_down).astype(jnp.bfloat16)
    gelu_pull = jax.vjp(gelu_exact, hidden_pre)[1]
    pre_grad = gelu_pull(act_grad.astype(jnp.float32))[0].astype(jnp.bfloat16)
    up_bias_grad = jnp.sum(pre_grad.astype(jnp.float32), 0)
    up_weight_grad = outer_sum(second_in, pre_grad)
    second_grad = back_product(pre_grad, back_up).reshape(rows, span, width)
    norm_pull_two = jax.vjp(layer_norm, middle, gains[1], shifts[1])[1]
    middle_norm_grad, gain_two_grad, shift_two_grad = norm_pull_two(second_grad)
    middle_grad = upstream + middle_norm_grad
    branch_grad = middle_grad.reshape(count, width).astype(jnp.bfloat16)
    out_bias_grad = jnp.sum(branch_grad.astype(jnp.float32), 0)
    out_weight_grad = outer_sum(mixed_low, branch_grad)
    mixed_grad = back_product(branch_grad, back_out).astype(jnp.bfloat16)
    mixed_blocks = mixed_grad.reshape(groups, block, span, width)

    def query_back(items):
        query_blk, pair_blk, own_seg, far_seg, log_total, grad_blk = items
        scores = masked_scores(query_blk, pair_blk[..., :width], own_seg, far_seg)
        probs = jnp.exp(scores - log_total)
        probs_low = probs.astype(jnp.bfloat16)
        query_heads = query_blk.reshape(block, span, HEADS, head_dim)
        key_heads = pair_blk[..., :width].reshape(block, total_keys, HEADS, head_dim)
        value_heads = pair_blk[..., width:].reshape(block, total_keys, HEADS, head_dim)
        grad_heads = grad_blk.reshape(block, span, HEADS, head_dim)
        prob_grad = jnp.einsum(
            "bqhd,bkhd->bhqk", grad_heads, value_heads, preferred_element_type=jnp.float32
        )
        inner = jnp.sum(probs * prob_grad, -1, keepdims=True)
        score_grad = (probs * (prob_grad - inner)).astype(jnp.bfloat16)
        query_grad = (
            jnp.einsum("bhqk,bkhd->bqhd", score_grad, key_heads, preferred_element_type=jnp.float32)
            * scale
        )
        key_grad = (
            jnp.einsum(
                "bhqk,bqhd->bkhd", score_grad, query_heads, preferred_element_type=jnp.float32
            )
            * scale
        )
        value_grad = jnp.einsum(
            "bhqk,bqhd->bkhd", probs_low, grad_heads, preferred_element_type=jnp.float32
        )
        pair_grad = jnp.concatenate(
            [
                key_grad.reshape(block, total_keys, width),
                value_grad.reshape(block, total_keys, width),
            ],
            -1,
        )
        return (query_grad.reshape(block, span, width), pair_grad, inner)

    query_grads, pair_grads, unused_inner = lax.map(
        query_back,
        (query_blocks, pair_blocks, own_segments, far_segments, log_totals, mixed_blocks),
    )
    pair_grads = pair_grads.reshape(rows, total_keys, 2 * width)
    local_pair_grads = lax.psum_scatter(pair_grads, "tm", scatter_dimension=1, tiled=True).astype(
        jnp.bfloat16
    )
    query_low = query_grads.reshape(count, width).astype(jnp.bfloat16)
    local_pair_grads = local_pair_grads.reshape(count, 2 * width)
    qkv_grad = jnp.concatenate([query_low, local_pair_grads], 1)
    qkv_weight_grad = outer_sum(first_in, qkv_grad)
    qv_bias_grad = jnp.stack(
        [
            jnp.sum(query_low.astype(jnp.float32), 0),
            jnp.sum(local_pair_grads[:, width:].astype(jnp.float32), 0),
        ]
    )
    first_grad = back_product(qkv_grad, back_qkv).reshape(rows, span, width)
    norm_pull_one = jax.vjp(layer_norm, start, gains[0], shifts[0])[1]
    start_norm_grad, gain_one_grad, shift_one_grad = norm_pull_one(first_grad)
    start_grad = middle_grad + start_norm_grad
    embed_grad = jnp.sum(jnp.where(masked, start_grad, 0.0), (0, 1))
    patch_grad = jnp.where(masked, 0.0, start_grad)
    (
        embed_sum,
        gain_sum,
        shift_sum,
        qkv_sum,
        qv_sum,
        out_sum,
        branch_sum,
        up_sum,
        up_bias_sum,
        down_sum,
    ) = (
        lax.psum_scatter(embed_grad, ("batch", "tm"), scatter_dimension=0, tiled=True),
        lax.psum_scatter(
            jnp.stack([gain_one_grad, gain_two_grad]),
            ("batch", "tm"),
            scatter_dimension=1,
            tiled=True,
        ),
        lax.psum_scatter(
            jnp.stack([shift_one_grad, shift_two_grad]),
            ("batch", "tm"),
            scatter_dimension=1,
            tiled=True,
        ),
        lax.psum_scatter(qkv_weight_grad, ("batch", "tm"), scatter_dimension=0, tiled=True),
        lax.psum_scatter(qv_bias_grad, ("batch", "tm"), scatter_dimension=1, tiled=True),
        lax.psum_scatter(out_weight_grad, ("batch", "tm"), scatter_dimension=0, tiled=True),
        lax.psum_scatter(
            jnp.stack([out_bias_grad, down_bias_grad]),
            ("batch", "tm"),
            scatter_dimension=1,
            tiled=True,
        ),
        lax.psum_scatter(up_weight_grad, ("batch", "tm"), scatter_dimension=0, tiled=True),
        lax.psum_scatter(up_bias_grad, ("batch", "tm"), scatter_dimension=0, tiled=True),
        lax.psum_scatter(down_weight_grad, ("batch", "tm"), scatter_dimension=0, tiled=True),
    )
    return (
        output,
        patch_grad,
        embed_sum,
        gain_sum,
        shift_sum,
        qkv_sum,
        qv_sum,
        out_sum,
        branch_sum,
        up_sum,
        up_bias_sum,
        down_sum,
    )


def solution(mesh):
    wide, deep = mesh.shape["batch"] * mesh.shape["tm"], mesh.shape["batch"] // 2

    def on_device(patches, *rest):
        width = patches.shape[-1]
        fits = mesh.shape["tm"] == patches.shape[0] == 4 and width % (8 * wide) == 0 and patches.shape[1] == 256
        return by_rows(deep, patches, *rest) if fits else by_patches(patches, *rest)

    return jax.shard_map(
        on_device,
        mesh=mesh,
        in_specs=(
            P("batch", "tm", None),
            P("batch", "tm"),
            P("batch", "tm"),
            P("batch", "tm", None),
            P(("batch", "tm")),
            P(None, ("batch", "tm")),
            P(None, ("batch", "tm")),
            P(("batch", "tm"), None),
            P(None, ("batch", "tm")),
            P(("batch", "tm"), None),
            P(None, ("batch", "tm")),
            P(("batch", "tm"), None),
            P(("batch", "tm")),
            P(("batch", "tm"), None),
        ),
        out_specs=(
            P("batch", "tm", None),
            P("batch", "tm", None),
            P(("batch", "tm")),
            P(None, ("batch", "tm")),
            P(None, ("batch", "tm")),
            P(("batch", "tm"), None),
            P(None, ("batch", "tm")),
            P(("batch", "tm"), None),
            P(None, ("batch", "tm")),
            P(("batch", "tm"), None),
            P(("batch", "tm")),
            P(("batch", "tm"), None),
        ),
        check_vma=False,
    )
```

```python
import functools
import math

import jax
import jax.numpy as jnp
from jax import lax
from jax.experimental import pallas as pl
from jax.experimental.pallas import tpu as pltpu
from jax.sharding import PartitionSpec as P

HEADS = 12
EPS = 1e-06
FAR = -1e30
LOG2E = math.log2(math.e)
BF = jnp.bfloat16
F32 = jnp.float32
MESH = pl.DeviceIdType.MESH
HBM = pl.BlockSpec(memory_space=pl.ANY)
SLOPE = 0.36
TAIL = (
    0.14371305209487725,
    0.14177235930704382,
    0.1397197719471602,
    0.026547986328787306,
    0.18095585464885458,
    -0.1797659534284226,
    0.04705662553510592,
)


FORWARD_STEPS = {
    "start": {
        0: [
            ("first", "vector"),
            ("first", "qkv"),
            ("first", "out"),
            ("first", "up"),
            (0, "vector", 0, 3),
            (0, "qkv", 0, 3),
            (0, "out", 0, 3),
            (1, "vector", 0, 4),
            (1, "qkv", 0, 2),
            (1, "qkv", 2, 4),
            ("rows",),
            ("first", "down"),
            (2, "vector", 0, 8),
            (1, "out", 0, 2),
            (1, "out", 2, 4),
            ("finish", "vector"),
            (2, "qkv", 0, 4),
            ("spread",),
            (2, "qkv", 4, 8),
            ("finish", "qkv"),
        ],
    },
    "project": {
        2: [
            (0, "up", 0, 3),
        ],
    },
    "attend": {
        0: [
            (0, "down", 0, 1),
        ],
        2: [
            (2, "out", 0, 4),
            (2, "out", 4, 8),
        ],
        3: [
            ("finish", "out"),
            (1, "up", 0, 2),
        ],
        5: [
            (1, "up", 2, 4),
            (1, "down", 0, 3),
        ],
        8: [
            (1, "down", 3, 6),
            (2, "up", 0, 4),
        ],
        9: [
            (2, "up", 4, 8),
        ],
        10: [
            ("finish", "up"),
            ("cotangent",),
        ],
    },
    "rise": {
        1: [
            (2, "down", 0, 4),
        ],
        2: [
            (2, "down", 4, 8),
        ],
        3: [
            ("finish", "down"),
        ],
    },
}


BACKWARD_STEPS = {
    "feed": {
        2: [
            ("settle", "up", 0),
        ],
        5: [
            ("settle", "down", 0),
        ],
        6: [
            ("settle", "down", 1),
        ],
        7: [
            ("turn", 0),
            ("settle", "up", 1),
            ("settle", "down", 2),
        ],
        9: [
            ("turn", 1),
            ("add", "up", 2, 0),
        ],
        11: [
            ("turn", 2),
            ("settle", "down", 3),
            ("settle", "up", 2),
        ],
    },
    "attend": {
        1: [
            ("turn", 3),
            ("settle", "up", 3),
        ],
        4: [
            ("settle", "out", 0),
        ],
        6: [
            ("add", "up", 2, 3),
            ("add", "up", 2, 1),
            ("add", "up", 1, 0),
            ("settle", "qkv", 0),
        ],
        8: [
            ("add", "up", 1, 1),
            ("add", "out", 2, 0),
            ("add", "qkv", 2, 0),
            ("add", "up", 1, 3),
        ],
        9: [
            ("add", "up", 2, 2),
        ],
        10: [
            ("add", "out", 1, 0),
            ("add", "down", 1, 0),
        ],
    },
    "close": {
        0: [
            ("settle", "qkv", 2),
        ],
        1: [
            ("add", "down", 0, 0),
        ],
    },
    "tail": {
        0: [
            ("add", "up", 1, 2),
            ("add", "up", 0, 0),
            ("add", "up", 0, 1),
            ("add", "qkv", 2, 2),
            ("vector send", 0),
            ("add", "out", 0, 0),
            ("settle", "qkv", 1),
            ("vector add", 0),
            ("deliver", "out"),
            ("add", "qkv", 2, 1),
            ("vector send", 1),
            ("add", "qkv", 1, 0),
            ("add", "up", 0, 2),
            ("deliver", "down"),
            ("add", "qkv", 1, 2),
            ("add", "up", 0, 3),
            ("deliver", "up"),
            ("vector add", 1),
            ("add", "qkv", 0, 0),
            ("vector send", 2),
            ("vector add", 2),
            ("vector send", 3),
            ("add", "qkv", 1, 1),
            ("add", "qkv", 0, 2),
            ("add", "qkv", 0, 1),
            ("deliver", "qkv"),
            ("vector add", 3),
        ],
    },
}


def nn(left, right):
    return jnp.dot(left, right, preferred_element_type=F32)


def nt(left, right):
    return lax.dot_general(left, right, (((1,), (1,)), ((), ())), preferred_element_type=F32)


def tn(left, right):
    return lax.dot_general(left, right, (((0,), (0,)), ((), ())), preferred_element_type=F32)


def gelu_and_slope(pre):
    size = jnp.abs(pre)
    t = 1.0 / (1.0 + SLOPE * size)
    poly = jnp.full_like(t, TAIL[-1])
    for term in TAIL[-2::-1]:
        poly = poly * t + term
    bell = jnp.exp2(pre * pre * (-0.5 * LOG2E))
    lower = poly * t * bell
    cdf = jnp.where(pre >= 0, 1.0 - lower, lower)
    return pre * cdf, cdf + pre * bell * (1.0 / math.sqrt(2.0 * math.pi))


def moments(hidden):
    center = hidden - jnp.mean(hidden, -1, keepdims=True)
    return center, lax.rsqrt(jnp.mean(center * center, -1, keepdims=True) + EPS)


def norm_back(normed, rate, gain, grad):
    scaled = grad * gain
    shared = jnp.mean(scaled * normed, -1, keepdims=True)
    return rate * (scaled - jnp.mean(scaled, -1, keepdims=True) - normed * shared)


def column_sum(values):
    return jnp.sum(values, 0, keepdims=True)


class Place:
    def __init__(self, deep):
        batch, tm = lax.axis_index("batch"), lax.axis_index("tm")
        self.deep = deep
        self.batch, self.tm = batch, tm
        self.z, self.y = batch // 2, batch % 2
        self.x, self.c = tm // 2, tm % 2

    def device(self, z=None, y=None, x=None, c=None):
        z = self.z if z is None else z
        y = self.y if y is None else y
        x = self.x if x is None else x
        c = self.c if c is None else c
        return (z * 2 + y, x * 2 + c)

    def mate(self, k):
        return (self.x + k // 2) % 2 * 2 + (self.c + k % 2) % 2

    def enter(self):
        barrier = pltpu.get_barrier_semaphore()
        others = [self.device(c=1 - self.c), self.device(x=1 - self.x), self.device(y=1 - self.y)]
        others.append(self.device(x=1 - self.x, c=1 - self.c))
        others += [self.device(z=(self.z + d) % self.deep) for d in range(1, self.deep)]
        for other in others:
            pl.semaphore_signal(barrier, inc=1, device_id=other, device_id_type=MESH)
        pl.semaphore_wait(barrier, len(others))


def remote(src, dst, send, recv, device):
    return pltpu.make_async_remote_copy(
        src_ref=src, dst_ref=dst, send_sem=send, recv_sem=recv, device_id=device, device_id_type=MESH
    )


class Route:
    def __init__(self, place, order, crossed):
        self.place, self.order, self.crossed = place, order, crossed
        c = place.c
        self.own = {
            "z": place.z,
            "p": c * place.y + (1 - c) * place.x if crossed else place.x,
            "q": c * place.x + (1 - c) * place.y if crossed else place.y,
        }
        self.size = {"z": place.deep, "p": 2, "q": 2}
        self.sizes = [self.size[axis] for axis in order]

    def shifted(self, shifts):
        at = {a: (self.own[a] + s % self.size[a]) % self.size[a] for a, s in zip(self.order, shifts)}
        c = self.place.c
        if self.crossed:
            return at["z"], c * at["p"] + (1 - c) * at["q"], c * at["q"] + (1 - c) * at["p"]
        return at["z"], at["q"], at["p"]

    def device(self, shifts):
        z, y, x = self.shifted(shifts)
        return self.place.device(z=z, y=y, x=x)

    def chip(self, shifts):
        z, y, x = self.shifted(shifts)
        return (z * 2 + y) * 2 + x

    def offsets(self, upto):
        found = [()]
        for stage, size in enumerate(self.sizes):
            found = [f + (o,) for f in found for o in range(size if stage < upto else 1)]
        return found

    def index(self, offset):
        flat = 0
        for o, size in zip(offset, self.sizes):
            flat = flat * size + o
        return flat


class Gather:
    def __init__(self, place, route, shard, joined, full, local, sends, recvs):
        self.place, self.route = place, route
        self.shard, self.joined, self.full = shard, joined, full
        self.local, self.sends, self.recvs = local, sends, recvs
        self.rows = shard.shape[0]
        self.half = shard.shape[1] // 2
        self.count = 0

    def columns(self, c):
        return pl.ds(pl.multiple_of(c * self.half, 128), self.half)

    def region(self, chip, c):
        rows = 2 * self.rows
        return self.full.at[pl.ds(pl.multiple_of(chip * rows, 16), rows), self.columns(c)]

    def ship(self, src, dst, recv, device):
        remote(src, dst, self.sends.at[self.count], recv, device).start()
        self.count += 1

    def join(self):
        place = self.place
        own = pl.ds(pl.multiple_of(place.c * self.rows, 8), self.rows)
        self.mine = pltpu.make_async_copy(
            self.shard.at[:, self.columns(place.c)], self.joined.at[own], self.local
        )
        self.mine.start()
        self.pair = self.recvs.at[0]
        self.ship(
            self.shard.at[:, self.columns(1 - place.c)],
            self.joined.at[own],
            self.recvs.at[0],
            place.device(c=1 - place.c),
        )

    def arrive(self, offset, stage):
        route, place = self.route, self.place
        chip = route.chip([-o for o in offset])
        block = self.region(chip, place.c)
        for later in range(stage + 1, 3):
            for d in range(1, route.sizes[later]):
                shifts = [0, 0, 0]
                shifts[later] = d
                seen = list(offset)
                seen[later] = d
                self.ship(block, block, self.recvs.at[1 + route.index(seen)], route.device(shifts))
        total = math.prod(route.sizes)
        self.ship(
            block,
            block,
            self.recvs.at[1 + total + route.index(offset)],
            place.device(c=1 - place.c),
        )

    def first(self):
        place = self.place
        self.mine.wait()
        own = pl.ds(pl.multiple_of((1 - place.c) * self.rows, 8), self.rows)
        remote(
            self.joined.at[own], self.joined.at[own], self.sends.at[0], self.recvs.at[0], place.device(c=1 - place.c)
        ).wait()
        chip = self.route.chip([0, 0, 0])
        self.region(chip, place.c)[...] = self.joined[...].astype(BF)
        self.arrive((0, 0, 0), -1)

    def stage(self, stage, some=slice(None)):
        route = self.route
        for offset in [o for o in route.offsets(stage + 1) if o[stage] > 0][some]:
            block = self.region(route.chip([-o for o in offset]), self.place.c)
            remote(
                block, block, self.sends.at[0], self.recvs.at[1 + route.index(offset)], self.place.device()
            ).wait_recv()
            self.arrive(offset, stage)

    def finish(self):
        route = self.route
        total = math.prod(route.sizes)
        for offset in route.offsets(3):
            block = self.region(route.chip([-o for o in offset]), 1 - self.place.c)
            remote(
                block,
                block,
                self.sends.at[0],
                self.recvs.at[1 + total + route.index(offset)],
                self.place.device(),
            ).wait_recv()

    def drain(self):
        block = self.region(self.route.chip([0, 0, 0]), self.place.c)
        for n in range(1, self.count):
            remote(block, block, self.sends.at[n], self.recvs.at[0], self.place.device()).wait_send()


class VectorSum:
    def __init__(self, place, held, slots, sends, recvs):
        self.held, self.slots = held, slots
        stages = [
            [place.device(c=1 - place.c)],
            [place.device(x=1 - place.x)],
            [place.device(y=1 - place.y)],
            [place.device(z=(place.z + d) % place.deep) for d in range(1, place.deep)],
        ]
        self.copies, slot = [], 0
        for stage, others in enumerate(stages):
            self.copies.append([])
            for other in others:
                copy = remote(held.at[stage], slots.at[slot], sends.at[slot], recvs.at[slot], other)
                self.copies[-1].append((copy, slot))
                slot += 1

    def send(self, stage):
        for copy, _ in self.copies[stage]:
            copy.start()

    def add(self, stage):
        total = self.held[stage]
        for copy, slot in self.copies[stage]:
            copy.wait()
            total = total + self.slots[slot]
        self.held[stage + 1] = total


def gather_vectors(mask_embed, norm_gain, norm_shift, qv_bias, branch_bias, up_bias):
    lines = jnp.concatenate([mask_embed[None], norm_gain, norm_shift, qv_bias, branch_bias], 0)
    lines = jnp.pad(lines, ((0, 0), (0, 128 - lines.shape[1])))
    rest = jnp.concatenate([lines[8:], jnp.pad(up_bias, (0, 128 - up_bias.shape[0]))[None]], 0)
    return jnp.concatenate([lines[:8], jnp.pad(rest, ((0, 6), (0, 0)))], 1)


def spread_vectors(blocks, vectors):
    width = vectors.shape[1]
    devices = blocks.shape[0] // 8
    piece = width // devices
    table = blocks[...].astype(F32)
    vectors[...] = jnp.zeros_like(vectors)

    def put(rows, at, start):
        window = min(start // 128 * 128, width - 256)
        wide = jnp.concatenate([rows, jnp.zeros_like(rows)], 1)
        wide = pltpu.roll(wide, start - window, 1)
        vectors[at, window : window + 256] = vectors[at, window : window + 256] + wide

    for d in range(devices):
        block = table[8 * d : 8 * d + 8]
        put(block[:, :128], slice(0, 8), piece * d)
        put(block[0:1, 128:], slice(8, 9), piece * d)
        up = 4 * piece * d
        put(block[1:2, 128:], slice(9 + up // width, 10 + up // width), up % width)


def code_columns(code, source):
    turned = jnp.transpose(code[source])
    flags = jnp.concatenate([turned[:, 0:1], turned[:, 1:2]], 0)
    clips = jnp.concatenate([turned[:, 2:3], turned[:, 3:4]], 0)
    return flags, clips


def forward_kernel(
    deep,
    patches,
    cotangent,
    code_in,
    shard_vector,
    shard_qkv,
    shard_out,
    shard_up,
    shard_down,
    o_qkv,
    o_out,
    o_up,
    o_down,
    o_small,
    o_x,
    o_cot,
    o_code,
    o_first,
    o_q,
    o_k,
    o_v,
    o_mixed,
    o_second,
    o_rate,
    o_middle,
    o_act,
    o_slope,
    o_expon,
    o_result,
    w_qkv,
    w_out,
    w_up,
    w_down,
    j_qkv,
    j_out,
    j_up,
    j_down,
    j_vector,
    w_vector,
    small,
    x,
    code,
    first,
    q,
    k,
    v,
    mixed,
    second,
    rate,
    middle,
    expon,
    slope,
    result,
    q_code,
    k_code,
    join_sems,
    gather_sends,
    gather_recvs,
    row_sends,
    row_recvs,
    local_sems,
    expon_sems,
    act_sems,
):
    place = Place(deep)
    span, width = patches.shape[1:]
    rows = x.shape[0]
    sources = rows // span
    half = width // HEADS
    pairs = HEADS // 2
    inner = w_up.shape[1]
    chunks = inner // width

    place.enter()

    kinds = ((patches, x), (code_in, code), (cotangent, o_cot))

    def own_part(kind):
        src, dst = kinds[kind]
        to = dst.at[pl.ds(pl.multiple_of(place.tm * span, span), span)] if kind != 1 else dst.at[place.tm]
        return pltpu.make_async_copy(src.at[place.tm], to, local_sems.at[1 + kind])

    def row_copy(kind, step, to):
        src, dst = kinds[kind]
        here = dst.at[pl.ds(pl.multiple_of(place.tm * span, span), span)] if kind != 1 else dst.at[place.tm]
        return remote(
            src.at[to], here, row_sends.at[kind, step], row_recvs.at[kind, step], (place.batch, to)
        )

    def row_wait(kind, step):
        src, dst = kinds[kind]
        source = place.mate(step)
        there = dst.at[pl.ds(pl.multiple_of(source * span, span), span)] if kind != 1 else dst.at[source]
        remote(
            there, there, row_sends.at[kind, step], row_recvs.at[kind, step], (place.batch, source)
        ).wait_recv()

    zpq = Route(place, "zpq", True)
    zxy = Route(place, "zpq", False)
    pzq = Route(place, "pzq", True)
    gathers = [
        Gather(place, route, shard, joined, full, join_sems.at[i], gather_sends.at[i], gather_recvs.at[i])
        for i, (route, shard, joined, full) in enumerate(
            (
                (zpq, shard_vector, j_vector, w_vector),
                (zxy, shard_qkv, j_qkv, w_qkv),
                (zxy, shard_out, j_out, w_out),
                (zpq, shard_up, j_up, w_up),
                (pzq, shard_down, j_down, w_down),
            )
        )
    ]
    for gather in gathers:
        gather.join()
    named = dict(zip(("vector", "qkv", "out", "up", "down"), gathers))

    def send_rows(kinds):
        for kind in kinds:
            for step in range(1, sources):
                row_copy(kind, step, place.mate(step)).start()

    def run(steps):
        for what, *which in steps:
            if what == "rows":
                send_rows((1, 0))
            elif what == "cotangent":
                send_rows((2,))
            elif what == "spread":
                spread_vectors(w_vector, small)
            elif what == "first":
                named[which[0]].first()
            elif what == "finish":
                named[which[0]].finish()
            else:
                named[which[0]].stage(what, slice(which[1], which[2]))

    def after(loop, index, part=0, parts=1):
        for when, steps in FORWARD_STEPS.get(loop, {}).items():
            if when % parts == part:
                pl.when(index == when // parts)(functools.partial(run, steps))

    for kind in (1, 0):
        own_part(kind).start()
    run(FORWARD_STEPS["start"][0])
    keeping = []

    def keep(src, dst):
        copy = pltpu.make_async_copy(src, dst, local_sems.at[4 + len(keeping)])
        copy.start()
        keeping.append(copy)

    keep(w_qkv, o_qkv)
    keep(small, o_small)

    vectors = small
    lane = lax.broadcasted_iota(jnp.int32, (1, 2 * half), 1)
    low = lane < half
    own_lanes = [low.astype(F32), 1.0 - low.astype(F32)]

    for kind in (1, 0):
        own_part(kind).wait()

    @pl.loop(0, sources)
    def _(step):
        @pl.when(step > 0)
        def _():
            row_wait(1, step)
            row_wait(0, step)

        source = place.mate(step)
        at = pl.ds(pl.multiple_of(source * span, span), span)
        flags, clips = code_columns(code, source)
        start = jnp.where(flags == 1.0, vectors[0:1, :], x[at, :].astype(F32))
        middle[at, :] = start
        center, speed = moments(start)
        normed = (center * speed * vectors[1:2, :] + vectors[3:4, :]).astype(BF)
        first[at, :] = normed
        q[at, :] = (nn(normed, w_qkv[:, 0:width]) + vectors[5:6, :]).astype(BF) * (1.0 / math.sqrt(half))
        k[at, :] = nn(normed, w_qkv[:, width : 2 * width]).astype(BF)
        v[at, :] = (nn(normed, w_qkv[:, 2 * width :]) + vectors[6:7, :]).astype(BF)
        clip_lane = lax.broadcasted_iota(jnp.int32, (span, 2 * half), 1).astype(F32)
        for h in range(2):
            base = float(half * (1 - h))
            same = clip_lane - base == clips
            coded = jnp.logical_and(clip_lane >= base, clip_lane < base + 5.0)
            q_code[h, at, :] = jnp.where(same, 1.0, 0.0).astype(BF)
            k_code[h, at, :] = jnp.where(jnp.logical_and(coded, jnp.logical_not(same)), FAR, 0.0).astype(BF)
        after("project", step)

    for src, dst in ((x, o_x), (code, o_code), (first, o_first), (q, o_q), (k, o_k), (v, o_v)):
        keep(src, dst)

    block = min(rows, 512)

    def expon_copy(p):
        return pltpu.make_async_copy(expon.at[p % 2], o_expon.at[pl.ds(2 * p, 2)], expon_sems.at[p % 2])

    def attend(p):
        lanes = pl.ds(pl.multiple_of(p * 2 * half, 128), 2 * half)

        @pl.when(p >= 2)
        def _():
            expon_copy(p - 2).wait()

        slot = p % 2
        keys, values = [], []
        for h in range(2):
            mask = own_lanes[h].astype(BF)
            keys.append(k[:, lanes] * mask + k_code[h])
            values.append(v[:, lanes] * mask + own_lanes[1 - h].astype(BF))
        for part in range(rows // block):
            at = pl.ds(part * block, block)
            mixes = []
            for h in range(2):
                query = q[at, lanes] * own_lanes[h].astype(BF) + q_code[h, at, :]
                scores = nt(query, keys[h])
                peak = jnp.max(scores, -1, keepdims=True)
                weights = jnp.exp2((scores - peak) * LOG2E).astype(BF)
                expon[slot, h, at, :] = weights
                mixes.append(nn(weights, values[h]))
            top = jnp.where(low, mixes[0], mixes[1])
            totals = pltpu.roll(jnp.where(low, mixes[1], mixes[0]), half, 1)
            speed = 1.0 / totals
            rate[at, lanes] = speed
            mixed[at, lanes] = (top * speed).astype(BF)
            if part == rows // block - 1:
                expon_copy(p).start()
            after("attend", p, part, rows // block)

    pl.loop(0, pairs)(attend)
    for src, dst in ((w_out, o_out), (w_up, o_up), (mixed, o_mixed), (rate, o_rate)):
        keep(src, dst)
    for p in (pairs - 2, pairs - 1):
        expon_copy(p).wait()

    def act(j, at):
        return expon.at[j // 2, j % 2, at, pl.ds(0, width)]

    def slope_copies(step):
        at = pl.ds(pl.multiple_of(step * span, span), span)
        return [
            pltpu.make_async_copy(slope.at[step % 2, j], o_slope.at[j, at], act_sems.at[step % 2, j])
            for j in range(chunks)
        ]

    def act_copies(step):
        at = pl.ds(pl.multiple_of(step * span, span), span)
        return [pltpu.make_async_copy(act(j, at), o_act.at[j, at], act_sems.at[2, j]) for j in range(chunks)]

    def rise(step):
        @pl.when(step >= 2)
        def _():
            for copy in slope_copies(step - 2):
                copy.wait()

        at = pl.ds(pl.multiple_of(step * span, span), span)
        hidden = middle[at, :] + nn(mixed[at, :], w_out[...]) + vectors[7:8, :]
        middle[at, :] = hidden
        center, speed = moments(hidden)
        normed = (center * speed * vectors[2:3, :] + vectors[4:5, :]).astype(BF)
        second[at, :] = normed
        for j in range(chunks):
            pre = nn(normed, w_up[:, j * width : (j + 1) * width]) + vectors[9 + j : 10 + j, :]
            value, steep = gelu_and_slope(pre)
            expon[j // 2, j % 2, at, 0:width] = value.astype(BF)
            slope[step % 2, j] = steep.astype(BF)
        for copy in slope_copies(step) + act_copies(step):
            copy.start()
        after("rise", step)

    def fall(step):
        at = pl.ds(pl.multiple_of(step * span, span), span)
        total = middle[at, :] + vectors[8:9, :]
        for j in range(chunks):
            total = total + nn(expon[j // 2, j % 2, at, 0:width], w_down[j * width : (j + 1) * width, :])
        result[at, :] = total.astype(BF)

    pl.loop(0, sources)(rise)
    keep(second, o_second)
    keep(middle, o_middle)
    keep(w_down, o_down)
    pl.loop(0, sources)(fall)
    keep(result, o_result)
    for step in range(sources):
        for copy in act_copies(step):
            copy.wait()
    for step in (sources - 2, sources - 1):
        for copy in slope_copies(step):
            copy.wait()
    for step in range(1, sources):
        row_wait(2, step)
        for kind in (0, 1, 2):
            row_copy(kind, step, place.mate(step)).wait_send()
    for copy in keeping:
        copy.wait()
    for gather in gathers:
        gather.drain()


def forward(deep, patches, cotangent, code, vector, qkv, out, up, down):
    sources, span, width = patches.shape
    rows = sources * span
    chips = deep * 4
    inner = up.shape[1]
    chunks = inner // width
    shape = jax.ShapeDtypeStruct
    shards = (qkv, out, up, down)
    fulls = [(2 * chips * s.shape[0], s.shape[1]) for s in shards]
    plane = (rows, width)
    outs = [shape(f, BF) for f in fulls]
    outs += [shape((16, width), F32), shape(plane, BF), shape(plane, BF), shape(code.shape, F32)]
    outs += [shape(plane, BF)] * 6 + [shape(plane, F32)] * 2
    outs += [shape((chunks, rows, width), BF)] * 2
    outs += [shape((HEADS, rows, rows), BF), shape(plane, BF)]
    scratch = [pltpu.VMEM(f, BF) for f in fulls]
    scratch += [pltpu.VMEM((2 * s.shape[0], s.shape[1] // 2), F32) for s in shards]
    scratch += [
        pltpu.VMEM((16, vector.shape[1] // 2), F32),
        pltpu.VMEM((16 * chips, vector.shape[1]), BF),
        pltpu.VMEM((16, width), F32),
        pltpu.VMEM(plane, BF),
        pltpu.VMEM(code.shape, F32),
    ]
    scratch += [pltpu.VMEM(plane, BF)] * 6 + [pltpu.VMEM(plane, F32)] * 2
    scratch += [
        pltpu.VMEM((2, 2, rows, rows), BF),
        pltpu.VMEM((2, chunks, span, width), BF),
        pltpu.VMEM(plane, BF),
        pltpu.VMEM((2, rows, 128), BF),
        pltpu.VMEM((2, rows, 128), BF),
    ]
    dma = pltpu.SemaphoreType.DMA
    scratch += [
        dma((5,)),
        dma((5, 1 + 2 * chips)),
        dma((5, 1 + 2 * chips)),
        dma((4, sources)),
        dma((4, sources)),
        dma((20,)),
        dma((2,)),
        dma((3, chunks)),
    ]
    return pl.pallas_call(
        functools.partial(forward_kernel, deep),
        out_shape=outs,
        in_specs=[HBM] * 8,
        out_specs=[HBM] * len(outs),
        scratch_shapes=scratch,
        compiler_params=pltpu.CompilerParams(
            collective_id=0, has_side_effects=True, vmem_limit_bytes=62 * 2**20
        ),
        name="forward",
    )(patches, cotangent, code, vector, qkv, out, up, down)


class Scatter:
    def __init__(self, place, route, held, slots, final, sends, recvs, piece=None):
        self.place, self.route = place, route
        self.held, self.slots, self.final = held, slots, final
        self.sends, self.recvs = sends, recvs
        self.rows = slots.shape[1]
        self.width = piece
        self.sent = []

    def region(self, shifts):
        return pl.ds(pl.multiple_of(self.route.chip(shifts) * self.rows, 16), self.rows)

    def columns(self, piece):
        if piece is None:
            return pl.ds(0, self.held.shape[1])
        return pl.ds(pl.multiple_of(piece * self.width, 128), self.width)

    def parts(self, stage):
        route = self.route
        for d in range(1, route.sizes[stage]):
            for earlier in route.offsets(stage):
                offset = list(earlier)
                offset[stage] = d
                yield d, [-o for o in earlier], route.index(offset) - 1

    def copy(self, stage, d, back, slot, piece):
        shifts, to = list(back), [0, 0, 0]
        shifts[stage] = to[stage] = d
        columns = self.columns(piece)
        n = 0 if piece is None else piece
        return remote(
            self.held.at[self.region(shifts), columns],
            self.slots.at[slot, :, columns],
            self.sends.at[n, slot],
            self.recvs.at[n, slot],
            self.route.device(to),
        )

    def send(self, stage, piece=None):
        self.sent.append((stage, piece))
        for d, back, slot in self.parts(stage):
            self.copy(stage, d, back, slot, piece).start()

    def add(self, stage, piece=None):
        found = {}
        columns = self.columns(piece)
        for d, back, slot in self.parts(stage):
            self.copy(stage, d, back, slot, piece).wait_recv()
            found.setdefault(tuple(back), []).append(slot)
        for back, slots in found.items():
            at = self.region(back)
            total = self.held[at, columns].astype(F32)
            for slot in slots:
                total = total + self.slots[slot, :, columns].astype(F32)
            if stage == 0:
                self.final[:, columns] = total
            else:
                self.held[at, columns] = total.astype(BF)

    def drain(self):
        for stage, piece in self.sent:
            for d, back, slot in self.parts(stage):
                self.copy(stage, d, back, slot, piece).wait_send()


class RowScatter(Scatter):
    def part_q(self, z, p):
        place = self.place
        behind = (place.z - z + place.deep) % place.deep
        return [p, (place.deep - behind) % place.deep, 0], (p * place.deep + behind) * 2

    def copy_q(self, z, p):
        shifts, slot = self.part_q(z, p)
        return self.copy(2, 1, shifts, slot, None)

    def send_q(self, z):
        for p in range(2):
            self.copy_q(z, p).start()

    def add_q(self, z):
        for p in range(2):
            shifts, slot = self.part_q(z, p)
            self.copy_q(z, p).wait_recv()
            at = self.region(shifts)
            self.held[at, :] = (self.held[at, :].astype(F32) + self.slots[slot].astype(F32)).astype(BF)

    def copy_z(self, z, p):
        place = self.place
        ahead = (z - place.z + place.deep) % place.deep
        return self.copy(1, ahead, [p, 0, 0], (p * place.deep + ahead) * 2 - 1, None)

    def send_z(self, z):
        @pl.when(self.place.z != z)
        def _():
            for p in range(2):
                self.copy_z(z, p).start()

    def drain(self):
        place = self.place
        for z in range(place.deep):
            for p in range(2):
                self.copy_q(z, p).wait_send()
        for d, back, slot in self.parts(1):
            self.copy(1, d, back, slot, None).wait_send()
        super().drain()


def backward_kernel(
    deep,
    i_qkv,
    i_out,
    i_up,
    i_down,
    i_small,
    i_x,
    i_cot,
    i_code,
    i_first,
    i_q,
    i_k,
    i_v,
    i_mixed,
    i_second,
    i_rate,
    i_middle,
    i_act,
    i_slope,
    i_expon,
    i_result,
    i_own_cot,
    o_qkv,
    o_out,
    o_up,
    o_down,
    o_small,
    o_patch,
    o_result,
    w_qkv,
    w_out,
    w_up,
    w_down,
    upstream,
    second,
    gathered,
    middle,
    expon,
    score_grad,
    trio,
    rate,
    mixed,
    staged,
    h_qkv,
    h_out,
    h_up,
    h_down,
    s_qkv,
    s_out,
    s_up,
    s_down,
    f_qkv,
    f_out,
    f_up,
    f_down,
    vectors,
    code,
    small,
    small_slots,
    patch,
    load_sems,
    chunk_sems,
    pair_sems,
    hand_sends,
    hand_recvs,
    scatter_sends,
    scatter_recvs,
    final_sends,
    final_recvs,
    small_sends,
    small_recvs,
    row_sends,
    row_recvs,
    local_sems,
):
    place = Place(deep)
    rows, width = upstream.shape
    sources, span = patch.shape[:2]
    half = width // HEADS
    pairs = HEADS // 2
    chunks = i_act.shape[0]
    part = width // 2
    first = second
    mixed_grad = upstream
    first_grad = gathered

    loads = [
        pltpu.make_async_copy(src, dst, load_sems.at[i])
        for i, (src, dst) in enumerate(
            (
                (i_second, second),
                (i_middle, middle),
                (i_small, vectors),
                (i_code, code),
                (i_out, w_out),
                (i_qkv, w_qkv),
            )
        )
    ]

    def chunk_loads(j):
        slot = j % 2
        columns = pl.ds(pl.multiple_of(j * width, 128), width)
        moves = (
            (i_down.at[columns], w_down.at[slot]),
            (i_up.at[:, columns], w_up.at[slot]),
            (i_act.at[j], expon.at[slot, 0, :, pl.ds(0, width)]),
            (i_slope.at[j], expon.at[slot, 1, :, pl.ds(0, width)]),
        )
        return [pltpu.make_async_copy(src, dst, chunk_sems.at[slot, n]) for n, (src, dst) in enumerate(moves)]

    def pair_loads(p):
        slot = p % 2
        lanes = pl.ds(pl.multiple_of(p * 2 * half, 128), 2 * half)
        moves = (
            (i_expon.at[pl.ds(2 * p, 2)], expon.at[slot]),
            (i_q.at[:, lanes], trio.at[slot, 0]),
            (i_k.at[:, lanes], trio.at[slot, 1]),
            (i_v.at[:, lanes], trio.at[slot, 2]),
            (i_rate.at[:, lanes], rate.at[slot]),
            (i_mixed.at[:, lanes], mixed.at[slot]),
        )
        return [pltpu.make_async_copy(src, dst, pair_sems.at[slot, n]) for n, (src, dst) in enumerate(moves)]

    for step in range(sources):
        source = place.mate(step)
        at = pl.ds(pl.multiple_of(source * span, span), span)
        loads.insert(
            step,
            pltpu.make_async_copy(
                i_own_cot.at[place.tm] if step == 0 else i_cot.at[at], upstream.at[at], load_sems.at[6 + step]
            ),
        )
    early = sources + 1
    for copy in loads[:early] + chunk_loads(0) + loads[early:]:
        copy.start()
    place.enter()

    def result_copy(step):
        to = place.mate(step)
        return remote(
            i_result.at[pl.ds(pl.multiple_of(to * span, span), span)],
            o_result.at[place.tm],
            row_sends.at[1, step],
            row_recvs.at[1, step],
            (place.batch, to),
        )

    result_in = pltpu.make_async_copy(
        i_result.at[pl.ds(pl.multiple_of(place.tm * span, span), span)], patch.at[sources - 1], local_sems.at[5]
    )
    result_in.start()
    result_out = pltpu.make_async_copy(patch.at[sources - 1], o_result.at[place.tm], local_sems.at[5])
    for step in range(1, sources):
        result_copy(step).start()

    zpq = Route(place, "zpq", True)
    pzq = Route(place, "pzq", True)
    xzy = Route(place, "pzq", False)
    zxy = Route(place, "zpq", False)
    by_qkv = Scatter(place, xzy, h_qkv, s_qkv, f_qkv, scatter_sends.at[0], scatter_recvs.at[0], part)
    by_out = Scatter(place, zpq, h_out, s_out, f_out, scatter_sends.at[1], scatter_recvs.at[1], part)
    by_up = Scatter(place, zxy, h_up, s_up, f_up, scatter_sends.at[2], scatter_recvs.at[2], part)
    by_down = RowScatter(place, pzq, h_down, s_down, f_down, scatter_sends.at[3], scatter_recvs.at[3])
    scatters = [by_qkv, by_out, by_up, by_down]

    def columns(c):
        return pl.ds(pl.multiple_of(c * part, 128), part)

    def hand(slot, held, n):
        return remote(
            staged.at[slot, :, columns(1 - place.c)],
            held,
            hand_sends.at[n],
            hand_recvs.at[n],
            place.device(c=1 - place.c),
        )

    def settle(slot, held, n):
        copy = hand(slot, held, n)
        copy.wait_recv()
        held[...] = (held[...].astype(F32) + staged[slot, :, columns(place.c)].astype(F32)).astype(BF)
        copy.wait_send()

    def down_chunk(j):
        return (2 * (j % 2), h_down.at[pl.ds(pl.multiple_of(j * width, 128), width)], j)

    def up_chunk(j):
        return (2 * (j % 2) + 1, h_up.at[:, pl.ds(pl.multiple_of(j * part, 128), part)], chunks + j)

    def qkv_chunk(i):
        return (1 + i, h_qkv.at[:, pl.ds(pl.multiple_of(i * part, 128), part)], 2 * chunks + 1 + i)

    def out_chunk(i):
        return (0, h_out, 2 * chunks)

    named = {
        "qkv": (by_qkv, qkv_chunk),
        "out": (by_out, out_chunk),
        "up": (by_up, up_chunk),
        "down": (by_down, down_chunk),
    }
    summed = VectorSum(place, small, small_slots, small_sends, small_recvs)

    def run(steps):
        for what, *which in steps:
            if what == "vector send":
                summed.send(which[0])
            elif what == "vector add":
                summed.add(which[0])
            elif what == "turn":
                by_down.add_q(which[0])
                by_down.send_z(which[0])
            elif what == "deliver":
                deliver(*deliveries[which[0]])
            elif what == "settle":
                scatter, chunk = named[which[0]]
                settle(*chunk(which[1]))
                if scatter is by_down:
                    scatter.send_q(which[1])
                else:
                    scatter.send(2, which[1])
            else:
                scatter = named[which[0]][0]
                stage = which[1]
                piece = None if scatter is by_down else which[2]
                scatter.add(stage, piece)
                if stage > 0:
                    scatter.send(stage - 1, piece)

    def after(loop, index=0, part=0, parts=1):
        for when, steps in BACKWARD_STEPS.get(loop, {}).items():
            if when % parts == part:
                pl.when(index == when // parts)(functools.partial(run, steps))

    for copy in loads[:early]:
        copy.wait()

    def feed(j):
        @pl.when(j < chunks - 1)
        def _():
            for copy in chunk_loads(j + 1):
                copy.start()

        for copy in chunk_loads(j):
            copy.wait()
        slot = j % 2
        act_grad = nt(upstream[...], w_down[slot]).astype(BF).astype(F32)
        pre_grad = (act_grad * expon[slot, 1, :, 0:width].astype(F32)).astype(BF)
        small[0, pl.ds(9 + j, 1), :] = column_sum(pre_grad.astype(F32))
        staged[down_chunk(j)[0]] = tn(expon[slot, 0, :, 0:width], upstream[...]).astype(BF)
        hand(*down_chunk(j)).start()
        after("feed", j, 0, 3)
        staged[up_chunk(j)[0]] = tn(second[...], pre_grad).astype(BF)
        hand(*up_chunk(j)).start()
        after("feed", j, 1, 3)
        grown = nt(pre_grad, w_up[slot])

        @pl.when(j == 0)
        def _():
            gathered[...] = grown

        @pl.when(j > 0)
        def _():
            gathered[...] = gathered[...] + grown

        after("feed", j, 2, 3)

    pl.loop(0, chunks)(feed)
    whole_mixed = pltpu.make_async_copy(i_mixed, expon.at[1, 1, :, pl.ds(0, width)], local_sems.at[0])
    whole_mixed.start()
    for copy in pair_loads(0):
        copy.start()
    load_first = pltpu.make_async_copy(i_first, first, local_sems.at[1])
    load_first.start()
    for copy in loads[early:]:
        copy.wait()
    for row in (0, 1, 2, 3, 4, 5, 6, 7, 8, 13, 14, 15):
        small[0, row : row + 1, :] = jnp.zeros((1, width), F32)

    def bend(n):
        at = pl.ds(pl.multiple_of(n * span, span), span)
        center, speed = moments(middle[at, :])
        normed = center * speed
        grad = gathered[at, :]
        small[0, 2:3, :] = small[0, 2:3, :] + column_sum(grad * normed)
        small[0, 4:5, :] = small[0, 4:5, :] + column_sum(grad)
        above = upstream[at, :].astype(F32)
        small[0, 8:9, :] = small[0, 8:9, :] + column_sum(above)
        total = above + norm_back(normed, speed, vectors[2:3, :], grad)
        middle[at, :] = total
        low_total = total.astype(BF)
        small[0, 7:8, :] = small[0, 7:8, :] + column_sum(low_total.astype(F32))
        mixed_grad[at, :] = nt(low_total, w_out[...]).astype(BF)

    pl.loop(0, sources)(bend)
    run(BACKWARD_STEPS.get("bend", {}).get(0, []))
    whole_mixed.wait()
    staged[0] = tn(expon[1, 1, :, 0:width], middle[...].astype(BF)).astype(BF)
    hand(*out_chunk(0)).start()
    run(BACKWARD_STEPS.get("out", {}).get(0, []))
    load_first.wait()
    result_in.wait()
    result_out.start()

    lane = lax.broadcasted_iota(jnp.int32, (1, 2 * half), 1)
    low = lane < half
    own_lanes = [low.astype(F32), 1.0 - low.astype(F32)]
    block = min(rows, 512)

    def attend(p):
        slot = p % 2
        lanes = pl.ds(pl.multiple_of(p * 2 * half, 128), 2 * half)

        @pl.when(p < pairs - 1)
        def _():
            for copy in pair_loads(p + 1):
                copy.start()

        for copy in pair_loads(p):
            copy.wait()
        scaled = (mixed_grad[:, lanes].astype(F32) * rate[slot]).astype(BF)
        product = scaled.astype(F32) * mixed[slot].astype(F32)
        query, key, value = trio[slot, 0], trio[slot, 1], trio[slot, 2]
        key_grads, value_grads, query_grads = [], [], []
        for h in range(2):
            inner = jnp.sum(product * own_lanes[h], -1, keepdims=True)
            lone = scaled * own_lanes[h].astype(BF)
            query_parts = []
            for n in range(rows // block):
                at = slice(n * block, (n + 1) * block)
                grad = nt(lone[at], value)
                weights = expon[slot, h, at, :].astype(F32)
                grad = (weights * (grad - inner[at])).astype(BF)
                score_grad[h, at, :] = grad
                query_parts.append(nn(grad, key))
            query_grads.append(jnp.concatenate(query_parts, 0))
            key_grads.append(tn(query, score_grad[h]))
            value_grads.append(tn(scaled, expon[slot, h]))
            if h == 0:
                after("attend", p, 0, 2)
        query_grad = (jnp.where(low, query_grads[0], query_grads[1]) * (1.0 / math.sqrt(half))).astype(BF)
        key_grad = jnp.concatenate([key_grads[0][:half], key_grads[1][half:]], 0).T.astype(BF)
        value_grad = jnp.concatenate([value_grads[0][:half], value_grads[1][half:]], 0).T.astype(BF)
        small[0, 5:6, lanes] = column_sum(query_grad.astype(F32))
        small[0, 6:7, lanes] = column_sum(value_grad.astype(F32))
        grads = jnp.concatenate([query_grad, key_grad, value_grad], 1)
        where = pl.ds(pl.multiple_of(slot * part, 128), part)
        staged[1 + p // 2, :, where] = tn(first[...], grads).astype(BF)
        weight = jnp.concatenate(
            [w_qkv[:, pl.ds(pl.multiple_of(p * 2 * half + n * width, 128), 2 * half)] for n in range(3)], 1
        )
        grown = nt(grads, weight)

        @pl.when(p == 0)
        def _():
            first_grad[...] = grown

        @pl.when(p > 0)
        def _():
            first_grad[...] = first_grad[...] + grown

        @pl.when(p % 2 == 1)
        def _():
            hand(*qkv_chunk(p // 2)).start()

        after("attend", p, 1, 2)

    pl.loop(0, pairs)(attend)
    load_x = pltpu.make_async_copy(i_x, expon.at[0, 0, :, pl.ds(0, width)], local_sems.at[2])
    load_x.start()
    load_x.wait()
    result_out.wait()

    def close(step):
        source = place.mate(sources - 1 - step)
        at = pl.ds(pl.multiple_of(source * span, span), span)
        turned = jnp.transpose(code[source])
        flags = jnp.concatenate([turned[:, 0:1], turned[:, 1:2]], 0) == 1.0
        start = jnp.where(flags, vectors[0:1, :], expon[0, 0, at, 0:width].astype(F32))
        center, speed = moments(start)
        normed = center * speed
        grad = first_grad[at, :]
        small[0, 1:2, :] = small[0, 1:2, :] + column_sum(grad * normed)
        small[0, 3:4, :] = small[0, 3:4, :] + column_sum(grad)
        total = middle[at, :] + norm_back(normed, speed, vectors[1:2, :], grad)
        small[0, 0:1, :] = small[0, 0:1, :] + column_sum(jnp.where(flags, total, 0.0))
        patch[step] = jnp.where(flags, 0.0, total).astype(BF)

        @pl.when(step < sources - 1)
        def _():
            remote(
                patch.at[step],
                o_patch.at[place.tm],
                row_sends.at[0, sources - 1 - step],
                row_recvs.at[0, sources - 1 - step],
                (place.batch, source),
            ).start()

        after("close", step)

    pl.loop(0, sources)(close)
    own_patch = pltpu.make_async_copy(patch.at[sources - 1], o_patch.at[place.tm], local_sems.at[3])
    own_patch.start()
    moves = []

    def deliver(final, target, pieces):
        shard = target.shape[0]
        for near, far, jump, size in pieces:
            to = pl.ds(pl.multiple_of(far + place.c * jump, 128), size)
            mine = pl.ds(pl.multiple_of(place.c * shard, 8), shard)
            theirs = pl.ds(pl.multiple_of((1 - place.c) * shard, 8), shard)
            n = len(moves) // 2
            moves.append(
                pltpu.make_async_copy(final.at[mine, pl.ds(near, size)], target.at[:, to], local_sems.at[6 + n])
            )
            moves.append(
                remote(
                    final.at[theirs, pl.ds(near, size)],
                    target.at[:, to],
                    final_sends.at[n],
                    final_recvs.at[n],
                    place.device(c=1 - place.c),
                )
            )
            moves[-2].start()
            moves[-1].start()

    deliveries = {
        "down": (f_down, o_down, [(0, 0, part, part)]),
        "up": (f_up, o_up, [(j * part, j * width, part, part) for j in range(chunks)]),
        "out": (f_out, o_out, [(0, 0, part, part)]),
        "qkv": (
            f_qkv,
            o_qkv,
            [
                (i * part + n * 2 * half, n * width + i * 4 * half, 2 * half, 2 * half)
                for i in range(3)
                for n in range(3)
            ],
        ),
    }
    run(BACKWARD_STEPS["tail"][0])
    own_small = pltpu.make_async_copy(small.at[4], o_small, local_sems.at[4])
    own_small.start()
    for move in moves:
        move.wait()
    for step in range(1, sources):
        copy = remote(
            patch.at[0], o_patch.at[place.mate(step)], row_sends.at[0, step], row_recvs.at[0, step], place.device()
        )
        copy.wait_recv()
        copy.wait_send()
        result_copy(step).wait()
    own_patch.wait()
    own_small.wait()
    for scatter in scatters:
        scatter.drain()


def backward(deep, saved, shards, cotangent):
    sources, span, width = cotangent.shape
    rows = sources * span
    chips = deep * 4
    chunks = shards[2].shape[1] // width
    shape = jax.ShapeDtypeStruct
    plane = (rows, width)
    small = saved[4]
    code = saved[7]
    halves = [(2 * chips * s.shape[0], s.shape[1] // 2) for s in shards]
    outs = [shape(s.shape, F32) for s in shards] + [shape(small.shape, F32)] + [shape(cotangent.shape, BF)] * 2
    scratch = [
        pltpu.VMEM(saved[0].shape, BF),
        pltpu.VMEM(saved[1].shape, BF),
        pltpu.VMEM((2, width, width), BF),
        pltpu.VMEM((2, width, width), BF),
        pltpu.VMEM(plane, BF),
        pltpu.VMEM(plane, BF),
        pltpu.VMEM(plane, F32),
        pltpu.VMEM(plane, F32),
        pltpu.VMEM((2, 2, rows, rows), BF),
        pltpu.VMEM((2, rows, rows), BF),
        pltpu.VMEM((2, 3, rows, 2 * width // HEADS), BF),
        pltpu.VMEM((2, rows, 2 * width // HEADS), F32),
        pltpu.VMEM((2, rows, 2 * width // HEADS), BF),
        pltpu.VMEM((4, width, width), BF),
    ]
    scratch += [pltpu.VMEM(h, BF) for h in halves]
    scratch += [pltpu.VMEM((chips - 1, 2 * s.shape[0], s.shape[1] // 2), BF) for s in shards]
    scratch += [pltpu.VMEM((2 * s.shape[0], s.shape[1] // 2), F32) for s in shards]
    scratch += [
        pltpu.VMEM(small.shape, F32),
        pltpu.VMEM(code.shape, F32),
        pltpu.VMEM((5,) + small.shape, F32),
        pltpu.VMEM((2 + deep,) + small.shape, F32),
        pltpu.VMEM(cotangent.shape, BF),
    ]
    dma = pltpu.SemaphoreType.DMA
    scratch += [
        dma((6 + sources,)),
        dma((2, 4)),
        dma((2, 6)),
        dma((2 * chunks + 4,)),
        dma((2 * chunks + 4,)),
        dma((4, chunks, chips - 1)),
        dma((4, chunks, chips - 1)),
        dma((11 + chunks,)),
        dma((11 + chunks,)),
        dma((2 + deep,)),
        dma((2 + deep,)),
        dma((2, sources)),
        dma((2, sources)),
        dma((17 + chunks,)),
    ]
    return pl.pallas_call(
        functools.partial(backward_kernel, deep),
        out_shape=outs,
        in_specs=[HBM] * (len(saved) + 1),
        out_specs=[HBM] * len(outs),
        scratch_shapes=scratch,
        compiler_params=pltpu.CompilerParams(
            collective_id=1, has_side_effects=True, vmem_limit_bytes=63 * 2**20
        ),
        name="backward",
    )(*saved, cotangent)


def by_rows(
    deep,
    patches,
    segment_ids,
    mask_flags,
    cotangent,
    mask_embed,
    norm_gain,
    norm_shift,
    qkv_weight,
    qv_bias,
    out_weight,
    branch_bias,
    up_weight,
    up_bias,
    down_weight,
):
    sources, span, width = patches.shape
    shards = (qkv_weight, out_weight, up_weight, down_weight)
    lane = 128
    code = jnp.concatenate([mask_flags.reshape(sources, -1, lane), segment_ids.reshape(sources, -1, lane)], 1)
    code = jnp.pad(code.astype(F32), ((0, 0), (0, 8 - code.shape[1]), (0, 0)))
    vector = gather_vectors(mask_embed, norm_gain, norm_shift, qv_bias, branch_bias, up_bias)
    saved = forward(deep, patches, cotangent, code, vector, *shards)
    *grads, sums, patch_grad, result = backward(deep, saved, shards, cotangent)
    device = lax.axis_index("batch") * 4 + lax.axis_index("tm")
    piece = mask_embed.shape[0]
    own = lax.dynamic_slice(sums, (0, device * piece), (9, piece))
    up_sum = lax.dynamic_slice(sums[9:13].reshape(-1), (device * up_bias.shape[0],), up_bias.shape)
    return (
        result.astype(F32),
        patch_grad.astype(F32),
        own[0],
        own[1:3],
        own[3:5],
        grads[0],
        own[5:7],
        grads[1],
        own[7:9],
        grads[2],
        up_sum,
        grads[3],
    )


def layer_norm(hidden, gain, shift):
    center = hidden - jnp.mean(hidden, -1, keepdims=True)
    spread = jnp.mean(center * center, -1, keepdims=True)
    return center * lax.rsqrt(spread + EPS) * gain + shift


def gelu_exact(values):
    return jax.nn.gelu(values, approximate=False)


def outer_sum(left, right):
    return lax.dot_general(
        left, right, (((0,), (0,)), ((), ())), preferred_element_type=jnp.float32
    )


def back_product(grad, weight):
    return lax.dot_general(
        grad, weight, (((1,), (1,)), ((), ())), preferred_element_type=jnp.float32
    )


def by_patches(
    patches,
    segment_ids,
    mask_flags,
    cotangent,
    mask_embed,
    norm_gain,
    norm_shift,
    qkv_weight,
    qv_bias,
    out_weight,
    branch_bias,
    up_weight,
    up_bias,
    down_weight,
):
    rows, span, width = patches.shape
    head_dim = width // HEADS
    scale = 1.0 / math.sqrt(head_dim)
    count = rows * span
    block = min(rows, max(1, 512 // span))
    groups = rows // block
    (
        whole_embed,
        whole_gain,
        whole_shift,
        whole_qkv,
        whole_qvbias,
        whole_out,
        whole_bias,
        whole_up,
        whole_upbias,
        whole_down,
    ) = (
        lax.all_gather(mask_embed.astype(jnp.bfloat16), ("batch", "tm"), axis=0, tiled=True),
        lax.all_gather(norm_gain.astype(jnp.bfloat16), ("batch", "tm"), axis=1, tiled=True),
        lax.all_gather(norm_shift.astype(jnp.bfloat16), ("batch", "tm"), axis=1, tiled=True),
        lax.all_gather(qkv_weight.astype(jnp.bfloat16), ("batch", "tm"), axis=0, tiled=True),
        lax.all_gather(qv_bias.astype(jnp.bfloat16), ("batch", "tm"), axis=1, tiled=True),
        lax.all_gather(out_weight.astype(jnp.bfloat16), ("batch", "tm"), axis=0, tiled=True),
        lax.all_gather(branch_bias.astype(jnp.bfloat16), ("batch", "tm"), axis=1, tiled=True),
        lax.all_gather(up_weight.astype(jnp.bfloat16), ("batch", "tm"), axis=0, tiled=True),
        lax.all_gather(up_bias.astype(jnp.bfloat16), ("batch", "tm"), axis=0, tiled=True),
        lax.all_gather(down_weight.astype(jnp.bfloat16), ("batch", "tm"), axis=0, tiled=True),
    )
    gains = whole_gain.astype(jnp.float32)
    shifts = whole_shift.astype(jnp.float32)
    biases = whole_bias.astype(jnp.float32)
    qv_terms = whole_qvbias.astype(jnp.float32)
    masked = (mask_flags == 1)[..., None]
    start = jnp.where(masked, whole_embed.astype(jnp.float32), patches.astype(jnp.float32))
    first_in = layer_norm(start, gains[0], shifts[0]).astype(jnp.bfloat16).reshape(count, width)
    projected = jnp.dot(first_in, whole_qkv, preferred_element_type=jnp.float32)
    queries = (projected[:, :width] + qv_terms[0]).astype(jnp.bfloat16)
    keys_local = projected[:, width : 2 * width].astype(jnp.bfloat16)
    values_local = (projected[:, 2 * width :] + qv_terms[1]).astype(jnp.bfloat16)
    pairs = jnp.concatenate([keys_local, values_local], 1).reshape(rows, span, 2 * width)
    all_pairs, all_segments = (
        lax.all_gather(pairs, "tm", axis=1, tiled=True),
        lax.all_gather(segment_ids, "tm", axis=1, tiled=True),
    )
    total_keys = all_pairs.shape[1]
    query_blocks = queries.reshape(groups, block, span, width)
    pair_blocks = all_pairs.reshape(groups, block, total_keys, 2 * width)
    own_segments = segment_ids.reshape(groups, block, span)
    far_segments = all_segments.reshape(groups, block, total_keys)

    def masked_scores(query_blk, key_blk, query_seg, key_seg):
        lead = query_blk.shape[1]
        trail = key_blk.shape[1]
        query_heads = query_blk.reshape(block, lead, HEADS, head_dim)
        key_heads = key_blk.reshape(block, trail, HEADS, head_dim)
        scores = (
            jnp.einsum(
                "bqhd,bkhd->bhqk", query_heads, key_heads, preferred_element_type=jnp.float32
            )
            * scale
        )
        allowed = (query_seg[:, :, None] == key_seg[:, None, :])[:, None]
        return jnp.where(allowed, scores, FAR)

    def attend(items):
        query_blk, pair_blk, own_seg, far_seg = items
        scores = masked_scores(query_blk, pair_blk[..., :width], own_seg, far_seg)
        peak = jnp.max(scores, -1, keepdims=True)
        expon = jnp.exp(scores - peak)
        totals = jnp.sum(expon, -1, keepdims=True)
        probs_low = (expon / totals).astype(jnp.bfloat16)
        value_heads = pair_blk[..., width:].reshape(block, total_keys, HEADS, head_dim)
        mixed_blk = jnp.einsum(
            "bhqk,bkhd->bqhd", probs_low, value_heads, preferred_element_type=jnp.float32
        )
        return (mixed_blk.reshape(block, span, width), peak + jnp.log(totals))

    mixed, log_totals = lax.map(attend, (query_blocks, pair_blocks, own_segments, far_segments))
    mixed_low = mixed.reshape(count, width).astype(jnp.bfloat16)
    branch = jnp.dot(mixed_low, whole_out, preferred_element_type=jnp.float32) + biases[0]
    middle = start + branch.reshape(rows, span, width)
    second_in = layer_norm(middle, gains[1], shifts[1]).astype(jnp.bfloat16).reshape(count, width)
    hidden_pre = jnp.dot(
        second_in, whole_up, preferred_element_type=jnp.float32
    ) + whole_upbias.astype(jnp.float32)
    hidden_act = gelu_exact(hidden_pre).astype(jnp.bfloat16)
    result = jnp.dot(hidden_act, whole_down, preferred_element_type=jnp.float32) + biases[1]
    output = middle + result.reshape(rows, span, width)
    back_qkv, back_out, back_up, back_down = (
        lax.all_gather(qkv_weight.astype(jnp.bfloat16), ("batch", "tm"), axis=0, tiled=True),
        lax.all_gather(out_weight.astype(jnp.bfloat16), ("batch", "tm"), axis=0, tiled=True),
        lax.all_gather(up_weight.astype(jnp.bfloat16), ("batch", "tm"), axis=0, tiled=True),
        lax.all_gather(down_weight.astype(jnp.bfloat16), ("batch", "tm"), axis=0, tiled=True),
    )
    upstream = cotangent.astype(jnp.float32)
    result_grad = upstream.reshape(count, width).astype(jnp.bfloat16)
    down_bias_grad = jnp.sum(result_grad.astype(jnp.float32), 0)
    down_weight_grad = outer_sum(hidden_act, result_grad)
    act_grad = back_product(result_grad, back_down).astype(jnp.bfloat16)
    gelu_pull = jax.vjp(gelu_exact, hidden_pre)[1]
    pre_grad = gelu_pull(act_grad.astype(jnp.float32))[0].astype(jnp.bfloat16)
    up_bias_grad = jnp.sum(pre_grad.astype(jnp.float32), 0)
    up_weight_grad = outer_sum(second_in, pre_grad)
    second_grad = back_product(pre_grad, back_up).reshape(rows, span, width)
    norm_pull_two = jax.vjp(layer_norm, middle, gains[1], shifts[1])[1]
    middle_norm_grad, gain_two_grad, shift_two_grad = norm_pull_two(second_grad)
    middle_grad = upstream + middle_norm_grad
    branch_grad = middle_grad.reshape(count, width).astype(jnp.bfloat16)
    out_bias_grad = jnp.sum(branch_grad.astype(jnp.float32), 0)
    out_weight_grad = outer_sum(mixed_low, branch_grad)
    mixed_grad = back_product(branch_grad, back_out).astype(jnp.bfloat16)
    mixed_blocks = mixed_grad.reshape(groups, block, span, width)

    def query_back(items):
        query_blk, pair_blk, own_seg, far_seg, log_total, grad_blk = items
        scores = masked_scores(query_blk, pair_blk[..., :width], own_seg, far_seg)
        probs = jnp.exp(scores - log_total)
        probs_low = probs.astype(jnp.bfloat16)
        query_heads = query_blk.reshape(block, span, HEADS, head_dim)
        key_heads = pair_blk[..., :width].reshape(block, total_keys, HEADS, head_dim)
        value_heads = pair_blk[..., width:].reshape(block, total_keys, HEADS, head_dim)
        grad_heads = grad_blk.reshape(block, span, HEADS, head_dim)
        prob_grad = jnp.einsum(
            "bqhd,bkhd->bhqk", grad_heads, value_heads, preferred_element_type=jnp.float32
        )
        inner = jnp.sum(probs * prob_grad, -1, keepdims=True)
        score_grad = (probs * (prob_grad - inner)).astype(jnp.bfloat16)
        query_grad = (
            jnp.einsum("bhqk,bkhd->bqhd", score_grad, key_heads, preferred_element_type=jnp.float32)
            * scale
        )
        key_grad = (
            jnp.einsum(
                "bhqk,bqhd->bkhd", score_grad, query_heads, preferred_element_type=jnp.float32
            )
            * scale
        )
        value_grad = jnp.einsum(
            "bhqk,bqhd->bkhd", probs_low, grad_heads, preferred_element_type=jnp.float32
        )
        pair_grad = jnp.concatenate(
            [
                key_grad.reshape(block, total_keys, width),
                value_grad.reshape(block, total_keys, width),
            ],
            -1,
        )
        return (query_grad.reshape(block, span, width), pair_grad, inner)

    query_grads, pair_grads, unused_inner = lax.map(
        query_back,
        (query_blocks, pair_blocks, own_segments, far_segments, log_totals, mixed_blocks),
    )
    pair_grads = pair_grads.reshape(rows, total_keys, 2 * width)
    local_pair_grads = lax.psum_scatter(pair_grads, "tm", scatter_dimension=1, tiled=True).astype(
        jnp.bfloat16
    )
    query_low = query_grads.reshape(count, width).astype(jnp.bfloat16)
    local_pair_grads = local_pair_grads.reshape(count, 2 * width)
    qkv_grad = jnp.concatenate([query_low, local_pair_grads], 1)
    qkv_weight_grad = outer_sum(first_in, qkv_grad)
    qv_bias_grad = jnp.stack(
        [
            jnp.sum(query_low.astype(jnp.float32), 0),
            jnp.sum(local_pair_grads[:, width:].astype(jnp.float32), 0),
        ]
    )
    first_grad = back_product(qkv_grad, back_qkv).reshape(rows, span, width)
    norm_pull_one = jax.vjp(layer_norm, start, gains[0], shifts[0])[1]
    start_norm_grad, gain_one_grad, shift_one_grad = norm_pull_one(first_grad)
    start_grad = middle_grad + start_norm_grad
    embed_grad = jnp.sum(jnp.where(masked, start_grad, 0.0), (0, 1))
    patch_grad = jnp.where(masked, 0.0, start_grad)
    (
        embed_sum,
        gain_sum,
        shift_sum,
        qkv_sum,
        qv_sum,
        out_sum,
        branch_sum,
        up_sum,
        up_bias_sum,
        down_sum,
    ) = (
        lax.psum_scatter(embed_grad, ("batch", "tm"), scatter_dimension=0, tiled=True),
        lax.psum_scatter(
            jnp.stack([gain_one_grad, gain_two_grad]),
            ("batch", "tm"),
            scatter_dimension=1,
            tiled=True,
        ),
        lax.psum_scatter(
            jnp.stack([shift_one_grad, shift_two_grad]),
            ("batch", "tm"),
            scatter_dimension=1,
            tiled=True,
        ),
        lax.psum_scatter(qkv_weight_grad, ("batch", "tm"), scatter_dimension=0, tiled=True),
        lax.psum_scatter(qv_bias_grad, ("batch", "tm"), scatter_dimension=1, tiled=True),
        lax.psum_scatter(out_weight_grad, ("batch", "tm"), scatter_dimension=0, tiled=True),
        lax.psum_scatter(
            jnp.stack([out_bias_grad, down_bias_grad]),
            ("batch", "tm"),
            scatter_dimension=1,
            tiled=True,
        ),
        lax.psum_scatter(up_weight_grad, ("batch", "tm"), scatter_dimension=0, tiled=True),
        lax.psum_scatter(up_bias_grad, ("batch", "tm"), scatter_dimension=0, tiled=True),
        lax.psum_scatter(down_weight_grad, ("batch", "tm"), scatter_dimension=0, tiled=True),
    )
    return (
        output,
        patch_grad,
        embed_sum,
        gain_sum,
        shift_sum,
        qkv_sum,
        qv_sum,
        out_sum,
        branch_sum,
        up_sum,
        up_bias_sum,
        down_sum,
    )


def solution(mesh):
    wide, deep = mesh.shape["batch"] * mesh.shape["tm"], mesh.shape["batch"] // 2

    def on_device(patches, *rest):
        width = patches.shape[-1]
        fits = mesh.shape["tm"] == patches.shape[0] == 4 and width % (8 * wide) == 0 and patches.shape[1] == 256
        return by_rows(deep, patches, *rest) if fits else by_patches(patches, *rest)

    return jax.shard_map(
        on_device,
        mesh=mesh,
        in_specs=(
            P("batch", "tm", None),
            P("batch", "tm"),
            P("batch", "tm"),
            P("batch", "tm", None),
            P(("batch", "tm")),
            P(None, ("batch", "tm")),
            P(None, ("batch", "tm")),
            P(("batch", "tm"), None),
            P(None, ("batch", "tm")),
            P(("batch", "tm"), None),
            P(None, ("batch", "tm")),
            P(("batch", "tm"), None),
            P(("batch", "tm")),
            P(("batch", "tm"), None),
        ),
        out_specs=(
            P("batch", "tm", None),
            P("batch", "tm", None),
            P(("batch", "tm")),
            P(None, ("batch", "tm")),
            P(None, ("batch", "tm")),
            P(("batch", "tm"), None),
            P(None, ("batch", "tm")),
            P(("batch", "tm"), None),
            P(None, ("batch", "tm")),
            P(("batch", "tm"), None),
            P(("batch", "tm")),
            P(("batch", "tm"), None),
        ),
        check_vma=False,
    )
```

```python
import functools
import math

import jax
import jax.numpy as jnp
from jax import lax
from jax.experimental import pallas as pl
from jax.experimental.pallas import tpu as pltpu
from jax.sharding import PartitionSpec as P

HEADS = 12
EPS = 1e-06
FAR = -1e30
LOG2E = math.log2(math.e)
BF = jnp.bfloat16
F32 = jnp.float32
MESH = pl.DeviceIdType.MESH
HBM = pl.BlockSpec(memory_space=pl.ANY)
SLOPE = 0.36
COEFFICIENTS = (
    0.14371305209487725,
    0.14177235930704382,
    0.1397197719471602,
    0.026547986328787306,
    0.18095585464885458,
    -0.1797659534284226,
    0.04705662553510592,
)


VECTOR, QKV, OUT, UP, DOWN = range(5)
START, PROJECT, ATTEND, RISE, FALL, FEED, BEND, MIX, CLOSE, TAIL = range(10)
FIRST, STAGE, FINISH, ROWS, COTANGENT, SPREAD = range(6)
SETTLE, TURN, ADD, VECTOR_SEND, VECTOR_ADD, DELIVER = range(6)

FORWARD_STEPS = {
    START: {
        0: [
            (FIRST, VECTOR),
            (FIRST, QKV),
            (STAGE, VECTOR, 0, 0, 3),
            (FIRST, OUT),
            (FIRST, UP),
            (STAGE, QKV, 0, 0, 3),
            (STAGE, VECTOR, 1, 0, 4),
            (STAGE, QKV, 1, 0, 4),
            (ROWS,),
            (STAGE, VECTOR, 2, 0, 8),
            (FINISH, VECTOR),
            (STAGE, QKV, 2, 0, 4),
            (STAGE, OUT, 0, 0, 3),
            (STAGE, QKV, 2, 4, 8),
            (SPREAD,),
            (FIRST, DOWN),
            (FINISH, QKV),
        ],
    },
    PROJECT: {
        1: [
            (STAGE, UP, 0, 0, 3),
        ],
    },
    ATTEND: {
        0: [
            (STAGE, OUT, 1, 0, 4),
        ],
        1: [
            (STAGE, UP, 1, 0, 4),
            (STAGE, DOWN, 0, 0, 1),
        ],
        3: [
            (STAGE, DOWN, 1, 0, 3),
            (STAGE, OUT, 2, 0, 4),
        ],
        4: [
            (STAGE, UP, 2, 0, 4),
            (STAGE, OUT, 2, 4, 8),
            (STAGE, UP, 2, 4, 8),
        ],
        5: [
            (FINISH, UP),
            (FINISH, OUT),
            (STAGE, DOWN, 1, 3, 6),
        ],
    },
    RISE: {
        0: [
            (COTANGENT,),
            (STAGE, DOWN, 2, 0, 4),
        ],
        1: [
            (STAGE, DOWN, 2, 4, 8),
        ],
        2: [
            (FINISH, DOWN),
        ],
    },
}


BACKWARD_STEPS = {
    FEED: {
        0: [
            (SETTLE, DOWN, 0),
            (SETTLE, UP, 0),
        ],
        1: [
            (SETTLE, DOWN, 1),
        ],
        2: [
            (SETTLE, UP, 1),
            (SETTLE, DOWN, 2),
            (TURN, 0),
        ],
        3: [
            (TURN, 1),
            (SETTLE, DOWN, 3),
            (TURN, 2),
            (SETTLE, UP, 3),
        ],
    },
    MIX: {
        0: [
            (SETTLE, UP, 2),
            (TURN, 3),
        ],
    },
    ATTEND: {
        1: [
            (ADD, UP, 2, 0),
            (SETTLE, OUT, 0),
            (ADD, UP, 2, 2),
            (ADD, UP, 2, 3),
        ],
        2: [
            (ADD, UP, 2, 1),
        ],
        3: [
            (ADD, OUT, 2, 0),
            (ADD, UP, 1, 2),
            (ADD, UP, 1, 1),
            (ADD, UP, 1, 3),
        ],
        4: [
            (SETTLE, QKV, 0),
            (ADD, OUT, 1, 0),
            (ADD, DOWN, 1, 0),
            (ADD, UP, 1, 0),
        ],
    },
    CLOSE: {
        1: [
            (ADD, OUT, 0, 0),
            (ADD, QKV, 2, 0),
            (ADD, UP, 0, 2),
            (ADD, UP, 0, 1),
        ],
        2: [
            (SETTLE, QKV, 1),
        ],
    },
    TAIL: {
        0: [
            (VECTOR_SEND, 0),
            (DELIVER, OUT),
            (ADD, DOWN, 0, 0),
            (ADD, QKV, 2, 1),
            (VECTOR_ADD, 0),
            (ADD, UP, 0, 3),
            (SETTLE, QKV, 2),
            (ADD, QKV, 2, 2),
            (VECTOR_SEND, 1),
            (ADD, UP, 0, 0),
            (ADD, QKV, 1, 0),
            (DELIVER, DOWN),
            (VECTOR_ADD, 1),
            (VECTOR_SEND, 2),
            (VECTOR_ADD, 2),
            (VECTOR_SEND, 3),
            (ADD, QKV, 1, 2),
            (ADD, QKV, 1, 1),
            (ADD, QKV, 0, 2),
            (ADD, QKV, 0, 0),
            (DELIVER, UP),
            (ADD, QKV, 0, 1),
            (DELIVER, QKV),
            (VECTOR_ADD, 3),
        ],
    },
}


def nn(left, right):
    return jnp.dot(left, right, preferred_element_type=F32)


def nt(left, right):
    return lax.dot_general(left, right, (((1,), (1,)), ((), ())), preferred_element_type=F32)


def tn(left, right):
    return lax.dot_general(left, right, (((0,), (0,)), ((), ())), preferred_element_type=F32)


def gelu_and_slope(pre):
    size = jnp.abs(pre)
    t = 1.0 / (1.0 + SLOPE * size)
    poly = jnp.full_like(t, COEFFICIENTS[-1])
    for term in COEFFICIENTS[-2::-1]:
        poly = poly * t + term
    bell = jnp.exp2(pre * pre * (-0.5 * LOG2E))
    lower = poly * t * bell
    cdf = jnp.where(pre >= 0, 1.0 - lower, lower)
    return pre * cdf, cdf + pre * bell * (1.0 / math.sqrt(2.0 * math.pi))


def moments(hidden):
    center = hidden - jnp.mean(hidden, -1, keepdims=True)
    return center, lax.rsqrt(jnp.mean(center * center, -1, keepdims=True) + EPS)


def norm_back(normed, rate, gain, grad):
    scaled = grad * gain
    shared = jnp.mean(scaled * normed, -1, keepdims=True)
    return rate * (scaled - jnp.mean(scaled, -1, keepdims=True) - normed * shared)


def column_sum(values):
    return jnp.sum(values, 0, keepdims=True)


class Place:
    def __init__(self, deep):
        batch, tm = lax.axis_index("batch"), lax.axis_index("tm")
        self.deep = deep
        self.batch, self.tm = batch, tm
        self.z, self.y = batch // 2, batch % 2
        self.x, self.c = tm // 2, tm % 2

    def device(self, z=None, y=None, x=None, c=None):
        z = self.z if z is None else z
        y = self.y if y is None else y
        x = self.x if x is None else x
        c = self.c if c is None else c
        return (z * 2 + y, x * 2 + c)

    def mate(self, k):
        return (self.x + k // 2) % 2 * 2 + (self.c + k % 2) % 2

    def enter(self):
        barrier = pltpu.get_barrier_semaphore()
        others = [self.device(c=1 - self.c), self.device(x=1 - self.x), self.device(y=1 - self.y)]
        others.append(self.device(x=1 - self.x, c=1 - self.c))
        others += [self.device(z=(self.z + d) % self.deep) for d in range(1, self.deep)]
        for other in others:
            pl.semaphore_signal(barrier, inc=1, device_id=other, device_id_type=MESH)
        pl.semaphore_wait(barrier, len(others))


def remote(src, dst, send, recv, device):
    return pltpu.make_async_remote_copy(
        src_ref=src, dst_ref=dst, send_sem=send, recv_sem=recv, device_id=device, device_id_type=MESH
    )


class Route:
    def __init__(self, place, order, crossed):
        self.place, self.order, self.crossed = place, order, crossed
        c = place.c
        self.own = {
            "z": place.z,
            "p": c * place.y + (1 - c) * place.x if crossed else place.x,
            "q": c * place.x + (1 - c) * place.y if crossed else place.y,
        }
        self.size = {"z": place.deep, "p": 2, "q": 2}
        self.sizes = [self.size[axis] for axis in order]

    def shifted(self, shifts):
        at = {a: (self.own[a] + s % self.size[a]) % self.size[a] for a, s in zip(self.order, shifts)}
        c = self.place.c
        if self.crossed:
            return at["z"], c * at["p"] + (1 - c) * at["q"], c * at["q"] + (1 - c) * at["p"]
        return at["z"], at["q"], at["p"]

    def device(self, shifts):
        z, y, x = self.shifted(shifts)
        return self.place.device(z=z, y=y, x=x)

    def chip(self, shifts):
        z, y, x = self.shifted(shifts)
        return (z * 2 + y) * 2 + x

    def offsets(self, upto):
        found = [()]
        for stage, size in enumerate(self.sizes):
            found = [f + (o,) for f in found for o in range(size if stage < upto else 1)]
        return found

    def index(self, offset):
        flat = 0
        for o, size in zip(offset, self.sizes):
            flat = flat * size + o
        return flat


class Gather:
    def __init__(self, place, route, shard, joined, full, local, sends, recvs):
        self.place, self.route = place, route
        self.shard, self.joined, self.full = shard, joined, full
        self.local, self.sends, self.recvs = local, sends, recvs
        self.rows = shard.shape[0]
        self.half = joined.shape[1]
        self.count = 0

    def columns(self, c):
        return pl.ds(pl.multiple_of(c * self.half, 128), self.half)

    def region(self, chip, c):
        rows = 2 * self.rows
        return self.full.at[pl.ds(pl.multiple_of(chip * rows, 16), rows), self.columns(c)]

    def ship(self, src, dst, recv, device):
        remote(src, dst, self.sends.at[self.count], recv, device).start()
        self.count += 1

    def join(self):
        place = self.place
        own = pl.ds(pl.multiple_of(place.c * self.rows, 8), self.rows)
        self.mine = pltpu.make_async_copy(
            self.shard.at[:, self.columns(place.c)], self.joined.at[own], self.local
        )
        self.mine.start()
        self.pair = self.recvs.at[0]
        self.ship(
            self.shard.at[:, self.columns(1 - place.c)],
            self.joined.at[own],
            self.recvs.at[0],
            place.device(c=1 - place.c),
        )

    def arrive(self, offset, stage):
        route, place = self.route, self.place
        chip = route.chip([-o for o in offset])
        block = self.region(chip, place.c)
        for later in range(stage + 1, 3):
            for d in range(1, route.sizes[later]):
                shifts = [0, 0, 0]
                shifts[later] = d
                seen = list(offset)
                seen[later] = d
                self.ship(block, block, self.recvs.at[1 + route.index(seen)], route.device(shifts))
        total = math.prod(route.sizes)
        self.ship(
            block,
            block,
            self.recvs.at[1 + total + route.index(offset)],
            place.device(c=1 - place.c),
        )

    def first(self):
        place = self.place
        self.mine.wait()
        own = pl.ds(pl.multiple_of((1 - place.c) * self.rows, 8), self.rows)
        remote(
            self.joined.at[own], self.joined.at[own], self.sends.at[0], self.recvs.at[0], place.device(c=1 - place.c)
        ).wait()
        chip = self.route.chip([0, 0, 0])
        self.region(chip, place.c)[...] = self.joined[...].astype(BF)
        self.arrive((0, 0, 0), -1)

    def stage(self, stage, some=slice(None)):
        route = self.route
        for offset in [o for o in route.offsets(stage + 1) if o[stage] > 0][some]:
            block = self.region(route.chip([-o for o in offset]), self.place.c)
            remote(
                block, block, self.sends.at[0], self.recvs.at[1 + route.index(offset)], self.place.device()
            ).wait_recv()
            self.arrive(offset, stage)

    def finish(self):
        route = self.route
        total = math.prod(route.sizes)
        for offset in route.offsets(3):
            block = self.region(route.chip([-o for o in offset]), 1 - self.place.c)
            remote(
                block,
                block,
                self.sends.at[0],
                self.recvs.at[1 + total + route.index(offset)],
                self.place.device(),
            ).wait_recv()

    def drain(self):
        block = self.region(self.route.chip([0, 0, 0]), self.place.c)
        for n in range(1, self.count):
            remote(block, block, self.sends.at[n], self.recvs.at[0], self.place.device()).wait_send()


class VectorSum:
    def __init__(self, place, held, slots, sends, recvs):
        self.held, self.slots = held, slots
        stages = [
            [place.device(c=1 - place.c)],
            [place.device(x=1 - place.x)],
            [place.device(y=1 - place.y)],
            [place.device(z=(place.z + d) % place.deep) for d in range(1, place.deep)],
        ]
        self.copies, slot = [], 0
        for stage, others in enumerate(stages):
            self.copies.append([])
            for other in others:
                copy = remote(held.at[stage], slots.at[slot], sends.at[slot], recvs.at[slot], other)
                self.copies[-1].append((copy, slot))
                slot += 1

    def send(self, stage):
        for copy, _ in self.copies[stage]:
            copy.start()

    def add(self, stage):
        total = self.held[stage]
        for copy, slot in self.copies[stage]:
            copy.wait()
            total = total + self.slots[slot]
        self.held[stage + 1] = total


def fill_vectors(block, mask_embed, norm_gain, norm_shift, qv_bias, branch_bias, up_bias):
    block[...] = jnp.zeros_like(block)
    piece = mask_embed.shape[1]
    row = 0
    for part in (mask_embed, norm_gain, norm_shift, qv_bias):
        block[row : row + part.shape[0], 0:piece] = part[...]
        row += part.shape[0]
    block[row : row + 1, 0:piece] = branch_bias[0:1, :]
    block[0:1, 128 : 128 + piece] = branch_bias[1:2, :]
    block[1:2, 128 : 128 + up_bias.shape[1]] = up_bias[...]


def spread_vectors(blocks, vectors):
    width = vectors.shape[1]
    devices = blocks.shape[0] // 8
    piece = width // devices
    table = blocks[...].astype(F32)
    vectors[...] = jnp.zeros_like(vectors)

    def put(rows, at, start):
        window = min(start // 128 * 128, width - 256)
        wide = jnp.concatenate([rows, jnp.zeros_like(rows)], 1)
        wide = pltpu.roll(wide, start - window, 1)
        vectors[at, window : window + 256] = vectors[at, window : window + 256] + wide

    for d in range(devices):
        block = table[8 * d : 8 * d + 8]
        put(block[:, :128], slice(0, 8), piece * d)
        put(block[0:1, 128:], slice(8, 9), piece * d)
        up = 4 * piece * d
        put(block[1:2, 128:], slice(9 + up // width, 10 + up // width), up % width)


def column_of(table, source, row):
    line = table[source, pl.ds(row, 1), :].astype(F32)
    tall = jnp.broadcast_to(line, (8, line.shape[1]))
    return jnp.concatenate([tall[:, n : n + 128].T[:, 0:1] for n in range(0, line.shape[1], 128)], 0)


def forward_kernel(
    deep,
    patches,
    cotangent,
    flags_in,
    clips_in,
    mask_embed,
    norm_gain,
    norm_shift,
    qv_bias,
    branch_bias,
    up_bias,
    shard_qkv,
    shard_out,
    shard_up,
    shard_down,
    o_qkv,
    o_out,
    o_up,
    o_down,
    o_small,
    o_x,
    o_cot,
    o_flags,
    o_first,
    o_q,
    o_k,
    o_v,
    o_mixed,
    o_second,
    o_rate,
    o_middle,
    o_act,
    o_slope,
    o_expon,
    o_result,
    w_qkv,
    w_out,
    w_up,
    w_down,
    j_qkv,
    j_out,
    j_up,
    j_down,
    j_vector,
    shard_vector,
    w_vector,
    small,
    x,
    flags_all,
    clips_all,
    first,
    q,
    k,
    v,
    mixed,
    second,
    rate,
    middle,
    expon,
    slope,
    result,
    q_code,
    k_code,
    join_sems,
    gather_sends,
    gather_recvs,
    row_sends,
    row_recvs,
    local_sems,
    expon_sems,
    act_sems,
):
    place = Place(deep)
    span, width = patches.shape[1:]
    rows = x.shape[0]
    sources = rows // span
    half = width // HEADS
    pairs = HEADS // 2
    inner = w_up.shape[1]
    chunks = inner // width

    fill_vectors(shard_vector, mask_embed, norm_gain, norm_shift, qv_bias, branch_bias, up_bias)
    place.enter()

    kinds = ((patches, x), (flags_in, flags_all), (clips_in, clips_all), (cotangent, o_cot))

    def landing(kind, source):
        dst = kinds[kind][1]
        if kind in (1, 2):
            return dst.at[source]
        return dst.at[pl.ds(pl.multiple_of(source * span, span), span)]

    def leaving(kind, to):
        src = kinds[kind][0]
        return src if kind in (1, 2) else src.at[to]

    def own_part(kind):
        return pltpu.make_async_copy(
            leaving(kind, place.tm), landing(kind, place.tm), local_sems.at[kind]
        )

    def row_copy(kind, step, to):
        return remote(
            leaving(kind, to),
            landing(kind, place.tm),
            row_sends.at[kind, step],
            row_recvs.at[kind, step],
            (place.batch, to),
        )

    def row_wait(kind, step):
        source = place.mate(step)
        there = landing(kind, source)
        remote(
            there, there, row_sends.at[kind, step], row_recvs.at[kind, step], (place.batch, source)
        ).wait_recv()

    zpq = Route(place, "zpq", True)
    zxy = Route(place, "zpq", False)
    pzq = Route(place, "pzq", True)
    xzy = Route(place, "pzq", False)
    named = {}
    for i, (name, route, shard, joined, full) in enumerate(
        (
            (VECTOR, zpq, shard_vector, j_vector, w_vector),
            (QKV, zxy, shard_qkv, j_qkv, w_qkv),
            (OUT, zxy, shard_out, j_out, w_out),
            (UP, zpq, shard_up, j_up, w_up),
            (DOWN, pzq, shard_down, j_down, w_down),
        )
    ):
        named[name] = Gather(
            place, route, shard, joined, full, join_sems.at[i], gather_sends.at[i], gather_recvs.at[i]
        )
    gathers = list(named.values())
    for gather in gathers:
        gather.join()
    def send_rows(kinds):
        for kind in kinds:
            for step in range(1, sources):
                row_copy(kind, step, place.mate(step)).start()

    def run(steps):
        for what, *which in steps:
            if what == ROWS:
                send_rows((1, 2, 0))
            elif what == COTANGENT:
                send_rows((3,))
            elif what == SPREAD:
                spread_vectors(w_vector, small)
            elif what == FIRST:
                named[which[0]].first()
            elif what == FINISH:
                named[which[0]].finish()
            else:
                named[which[0]].stage(which[1], slice(which[2], which[3]))

    def after(loop, index):
        for when, steps in FORWARD_STEPS.get(loop, {}).items():
            if isinstance(index, int):
                if index == when:
                    run(steps)
            else:
                pl.when(index == when)(functools.partial(run, steps))

    for kind in (1, 2, 0):
        own_part(kind).start()
    run(FORWARD_STEPS[START][0])
    keeping = []

    def keep(src, dst):
        copy = pltpu.make_async_copy(src, dst, local_sems.at[4 + len(keeping)])
        copy.start()
        keeping.append(copy)


    vectors = small
    lane = lax.broadcasted_iota(jnp.int32, (1, 2 * half), 1)
    low = lane < half
    own_lanes = [low.astype(F32), 1.0 - low.astype(F32)]

    for kind in (1, 2, 0):
        own_part(kind).wait()

    @pl.loop(0, sources)
    def _(step):
        @pl.when(step > 0)
        def _():
            for kind in (1, 2, 0):
                row_wait(kind, step)

        source = place.mate(step)
        at = pl.ds(pl.multiple_of(source * span, span), span)
        flags = column_of(flags_all, source, place.tm)
        clips = column_of(clips_all, source, place.tm)
        start = jnp.where(flags == 1.0, vectors[0:1, :], x[at, :].astype(F32))
        middle[at, :] = start
        center, speed = moments(start)
        normed = (center * speed * vectors[1:2, :] + vectors[3:4, :]).astype(BF)
        first[at, :] = normed
        q[at, :] = (nn(normed, w_qkv[:, 0:width]) + vectors[5:6, :]).astype(BF) * (1.0 / math.sqrt(half))
        k[at, :] = nn(normed, w_qkv[:, width : 2 * width]).astype(BF)
        v[at, :] = (nn(normed, w_qkv[:, 2 * width :]) + vectors[6:7, :]).astype(BF)
        clip_lane = lax.broadcasted_iota(jnp.int32, (span, 2 * half), 1).astype(F32)
        for h in range(2):
            base = float(half * (1 - h))
            same = clip_lane - base == clips
            coded = jnp.logical_and(clip_lane >= base, clip_lane < base + 5.0)
            q_code[h, at, :] = jnp.where(same, 1.0, 0.0).astype(BF)
            k_code[h, at, :] = jnp.where(jnp.logical_and(coded, jnp.logical_not(same)), FAR, 0.0).astype(BF)
        after(PROJECT, step)

    for src, dst in ((w_qkv, o_qkv), (small, o_small), (x, o_x), (flags_all, o_flags), (first, o_first), (q, o_q), (k, o_k), (v, o_v)):
        keep(src, dst)

    block = min(rows, 512)

    def expon_copy(p):
        return pltpu.make_async_copy(expon.at[p % 2], o_expon.at[pl.ds(2 * p, 2)], expon_sems.at[p % 2])

    def attend(p):
        lanes = pl.ds(pl.multiple_of(p * 2 * half, 128), 2 * half)

        @pl.when(p >= 2)
        def _():
            expon_copy(p - 2).wait()

        slot = p % 2
        keys, values = [], []
        for h in range(2):
            mask = own_lanes[h].astype(BF)
            keys.append(k[:, lanes] * mask + k_code[h])
            values.append(v[:, lanes] * mask + own_lanes[1 - h].astype(BF))
        for part in range(rows // block):
            at = pl.ds(part * block, block)
            mixes = []
            for h in range(2):
                query = q[at, lanes] * own_lanes[h].astype(BF) + q_code[h, at, :]
                scores = nt(query, keys[h])
                peak = jnp.max(scores, -1, keepdims=True)
                weights = jnp.exp2((scores - peak) * LOG2E).astype(BF)
                expon[slot, h, at, :] = weights
                mixes.append(nn(weights, values[h]))
            top = jnp.where(low, mixes[0], mixes[1])
            totals = pltpu.roll(jnp.where(low, mixes[1], mixes[0]), half, 1)
            speed = 1.0 / totals
            rate[at, lanes] = speed
            mixed[at, lanes] = (top * speed).astype(BF)
        expon_copy(p).start()
        after(ATTEND, p)

    pl.loop(0, pairs)(attend)
    for src, dst in ((w_out, o_out), (w_up, o_up), (mixed, o_mixed), (rate, o_rate)):
        keep(src, dst)
    for p in (pairs - 2, pairs - 1):
        expon_copy(p).wait()

    def act(j, at):
        return expon.at[j // 2, j % 2, at, pl.ds(0, width)]

    def slope_copies(step):
        at = pl.ds(pl.multiple_of(step * span, span), span)
        return [
            pltpu.make_async_copy(slope.at[step % 2, j], o_slope.at[j, at], act_sems.at[step % 2, j])
            for j in range(chunks)
        ]

    def act_copies(step):
        at = pl.ds(pl.multiple_of(step * span, span), span)
        return [pltpu.make_async_copy(act(j, at), o_act.at[j, at], act_sems.at[2, j]) for j in range(chunks)]

    def rise(step):
        @pl.when(step >= 2)
        def _():
            for copy in slope_copies(step - 2):
                copy.wait()

        at = pl.ds(pl.multiple_of(step * span, span), span)
        hidden = middle[at, :] + nn(mixed[at, :], w_out[...]) + vectors[7:8, :]
        middle[at, :] = hidden
        center, speed = moments(hidden)
        normed = (center * speed * vectors[2:3, :] + vectors[4:5, :]).astype(BF)
        second[at, :] = normed
        for j in range(chunks):
            pre = nn(normed, w_up[:, j * width : (j + 1) * width]) + vectors[9 + j : 10 + j, :]
            value, steep = gelu_and_slope(pre)
            expon[j // 2, j % 2, at, 0:width] = value.astype(BF)
            slope[step % 2, j] = steep.astype(BF)
        for copy in slope_copies(step) + act_copies(step):
            copy.start()
        after(RISE, step)

    def fall(step):
        at = pl.ds(pl.multiple_of(step * span, span), span)
        total = middle[at, :] + vectors[8:9, :]
        for j in range(chunks):
            total = total + nn(expon[j // 2, j % 2, at, 0:width], w_down[j * width : (j + 1) * width, :])
        result[at, :] = total.astype(BF)

    pl.loop(0, sources)(rise)
    keep(second, o_second)
    keep(middle, o_middle)
    keep(w_down, o_down)
    pl.loop(0, sources)(fall)
    keep(result, o_result)
    for step in range(sources):
        for copy in act_copies(step):
            copy.wait()
    for step in (sources - 2, sources - 1):
        for copy in slope_copies(step):
            copy.wait()
    for step in range(1, sources):
        row_wait(3, step)
        for kind in range(4):
            row_copy(kind, step, place.mate(step)).wait_send()
    for copy in keeping:
        copy.wait()
    for gather in gathers:
        gather.drain()


def forward(deep, patches, cotangent, flags, clips, vectors, shards):
    sources, span, width = patches.shape
    qkv, out, up, down = shards
    rows = sources * span
    chips = deep * 4
    inner = up.shape[1]
    chunks = inner // width
    shape = jax.ShapeDtypeStruct
    fulls = [(2 * chips * s.shape[0], s.shape[1]) for s in shards]
    plane = (rows, width)
    outs = [shape(f, BF) for f in fulls]
    outs += [shape((16, width), F32), shape(plane, BF), shape(plane, BF)]
    outs += [shape((sources,) + flags.shape, jnp.int32)]
    outs += [shape(plane, BF)] * 6 + [shape(plane, F32)] * 2
    outs += [shape((chunks, rows, width), BF)] * 2
    outs += [shape((HEADS, rows, rows), BF), shape(plane, BF)]
    scratch = [pltpu.VMEM(f, BF) for f in fulls]
    scratch += [pltpu.VMEM((2 * s.shape[0], s.shape[1] // 2), F32) for s in shards]
    scratch += [
        pltpu.VMEM((16, 128), F32),
        pltpu.VMEM((8, 256), F32),
        pltpu.VMEM((16 * chips, 256), BF),
        pltpu.VMEM((16, width), F32),
        pltpu.VMEM(plane, BF),
        pltpu.VMEM((sources,) + flags.shape, jnp.int32),
        pltpu.VMEM((sources,) + flags.shape, jnp.int32),
    ]
    scratch += [pltpu.VMEM(plane, BF)] * 6 + [pltpu.VMEM(plane, F32)] * 2
    scratch += [
        pltpu.VMEM((2, 2, rows, rows), BF),
        pltpu.VMEM((2, chunks, span, width), BF),
        pltpu.VMEM(plane, BF),
        pltpu.VMEM((2, rows, 128), BF),
        pltpu.VMEM((2, rows, 128), BF),
    ]
    dma = pltpu.SemaphoreType.DMA
    scratch += [
        dma((5,)),
        dma((5, 1 + 2 * chips)),
        dma((5, 1 + 2 * chips)),
        dma((4, sources)),
        dma((4, sources)),
        dma((20,)),
        dma((2,)),
        dma((3, chunks)),
    ]
    return pl.pallas_call(
        functools.partial(forward_kernel, deep),
        out_shape=outs,
        in_specs=[HBM] * 4 + [pl.BlockSpec(memory_space=pltpu.VMEM)] * 6 + [HBM] * 4,
        out_specs=[HBM] * len(outs),
        scratch_shapes=scratch,
        compiler_params=pltpu.CompilerParams(
            collective_id=0, has_side_effects=True, vmem_limit_bytes=62 * 2**20
        ),
        name="forward",
    )(patches, cotangent, flags, clips, *vectors, *shards)


class Scatter:
    def __init__(self, place, route, held, slots, final, sends, recvs, piece=None):
        self.place, self.route = place, route
        self.held, self.slots, self.final = held, slots, final
        self.sends, self.recvs = sends, recvs
        self.rows = slots.shape[1]
        self.width = piece
        self.sent = []

    def region(self, shifts):
        return pl.ds(pl.multiple_of(self.route.chip(shifts) * self.rows, 16), self.rows)

    def columns(self, piece):
        if piece is None:
            return pl.ds(0, self.held.shape[1])
        return pl.ds(pl.multiple_of(piece * self.width, 128), self.width)

    def parts(self, stage):
        route = self.route
        for d in range(1, route.sizes[stage]):
            for earlier in route.offsets(stage):
                offset = list(earlier)
                offset[stage] = d
                yield d, [-o for o in earlier], route.index(offset) - 1

    def copy(self, stage, d, back, slot, piece):
        shifts, to = list(back), [0, 0, 0]
        shifts[stage] = to[stage] = d
        columns = self.columns(piece)
        n = 0 if piece is None else piece
        return remote(
            self.held.at[self.region(shifts), columns],
            self.slots.at[slot, :, columns],
            self.sends.at[n, slot],
            self.recvs.at[n, slot],
            self.route.device(to),
        )

    def send(self, stage, piece=None):
        self.sent.append((stage, piece))
        for d, back, slot in self.parts(stage):
            self.copy(stage, d, back, slot, piece).start()

    def add(self, stage, piece=None):
        found = {}
        columns = self.columns(piece)
        for d, back, slot in self.parts(stage):
            self.copy(stage, d, back, slot, piece).wait_recv()
            found.setdefault(tuple(back), []).append(slot)
        for back, slots in found.items():
            at = self.region(back)
            total = self.held[at, columns].astype(F32)
            for slot in slots:
                total = total + self.slots[slot, :, columns].astype(F32)
            if stage == 0:
                self.final[:, columns] = total
            else:
                self.held[at, columns] = total.astype(BF)

    def drain(self):
        for stage, piece in self.sent:
            for d, back, slot in self.parts(stage):
                self.copy(stage, d, back, slot, piece).wait_send()


class RowScatter(Scatter):
    def part_q(self, z, p):
        place = self.place
        behind = (place.z - z + place.deep) % place.deep
        return [p, (place.deep - behind) % place.deep, 0], (p * place.deep + behind) * 2

    def copy_q(self, z, p):
        shifts, slot = self.part_q(z, p)
        return self.copy(2, 1, shifts, slot, None)

    def send_q(self, z):
        for p in range(2):
            self.copy_q(z, p).start()

    def add_q(self, z):
        for p in range(2):
            shifts, slot = self.part_q(z, p)
            self.copy_q(z, p).wait_recv()
            at = self.region(shifts)
            self.held[at, :] = (self.held[at, :].astype(F32) + self.slots[slot].astype(F32)).astype(BF)

    def copy_z(self, z, p):
        place = self.place
        ahead = (z - place.z + place.deep) % place.deep
        return self.copy(1, ahead, [p, 0, 0], (p * place.deep + ahead) * 2 - 1, None)

    def send_z(self, z):
        @pl.when(self.place.z != z)
        def _():
            for p in range(2):
                self.copy_z(z, p).start()

    def drain(self):
        place = self.place
        for z in range(place.deep):
            for p in range(2):
                self.copy_q(z, p).wait_send()
        for d, back, slot in self.parts(1):
            self.copy(1, d, back, slot, None).wait_send()
        super().drain()


def backward_kernel(
    deep,
    i_qkv,
    i_out,
    i_up,
    i_down,
    i_small,
    i_x,
    i_cot,
    i_flags,
    i_first,
    i_q,
    i_k,
    i_v,
    i_mixed,
    i_second,
    i_rate,
    i_middle,
    i_act,
    i_slope,
    i_expon,
    i_result,
    i_own_cot,
    o_qkv,
    o_out,
    o_up,
    o_down,
    o_small,
    o_patch,
    o_result,
    w_qkv,
    w_out,
    w_up,
    w_down,
    upstream,
    second,
    gathered,
    middle,
    expon,
    score_grad,
    trio,
    rate,
    mixed,
    staged,
    h_qkv,
    h_out,
    h_up,
    h_down,
    s_qkv,
    s_out,
    s_up,
    s_down,
    f_qkv,
    f_out,
    f_up,
    f_down,
    vectors,
    flags_all,
    small,
    small_slots,
    patch,
    load_sems,
    chunk_sems,
    pair_sems,
    hand_sends,
    hand_recvs,
    scatter_sends,
    scatter_recvs,
    final_sends,
    final_recvs,
    small_sends,
    small_recvs,
    row_sends,
    row_recvs,
    local_sems,
):
    place = Place(deep)
    rows, width = upstream.shape
    sources, span = patch.shape[:2]
    half = width // HEADS
    pairs = HEADS // 2
    chunks = i_act.shape[0]
    part = width // 2
    first = second
    mixed_grad = upstream
    first_grad = gathered

    loads = [
        pltpu.make_async_copy(src, dst, load_sems.at[i])
        for i, (src, dst) in enumerate(
            (
                (i_second, second),
                (i_middle, middle),
                (i_small, vectors),
                (i_flags, flags_all),
                (i_out, w_out),
                (i_qkv, w_qkv),
            )
        )
    ]

    def chunk_loads(j):
        slot = j % 2
        columns = pl.ds(pl.multiple_of(j * width, 128), width)
        moves = (
            (i_down.at[columns], w_down.at[slot]),
            (i_up.at[:, columns], w_up.at[slot]),
            (i_act.at[j], expon.at[slot, 0, :, pl.ds(0, width)]),
            (i_slope.at[j], expon.at[slot, 1, :, pl.ds(0, width)]),
        )
        return [pltpu.make_async_copy(src, dst, chunk_sems.at[slot, n]) for n, (src, dst) in enumerate(moves)]

    def pair_loads(p):
        slot = p % 2
        lanes = pl.ds(pl.multiple_of(p * 2 * half, 128), 2 * half)
        moves = (
            (i_expon.at[pl.ds(2 * p, 2)], expon.at[slot]),
            (i_q.at[:, lanes], trio.at[slot, 0]),
            (i_k.at[:, lanes], trio.at[slot, 1]),
            (i_v.at[:, lanes], trio.at[slot, 2]),
            (i_rate.at[:, lanes], rate.at[slot]),
            (i_mixed.at[:, lanes], mixed.at[slot]),
        )
        return [pltpu.make_async_copy(src, dst, pair_sems.at[slot, n]) for n, (src, dst) in enumerate(moves)]

    for step in range(sources):
        source = place.mate(step)
        at = pl.ds(pl.multiple_of(source * span, span), span)
        loads.insert(
            step,
            pltpu.make_async_copy(
                i_own_cot.at[place.tm] if step == 0 else i_cot.at[at], upstream.at[at], load_sems.at[6 + step]
            ),
        )
    early = sources + 1
    for copy in loads[:early] + chunk_loads(0) + loads[early:]:
        copy.start()
    place.enter()

    def result_copy(step):
        to = place.mate(step)
        return remote(
            i_result.at[pl.ds(pl.multiple_of(to * span, span), span)],
            o_result.at[place.tm],
            row_sends.at[1, step],
            row_recvs.at[1, step],
            (place.batch, to),
        )

    result_in = pltpu.make_async_copy(
        i_result.at[pl.ds(pl.multiple_of(place.tm * span, span), span)], patch.at[sources - 1], local_sems.at[5]
    )
    result_in.start()
    result_out = pltpu.make_async_copy(patch.at[sources - 1], o_result.at[place.tm], local_sems.at[5])
    for step in range(1, sources):
        result_copy(step).start()

    zpq = Route(place, "zpq", True)
    pzq = Route(place, "pzq", True)
    xzy = Route(place, "pzq", False)
    zxy = Route(place, "zpq", False)
    by_qkv = Scatter(place, xzy, h_qkv, s_qkv, f_qkv, scatter_sends.at[0], scatter_recvs.at[0], part)
    by_out = Scatter(place, zxy, h_out, s_out, f_out, scatter_sends.at[1], scatter_recvs.at[1], part)
    by_up = Scatter(place, zpq, h_up, s_up, f_up, scatter_sends.at[2], scatter_recvs.at[2], part)
    by_down = RowScatter(place, pzq, h_down, s_down, f_down, scatter_sends.at[3], scatter_recvs.at[3])
    scatters = [by_qkv, by_out, by_up, by_down]

    def columns(c):
        return pl.ds(pl.multiple_of(c * part, 128), part)

    def hand(slot, held, n):
        return remote(
            staged.at[slot, :, columns(1 - place.c)],
            held,
            hand_sends.at[n],
            hand_recvs.at[n],
            place.device(c=1 - place.c),
        )

    def settle(slot, held, n):
        copy = hand(slot, held, n)
        copy.wait_recv()
        held[...] = (held[...].astype(F32) + staged[slot, :, columns(place.c)].astype(F32)).astype(BF)
        copy.wait_send()

    def down_chunk(j):
        return (2 * (j % 2), h_down.at[pl.ds(pl.multiple_of(j * width, 128), width)], j)

    def up_chunk(j):
        return (2 * (j % 2) + 1, h_up.at[:, pl.ds(pl.multiple_of(j * part, 128), part)], chunks + j)

    def qkv_chunk(i):
        return (1 + i, h_qkv.at[:, pl.ds(pl.multiple_of(i * part, 128), part)], 2 * chunks + 1 + i)

    def out_chunk(i):
        return (0, h_out, 2 * chunks)

    named = {
        QKV: (by_qkv, qkv_chunk),
        OUT: (by_out, out_chunk),
        UP: (by_up, up_chunk),
        DOWN: (by_down, down_chunk),
    }
    summed = VectorSum(place, small, small_slots, small_sends, small_recvs)

    def run(steps):
        for what, *which in steps:
            if what == VECTOR_SEND:
                summed.send(which[0])
            elif what == VECTOR_ADD:
                summed.add(which[0])
            elif what == TURN:
                by_down.add_q(which[0])
                by_down.send_z(which[0])
            elif what == DELIVER:
                deliver(*deliveries[which[0]])
            elif what == SETTLE:
                scatter, chunk = named[which[0]]
                settle(*chunk(which[1]))
                if scatter is by_down:
                    scatter.send_q(which[1])
                else:
                    scatter.send(2, which[1])
            else:
                scatter = named[which[0]][0]
                stage = which[1]
                piece = None if scatter is by_down else which[2]
                scatter.add(stage, piece)
                if stage > 0:
                    scatter.send(stage - 1, piece)

    def after(loop, index):
        for when, steps in BACKWARD_STEPS.get(loop, {}).items():
            if isinstance(index, int):
                if index == when:
                    run(steps)
            else:
                pl.when(index == when)(functools.partial(run, steps))

    for copy in loads[:early]:
        copy.wait()

    def feed(j):
        @pl.when(j < chunks - 1)
        def _():
            for copy in chunk_loads(j + 1):
                copy.start()

        for copy in chunk_loads(j):
            copy.wait()
        slot = j % 2
        act_grad = nt(upstream[...], w_down[slot]).astype(BF).astype(F32)
        pre_grad = (act_grad * expon[slot, 1, :, 0:width].astype(F32)).astype(BF)
        small[0, pl.ds(9 + j, 1), :] = column_sum(pre_grad.astype(F32))
        staged[down_chunk(j)[0]] = tn(expon[slot, 0, :, 0:width], upstream[...]).astype(BF)
        hand(*down_chunk(j)).start()
        staged[up_chunk(j)[0]] = tn(second[...], pre_grad).astype(BF)
        hand(*up_chunk(j)).start()
        grown = nt(pre_grad, w_up[slot])

        @pl.when(j == 0)
        def _():
            gathered[...] = grown

        @pl.when(j > 0)
        def _():
            gathered[...] = gathered[...] + grown

        after(FEED, j)

    pl.loop(0, chunks)(feed)
    whole_mixed = pltpu.make_async_copy(i_mixed, expon.at[1, 1, :, pl.ds(0, width)], local_sems.at[0])
    whole_mixed.start()
    for copy in pair_loads(0):
        copy.start()
    load_first = pltpu.make_async_copy(i_first, first, local_sems.at[1])
    load_first.start()
    for copy in loads[early:]:
        copy.wait()
    for row in (0, 1, 2, 3, 4, 5, 6, 7, 8, 13, 14, 15):
        small[0, row : row + 1, :] = jnp.zeros((1, width), F32)

    def bend(n):
        at = pl.ds(pl.multiple_of(n * span, span), span)
        center, speed = moments(middle[at, :])
        normed = center * speed
        grad = gathered[at, :]
        small[0, 2:3, :] = small[0, 2:3, :] + column_sum(grad * normed)
        small[0, 4:5, :] = small[0, 4:5, :] + column_sum(grad)
        above = upstream[at, :].astype(F32)
        small[0, 8:9, :] = small[0, 8:9, :] + column_sum(above)
        total = above + norm_back(normed, speed, vectors[2:3, :], grad)
        middle[at, :] = total
        low_total = total.astype(BF)
        small[0, 7:8, :] = small[0, 7:8, :] + column_sum(low_total.astype(F32))
        mixed_grad[at, :] = nt(low_total, w_out[...]).astype(BF)

    pl.loop(0, sources)(bend)
    after(BEND, 0)
    whole_mixed.wait()
    staged[0] = tn(expon[1, 1, :, 0:width], middle[...].astype(BF)).astype(BF)
    hand(*out_chunk(0)).start()
    after(MIX, 0)
    load_first.wait()
    result_in.wait()
    result_out.start()

    lane = lax.broadcasted_iota(jnp.int32, (1, 2 * half), 1)
    low = lane < half
    own_lanes = [low.astype(F32), 1.0 - low.astype(F32)]
    block = min(rows, 512)

    def attend(p):
        slot = p % 2
        lanes = pl.ds(pl.multiple_of(p * 2 * half, 128), 2 * half)

        @pl.when(p < pairs - 1)
        def _():
            for copy in pair_loads(p + 1):
                copy.start()

        for copy in pair_loads(p):
            copy.wait()
        scaled = (mixed_grad[:, lanes].astype(F32) * rate[slot]).astype(BF)
        product = scaled.astype(F32) * mixed[slot].astype(F32)
        query, key, value = trio[slot, 0], trio[slot, 1], trio[slot, 2]
        key_grads, value_grads, query_grads = [], [], []
        for h in range(2):
            inner = jnp.sum(product * own_lanes[h], -1, keepdims=True)
            lone = scaled * own_lanes[h].astype(BF)
            query_parts = []
            for n in range(rows // block):
                at = slice(n * block, (n + 1) * block)
                grad = nt(lone[at], value)
                weights = expon[slot, h, at, :].astype(F32)
                grad = (weights * (grad - inner[at])).astype(BF)
                score_grad[h, at, :] = grad
                query_parts.append(nn(grad, key))
            query_grads.append(jnp.concatenate(query_parts, 0))
            key_grads.append(tn(query, score_grad[h]))
            value_grads.append(tn(scaled, expon[slot, h]))
        query_grad = (jnp.where(low, query_grads[0], query_grads[1]) * (1.0 / math.sqrt(half))).astype(BF)
        key_grad = jnp.concatenate([key_grads[0][:half], key_grads[1][half:]], 0).T.astype(BF)
        value_grad = jnp.concatenate([value_grads[0][:half], value_grads[1][half:]], 0).T.astype(BF)
        small[0, 5:6, lanes] = column_sum(query_grad.astype(F32))
        small[0, 6:7, lanes] = column_sum(value_grad.astype(F32))
        grads = jnp.concatenate([query_grad, key_grad, value_grad], 1)
        where = pl.ds(pl.multiple_of(slot * part, 128), part)
        staged[1 + p // 2, :, where] = tn(first[...], grads).astype(BF)
        weight = jnp.concatenate(
            [w_qkv[:, pl.ds(pl.multiple_of(p * 2 * half + n * width, 128), 2 * half)] for n in range(3)], 1
        )
        grown = nt(grads, weight)

        @pl.when(p == 0)
        def _():
            first_grad[...] = grown

        @pl.when(p > 0)
        def _():
            first_grad[...] = first_grad[...] + grown

        @pl.when(p % 2 == 1)
        def _():
            hand(*qkv_chunk(p // 2)).start()

        after(ATTEND, p)

    pl.loop(0, pairs)(attend)
    load_x = pltpu.make_async_copy(i_x, expon.at[0, 0, :, pl.ds(0, width)], local_sems.at[2])
    load_x.start()
    load_x.wait()
    result_out.wait()

    def close(step):
        source = place.mate(sources - 1 - step)
        at = pl.ds(pl.multiple_of(source * span, span), span)
        flags = column_of(flags_all, source, place.tm) == 1.0
        start = jnp.where(flags, vectors[0:1, :], expon[0, 0, at, 0:width].astype(F32))
        center, speed = moments(start)
        normed = center * speed
        grad = first_grad[at, :]
        small[0, 1:2, :] = small[0, 1:2, :] + column_sum(grad * normed)
        small[0, 3:4, :] = small[0, 3:4, :] + column_sum(grad)
        total = middle[at, :] + norm_back(normed, speed, vectors[1:2, :], grad)
        small[0, 0:1, :] = small[0, 0:1, :] + column_sum(jnp.where(flags, total, 0.0))
        patch[step] = jnp.where(flags, 0.0, total).astype(BF)

        @pl.when(step < sources - 1)
        def _():
            remote(
                patch.at[step],
                o_patch.at[place.tm],
                row_sends.at[0, sources - 1 - step],
                row_recvs.at[0, sources - 1 - step],
                (place.batch, source),
            ).start()

        after(CLOSE, step)

    pl.loop(0, sources)(close)
    own_patch = pltpu.make_async_copy(patch.at[sources - 1], o_patch.at[place.tm], local_sems.at[3])
    own_patch.start()
    moves = []

    def deliver(final, target, pieces):
        shard = target.shape[0]
        for near, far, jump, size in pieces:
            to = pl.ds(pl.multiple_of(far + place.c * jump, 128), size)
            mine = pl.ds(pl.multiple_of(place.c * shard, 8), shard)
            theirs = pl.ds(pl.multiple_of((1 - place.c) * shard, 8), shard)
            n = len(moves) // 2
            moves.append(
                pltpu.make_async_copy(final.at[mine, pl.ds(near, size)], target.at[:, to], local_sems.at[6 + n])
            )
            moves.append(
                remote(
                    final.at[theirs, pl.ds(near, size)],
                    target.at[:, to],
                    final_sends.at[n],
                    final_recvs.at[n],
                    place.device(c=1 - place.c),
                )
            )
            moves[-2].start()
            moves[-1].start()

    deliveries = {
        DOWN: (f_down, o_down, [(0, 0, part, part)]),
        UP: (f_up, o_up, [(j * part, j * width, part, part) for j in range(chunks)]),
        OUT: (f_out, o_out, [(0, 0, part, part)]),
        QKV: (
            f_qkv,
            o_qkv,
            [
                (i * part + n * 2 * half, n * width + i * 4 * half, 2 * half, 2 * half)
                for i in range(3)
                for n in range(3)
            ],
        ),
    }
    after(TAIL, 0)
    own_small = pltpu.make_async_copy(small.at[4], o_small, local_sems.at[4])
    own_small.start()
    for move in moves:
        move.wait()
    for step in range(1, sources):
        copy = remote(
            patch.at[0], o_patch.at[place.mate(step)], row_sends.at[0, step], row_recvs.at[0, step], place.device()
        )
        copy.wait_recv()
        copy.wait_send()
        result_copy(step).wait()
    own_patch.wait()
    own_small.wait()
    for scatter in scatters:
        scatter.drain()


def backward(deep, saved, shards, cotangent):
    sources, span, width = cotangent.shape
    rows = sources * span
    chips = deep * 4
    chunks = shards[2].shape[1] // width
    shape = jax.ShapeDtypeStruct
    plane = (rows, width)
    small = saved[4]
    flags = saved[7]
    halves = [(2 * chips * s.shape[0], s.shape[1] // 2) for s in shards]
    outs = [shape(s.shape, F32) for s in shards] + [shape(small.shape, F32)] + [shape(cotangent.shape, BF)] * 2
    scratch = [
        pltpu.VMEM(saved[0].shape, BF),
        pltpu.VMEM(saved[1].shape, BF),
        pltpu.VMEM((2, width, width), BF),
        pltpu.VMEM((2, width, width), BF),
        pltpu.VMEM(plane, BF),
        pltpu.VMEM(plane, BF),
        pltpu.VMEM(plane, F32),
        pltpu.VMEM(plane, F32),
        pltpu.VMEM((2, 2, rows, rows), BF),
        pltpu.VMEM((2, rows, rows), BF),
        pltpu.VMEM((2, 3, rows, 2 * width // HEADS), BF),
        pltpu.VMEM((2, rows, 2 * width // HEADS), F32),
        pltpu.VMEM((2, rows, 2 * width // HEADS), BF),
        pltpu.VMEM((4, width, width), BF),
    ]
    scratch += [pltpu.VMEM(h, BF) for h in halves]
    scratch += [pltpu.VMEM((chips - 1, 2 * s.shape[0], s.shape[1] // 2), BF) for s in shards]
    scratch += [pltpu.VMEM((2 * s.shape[0], s.shape[1] // 2), F32) for s in shards]
    scratch += [
        pltpu.VMEM(small.shape, F32),
        pltpu.VMEM(flags.shape, jnp.int32),
        pltpu.VMEM((5,) + small.shape, F32),
        pltpu.VMEM((2 + deep,) + small.shape, F32),
        pltpu.VMEM(cotangent.shape, BF),
    ]
    dma = pltpu.SemaphoreType.DMA
    scratch += [
        dma((6 + sources,)),
        dma((2, 4)),
        dma((2, 6)),
        dma((2 * chunks + 4,)),
        dma((2 * chunks + 4,)),
        dma((4, chunks, chips - 1)),
        dma((4, chunks, chips - 1)),
        dma((11 + chunks,)),
        dma((11 + chunks,)),
        dma((2 + deep,)),
        dma((2 + deep,)),
        dma((2, sources)),
        dma((2, sources)),
        dma((17 + chunks,)),
    ]
    return pl.pallas_call(
        functools.partial(backward_kernel, deep),
        out_shape=outs,
        in_specs=[HBM] * (len(saved) + 1),
        out_specs=[HBM] * len(outs),
        scratch_shapes=scratch,
        compiler_params=pltpu.CompilerParams(
            collective_id=1, has_side_effects=True, vmem_limit_bytes=63 * 2**20
        ),
        name="backward",
    )(*saved, cotangent)


def by_rows(
    deep,
    patches,
    segment_ids,
    mask_flags,
    cotangent,
    mask_embed,
    norm_gain,
    norm_shift,
    qkv_weight,
    qv_bias,
    out_weight,
    branch_bias,
    up_weight,
    up_bias,
    down_weight,
):
    sources, span, width = patches.shape
    shards = (qkv_weight, out_weight, up_weight, down_weight)
    vectors = (mask_embed[None], norm_gain, norm_shift, qv_bias, branch_bias, up_bias[None])
    saved = forward(deep, patches, cotangent, mask_flags, segment_ids, vectors, shards)
    *grads, sums, patch_grad, result = backward(deep, saved, shards, cotangent)
    device = lax.axis_index("batch") * 4 + lax.axis_index("tm")
    piece = mask_embed.shape[0]
    own = lax.dynamic_slice(sums, (0, device * piece), (9, piece))
    up_sum = lax.dynamic_slice(sums[9:13].reshape(-1), (device * up_bias.shape[0],), up_bias.shape)
    return (
        result.astype(F32),
        patch_grad.astype(F32),
        own[0],
        own[1:3],
        own[3:5],
        grads[0],
        own[5:7],
        grads[1],
        own[7:9],
        grads[2],
        up_sum,
        grads[3],
    )


def layer_norm(hidden, gain, shift):
    center = hidden - jnp.mean(hidden, -1, keepdims=True)
    spread = jnp.mean(center * center, -1, keepdims=True)
    return center * lax.rsqrt(spread + EPS) * gain + shift


def gelu_exact(values):
    return jax.nn.gelu(values, approximate=False)


def outer_sum(left, right):
    return lax.dot_general(
        left, right, (((0,), (0,)), ((), ())), preferred_element_type=jnp.float32
    )


def back_product(grad, weight):
    return lax.dot_general(
        grad, weight, (((1,), (1,)), ((), ())), preferred_element_type=jnp.float32
    )


def by_patches(
    patches,
    segment_ids,
    mask_flags,
    cotangent,
    mask_embed,
    norm_gain,
    norm_shift,
    qkv_weight,
    qv_bias,
    out_weight,
    branch_bias,
    up_weight,
    up_bias,
    down_weight,
):
    rows, span, width = patches.shape
    head_dim = width // HEADS
    scale = 1.0 / math.sqrt(head_dim)
    count = rows * span
    block = min(rows, max(1, 512 // span))
    groups = rows // block
    (
        whole_embed,
        whole_gain,
        whole_shift,
        whole_qkv,
        whole_qvbias,
        whole_out,
        whole_bias,
        whole_up,
        whole_upbias,
        whole_down,
    ) = (
        lax.all_gather(mask_embed.astype(jnp.bfloat16), ("batch", "tm"), axis=0, tiled=True),
        lax.all_gather(norm_gain.astype(jnp.bfloat16), ("batch", "tm"), axis=1, tiled=True),
        lax.all_gather(norm_shift.astype(jnp.bfloat16), ("batch", "tm"), axis=1, tiled=True),
        lax.all_gather(qkv_weight.astype(jnp.bfloat16), ("batch", "tm"), axis=0, tiled=True),
        lax.all_gather(qv_bias.astype(jnp.bfloat16), ("batch", "tm"), axis=1, tiled=True),
        lax.all_gather(out_weight.astype(jnp.bfloat16), ("batch", "tm"), axis=0, tiled=True),
        lax.all_gather(branch_bias.astype(jnp.bfloat16), ("batch", "tm"), axis=1, tiled=True),
        lax.all_gather(up_weight.astype(jnp.bfloat16), ("batch", "tm"), axis=0, tiled=True),
        lax.all_gather(up_bias.astype(jnp.bfloat16), ("batch", "tm"), axis=0, tiled=True),
        lax.all_gather(down_weight.astype(jnp.bfloat16), ("batch", "tm"), axis=0, tiled=True),
    )
    gains = whole_gain.astype(jnp.float32)
    shifts = whole_shift.astype(jnp.float32)
    biases = whole_bias.astype(jnp.float32)
    qv_terms = whole_qvbias.astype(jnp.float32)
    masked = (mask_flags == 1)[..., None]
    start = jnp.where(masked, whole_embed.astype(jnp.float32), patches.astype(jnp.float32))
    first_in = layer_norm(start, gains[0], shifts[0]).astype(jnp.bfloat16).reshape(count, width)
    projected = jnp.dot(first_in, whole_qkv, preferred_element_type=jnp.float32)
    queries = (projected[:, :width] + qv_terms[0]).astype(jnp.bfloat16)
    keys_local = projected[:, width : 2 * width].astype(jnp.bfloat16)
    values_local = (projected[:, 2 * width :] + qv_terms[1]).astype(jnp.bfloat16)
    pairs = jnp.concatenate([keys_local, values_local], 1).reshape(rows, span, 2 * width)
    all_pairs, all_segments = (
        lax.all_gather(pairs, "tm", axis=1, tiled=True),
        lax.all_gather(segment_ids, "tm", axis=1, tiled=True),
    )
    total_keys = all_pairs.shape[1]
    query_blocks = queries.reshape(groups, block, span, width)
    pair_blocks = all_pairs.reshape(groups, block, total_keys, 2 * width)
    own_segments = segment_ids.reshape(groups, block, span)
    far_segments = all_segments.reshape(groups, block, total_keys)

    def masked_scores(query_blk, key_blk, query_seg, key_seg):
        lead = query_blk.shape[1]
        trail = key_blk.shape[1]
        query_heads = query_blk.reshape(block, lead, HEADS, head_dim)
        key_heads = key_blk.reshape(block, trail, HEADS, head_dim)
        scores = (
            jnp.einsum(
                "bqhd,bkhd->bhqk", query_heads, key_heads, preferred_element_type=jnp.float32
            )
            * scale
        )
        allowed = (query_seg[:, :, None] == key_seg[:, None, :])[:, None]
        return jnp.where(allowed, scores, FAR)

    def attend(items):
        query_blk, pair_blk, own_seg, far_seg = items
        scores = masked_scores(query_blk, pair_blk[..., :width], own_seg, far_seg)
        peak = jnp.max(scores, -1, keepdims=True)
        expon = jnp.exp(scores - peak)
        totals = jnp.sum(expon, -1, keepdims=True)
        probs_low = (expon / totals).astype(jnp.bfloat16)
        value_heads = pair_blk[..., width:].reshape(block, total_keys, HEADS, head_dim)
        mixed_blk = jnp.einsum(
            "bhqk,bkhd->bqhd", probs_low, value_heads, preferred_element_type=jnp.float32
        )
        return (mixed_blk.reshape(block, span, width), peak + jnp.log(totals))

    mixed, log_totals = lax.map(attend, (query_blocks, pair_blocks, own_segments, far_segments))
    mixed_low = mixed.reshape(count, width).astype(jnp.bfloat16)
    branch = jnp.dot(mixed_low, whole_out, preferred_element_type=jnp.float32) + biases[0]
    middle = start + branch.reshape(rows, span, width)
    second_in = layer_norm(middle, gains[1], shifts[1]).astype(jnp.bfloat16).reshape(count, width)
    hidden_pre = jnp.dot(
        second_in, whole_up, preferred_element_type=jnp.float32
    ) + whole_upbias.astype(jnp.float32)
    hidden_act = gelu_exact(hidden_pre).astype(jnp.bfloat16)
    result = jnp.dot(hidden_act, whole_down, preferred_element_type=jnp.float32) + biases[1]
    output = middle + result.reshape(rows, span, width)
    back_qkv, back_out, back_up, back_down = (
        lax.all_gather(qkv_weight.astype(jnp.bfloat16), ("batch", "tm"), axis=0, tiled=True),
        lax.all_gather(out_weight.astype(jnp.bfloat16), ("batch", "tm"), axis=0, tiled=True),
        lax.all_gather(up_weight.astype(jnp.bfloat16), ("batch", "tm"), axis=0, tiled=True),
        lax.all_gather(down_weight.astype(jnp.bfloat16), ("batch", "tm"), axis=0, tiled=True),
    )
    upstream = cotangent.astype(jnp.float32)
    result_grad = upstream.reshape(count, width).astype(jnp.bfloat16)
    down_bias_grad = jnp.sum(result_grad.astype(jnp.float32), 0)
    down_weight_grad = outer_sum(hidden_act, result_grad)
    act_grad = back_product(result_grad, back_down).astype(jnp.bfloat16)
    gelu_pull = jax.vjp(gelu_exact, hidden_pre)[1]
    pre_grad = gelu_pull(act_grad.astype(jnp.float32))[0].astype(jnp.bfloat16)
    up_bias_grad = jnp.sum(pre_grad.astype(jnp.float32), 0)
    up_weight_grad = outer_sum(second_in, pre_grad)
    second_grad = back_product(pre_grad, back_up).reshape(rows, span, width)
    norm_pull_two = jax.vjp(layer_norm, middle, gains[1], shifts[1])[1]
    middle_norm_grad, gain_two_grad, shift_two_grad = norm_pull_two(second_grad)
    middle_grad = upstream + middle_norm_grad
    branch_grad = middle_grad.reshape(count, width).astype(jnp.bfloat16)
    out_bias_grad = jnp.sum(branch_grad.astype(jnp.float32), 0)
    out_weight_grad = outer_sum(mixed_low, branch_grad)
    mixed_grad = back_product(branch_grad, back_out).astype(jnp.bfloat16)
    mixed_blocks = mixed_grad.reshape(groups, block, span, width)

    def query_back(items):
        query_blk, pair_blk, own_seg, far_seg, log_total, grad_blk = items
        scores = masked_scores(query_blk, pair_blk[..., :width], own_seg, far_seg)
        probs = jnp.exp(scores - log_total)
        probs_low = probs.astype(jnp.bfloat16)
        query_heads = query_blk.reshape(block, span, HEADS, head_dim)
        key_heads = pair_blk[..., :width].reshape(block, total_keys, HEADS, head_dim)
        value_heads = pair_blk[..., width:].reshape(block, total_keys, HEADS, head_dim)
        grad_heads = grad_blk.reshape(block, span, HEADS, head_dim)
        prob_grad = jnp.einsum(
            "bqhd,bkhd->bhqk", grad_heads, value_heads, preferred_element_type=jnp.float32
        )
        inner = jnp.sum(probs * prob_grad, -1, keepdims=True)
        score_grad = (probs * (prob_grad - inner)).astype(jnp.bfloat16)
        query_grad = (
            jnp.einsum("bhqk,bkhd->bqhd", score_grad, key_heads, preferred_element_type=jnp.float32)
            * scale
        )
        key_grad = (
            jnp.einsum(
                "bhqk,bqhd->bkhd", score_grad, query_heads, preferred_element_type=jnp.float32
            )
            * scale
        )
        value_grad = jnp.einsum(
            "bhqk,bqhd->bkhd", probs_low, grad_heads, preferred_element_type=jnp.float32
        )
        pair_grad = jnp.concatenate(
            [
                key_grad.reshape(block, total_keys, width),
                value_grad.reshape(block, total_keys, width),
            ],
            -1,
        )
        return (query_grad.reshape(block, span, width), pair_grad, inner)

    query_grads, pair_grads, unused_inner = lax.map(
        query_back,
        (query_blocks, pair_blocks, own_segments, far_segments, log_totals, mixed_blocks),
    )
    pair_grads = pair_grads.reshape(rows, total_keys, 2 * width)
    local_pair_grads = lax.psum_scatter(pair_grads, "tm", scatter_dimension=1, tiled=True).astype(
        jnp.bfloat16
    )
    query_low = query_grads.reshape(count, width).astype(jnp.bfloat16)
    local_pair_grads = local_pair_grads.reshape(count, 2 * width)
    qkv_grad = jnp.concatenate([query_low, local_pair_grads], 1)
    qkv_weight_grad = outer_sum(first_in, qkv_grad)
    qv_bias_grad = jnp.stack(
        [
            jnp.sum(query_low.astype(jnp.float32), 0),
            jnp.sum(local_pair_grads[:, width:].astype(jnp.float32), 0),
        ]
    )
    first_grad = back_product(qkv_grad, back_qkv).reshape(rows, span, width)
    norm_pull_one = jax.vjp(layer_norm, start, gains[0], shifts[0])[1]
    start_norm_grad, gain_one_grad, shift_one_grad = norm_pull_one(first_grad)
    start_grad = middle_grad + start_norm_grad
    embed_grad = jnp.sum(jnp.where(masked, start_grad, 0.0), (0, 1))
    patch_grad = jnp.where(masked, 0.0, start_grad)
    (
        embed_sum,
        gain_sum,
        shift_sum,
        qkv_sum,
        qv_sum,
        out_sum,
        branch_sum,
        up_sum,
        up_bias_sum,
        down_sum,
    ) = (
        lax.psum_scatter(embed_grad, ("batch", "tm"), scatter_dimension=0, tiled=True),
        lax.psum_scatter(
            jnp.stack([gain_one_grad, gain_two_grad]),
            ("batch", "tm"),
            scatter_dimension=1,
            tiled=True,
        ),
        lax.psum_scatter(
            jnp.stack([shift_one_grad, shift_two_grad]),
            ("batch", "tm"),
            scatter_dimension=1,
            tiled=True,
        ),
        lax.psum_scatter(qkv_weight_grad, ("batch", "tm"), scatter_dimension=0, tiled=True),
        lax.psum_scatter(qv_bias_grad, ("batch", "tm"), scatter_dimension=1, tiled=True),
        lax.psum_scatter(out_weight_grad, ("batch", "tm"), scatter_dimension=0, tiled=True),
        lax.psum_scatter(
            jnp.stack([out_bias_grad, down_bias_grad]),
            ("batch", "tm"),
            scatter_dimension=1,
            tiled=True,
        ),
        lax.psum_scatter(up_weight_grad, ("batch", "tm"), scatter_dimension=0, tiled=True),
        lax.psum_scatter(up_bias_grad, ("batch", "tm"), scatter_dimension=0, tiled=True),
        lax.psum_scatter(down_weight_grad, ("batch", "tm"), scatter_dimension=0, tiled=True),
    )
    return (
        output,
        patch_grad,
        embed_sum,
        gain_sum,
        shift_sum,
        qkv_sum,
        qv_sum,
        out_sum,
        branch_sum,
        up_sum,
        up_bias_sum,
        down_sum,
    )


def solution(mesh):
    wide, deep = mesh.shape["batch"] * mesh.shape["tm"], mesh.shape["batch"] // 2

    def on_device(patches, *rest):
        width = patches.shape[-1]
        fits = mesh.shape["tm"] == patches.shape[0] == 4 and width % (8 * wide) == 0 and patches.shape[1] == 256
        return by_rows(deep, patches, *rest) if fits else by_patches(patches, *rest)

    return jax.shard_map(
        on_device,
        mesh=mesh,
        in_specs=(
            P("batch", "tm", None),
            P("batch", "tm"),
            P("batch", "tm"),
            P("batch", "tm", None),
            P(("batch", "tm")),
            P(None, ("batch", "tm")),
            P(None, ("batch", "tm")),
            P(("batch", "tm"), None),
            P(None, ("batch", "tm")),
            P(("batch", "tm"), None),
            P(None, ("batch", "tm")),
            P(("batch", "tm"), None),
            P(("batch", "tm")),
            P(("batch", "tm"), None),
        ),
        out_specs=(
            P("batch", "tm", None),
            P("batch", "tm", None),
            P(("batch", "tm")),
            P(None, ("batch", "tm")),
            P(None, ("batch", "tm")),
            P(("batch", "tm"), None),
            P(None, ("batch", "tm")),
            P(("batch", "tm"), None),
            P(None, ("batch", "tm")),
            P(("batch", "tm"), None),
            P(("batch", "tm")),
            P(("batch", "tm"), None),
        ),
        check_vma=False,
    )
```

```python
import functools
import math

import jax
import jax.numpy as jnp
from jax import lax
from jax.experimental import pallas as pl
from jax.experimental.pallas import tpu as pltpu
from jax.sharding import PartitionSpec as P

HEADS = 12
EPS = 1e-06
FAR = -1e30
LOG2E = math.log2(math.e)
BF = jnp.bfloat16
F32 = jnp.float32
MESH = pl.DeviceIdType.MESH
HBM = pl.BlockSpec(memory_space=pl.ANY)
SLOPE = 0.36
COEFFICIENTS = (
    0.14371305209487725,
    0.14177235930704382,
    0.1397197719471602,
    0.026547986328787306,
    0.18095585464885458,
    -0.1797659534284226,
    0.04705662553510592,
)


VECTOR, QKV, OUT, UP, DOWN = range(5)
START, PROJECT, ATTEND, RISE, FALL, FEED, BEND, MIX, CLOSE, TAIL = range(10)
FIRST, STAGE, FINISH, ROWS, COTANGENT, SPREAD = range(6)
SETTLE, TURN, ADD, VECTOR_SEND, VECTOR_ADD, DELIVER = range(6)

FORWARD_STEPS = {
    START: {
        0: [
            (FIRST, VECTOR),
            (FIRST, QKV),
            (FIRST, UP),
            (STAGE, VECTOR, 0, 0, 3),
            (FIRST, OUT),
            (STAGE, VECTOR, 1, 0, 4),
            (STAGE, QKV, 0, 0, 3),
            (STAGE, VECTOR, 2, 0, 8),
            (FINISH, VECTOR),
            (ROWS,),
            (STAGE, QKV, 1, 0, 4),
            (STAGE, QKV, 2, 0, 4),
            (SPREAD,),
            (STAGE, QKV, 2, 4, 8),
            (FINISH, QKV),
            (STAGE, UP, 0, 0, 3),
        ],
    },
    PROJECT: {
        1: [
            (FIRST, DOWN),
        ],
        3: [
            (STAGE, OUT, 0, 0, 3),
        ],
    },
    ATTEND: {
        1: [
            (STAGE, UP, 1, 0, 4),
        ],
        2: [
            (STAGE, OUT, 1, 0, 4),
            (STAGE, DOWN, 0, 0, 1),
        ],
        3: [
            (STAGE, UP, 2, 0, 4),
            (STAGE, DOWN, 1, 0, 3),
        ],
        5: [
            (STAGE, OUT, 2, 0, 4),
            (STAGE, OUT, 2, 4, 8),
            (STAGE, UP, 2, 4, 8),
            (FINISH, OUT),
            (FINISH, UP),
            (STAGE, DOWN, 1, 3, 6),
        ],
    },
    RISE: {
        0: [
            (STAGE, DOWN, 2, 0, 4),
            (COTANGENT,),
        ],
        1: [
            (STAGE, DOWN, 2, 4, 8),
        ],
        2: [
            (FINISH, DOWN),
        ],
    },
}


BACKWARD_STEPS = {
    FEED: {
        0: [
            (SETTLE, DOWN, 0),
            (SETTLE, UP, 0),
        ],
        1: [
            (SETTLE, DOWN, 1),
        ],
        2: [
            (SETTLE, UP, 1),
            (SETTLE, DOWN, 2),
            (TURN, 0),
        ],
        3: [
            (TURN, 1),
            (SETTLE, DOWN, 3),
            (TURN, 2),
            (SETTLE, UP, 3),
        ],
    },
    MIX: {
        0: [
            (SETTLE, UP, 2),
            (TURN, 3),
        ],
    },
    ATTEND: {
        0: [
            (SETTLE, OUT, 0),
        ],
        1: [
            (ADD, UP, 2, 0),
            (ADD, UP, 2, 2),
            (ADD, UP, 2, 3),
        ],
        2: [
            (ADD, UP, 2, 1),
        ],
        3: [
            (ADD, OUT, 2, 0),
            (ADD, UP, 1, 2),
            (ADD, UP, 1, 1),
            (ADD, UP, 1, 3),
        ],
        4: [
            (SETTLE, QKV, 0),
            (ADD, OUT, 1, 0),
            (ADD, DOWN, 1, 0),
            (ADD, UP, 1, 0),
        ],
    },
    CLOSE: {
        1: [
            (ADD, OUT, 0, 0),
            (ADD, QKV, 2, 0),
            (ADD, UP, 0, 2),
            (ADD, UP, 0, 1),
        ],
        2: [
            (SETTLE, QKV, 1),
        ],
    },
    TAIL: {
        0: [
            (VECTOR_SEND, 0),
            (DELIVER, OUT),
            (ADD, DOWN, 0, 0),
            (ADD, QKV, 2, 1),
            (VECTOR_ADD, 0),
            (ADD, UP, 0, 3),
            (SETTLE, QKV, 2),
            (VECTOR_SEND, 1),
            (ADD, UP, 0, 0),
            (ADD, QKV, 2, 2),
            (ADD, QKV, 1, 0),
            (DELIVER, DOWN),
            (VECTOR_ADD, 1),
            (VECTOR_SEND, 2),
            (VECTOR_ADD, 2),
            (ADD, QKV, 1, 1),
            (VECTOR_SEND, 3),
            (ADD, QKV, 1, 2),
            (ADD, QKV, 0, 2),
            (ADD, QKV, 0, 0),
            (DELIVER, UP),
            (ADD, QKV, 0, 1),
            (DELIVER, QKV),
            (VECTOR_ADD, 3),
        ],
    },
}


def nn(left, right):
    return jnp.dot(left, right, preferred_element_type=F32)


def nt(left, right):
    return lax.dot_general(left, right, (((1,), (1,)), ((), ())), preferred_element_type=F32)


def tn(left, right):
    return lax.dot_general(left, right, (((0,), (0,)), ((), ())), preferred_element_type=F32)


def gelu_and_slope(pre):
    size = jnp.abs(pre)
    t = 1.0 / (1.0 + SLOPE * size)
    poly = jnp.full_like(t, COEFFICIENTS[-1])
    for term in COEFFICIENTS[-2::-1]:
        poly = poly * t + term
    bell = jnp.exp2(pre * pre * (-0.5 * LOG2E))
    lower = poly * t * bell
    cdf = jnp.where(pre >= 0, 1.0 - lower, lower)
    return pre * cdf, cdf + pre * bell * (1.0 / math.sqrt(2.0 * math.pi))


def moments(hidden):
    center = hidden - jnp.mean(hidden, -1, keepdims=True)
    return center, lax.rsqrt(jnp.mean(center * center, -1, keepdims=True) + EPS)


def norm_back(normed, rate, gain, grad):
    scaled = grad * gain
    shared = jnp.mean(scaled * normed, -1, keepdims=True)
    return rate * (scaled - jnp.mean(scaled, -1, keepdims=True) - normed * shared)


def column_sum(values):
    return jnp.sum(values, 0, keepdims=True)


class Place:
    def __init__(self, deep):
        batch, tm = lax.axis_index("batch"), lax.axis_index("tm")
        self.deep = deep
        self.batch, self.tm = batch, tm
        self.z, self.y = batch // 2, batch % 2
        self.x, self.c = tm // 2, tm % 2

    def device(self, z=None, y=None, x=None, c=None):
        z = self.z if z is None else z
        y = self.y if y is None else y
        x = self.x if x is None else x
        c = self.c if c is None else c
        return (z * 2 + y, x * 2 + c)

    def mate(self, k):
        return (self.x + k // 2) % 2 * 2 + (self.c + k % 2) % 2

    def enter(self):
        barrier = pltpu.get_barrier_semaphore()
        others = [self.device(c=1 - self.c), self.device(x=1 - self.x), self.device(y=1 - self.y)]
        others.append(self.device(x=1 - self.x, c=1 - self.c))
        others += [self.device(z=(self.z + d) % self.deep) for d in range(1, self.deep)]
        for other in others:
            pl.semaphore_signal(barrier, inc=1, device_id=other, device_id_type=MESH)
        pl.semaphore_wait(barrier, len(others))


def remote(src, dst, send, recv, device):
    return pltpu.make_async_remote_copy(
        src_ref=src, dst_ref=dst, send_sem=send, recv_sem=recv, device_id=device, device_id_type=MESH
    )


class Route:
    def __init__(self, place, order, crossed):
        self.place, self.order, self.crossed = place, order, crossed
        c = place.c
        self.own = {
            "z": place.z,
            "p": c * place.y + (1 - c) * place.x if crossed else place.x,
            "q": c * place.x + (1 - c) * place.y if crossed else place.y,
        }
        self.size = {"z": place.deep, "p": 2, "q": 2}
        self.sizes = [self.size[axis] for axis in order]

    def shifted(self, shifts):
        at = {a: (self.own[a] + s % self.size[a]) % self.size[a] for a, s in zip(self.order, shifts)}
        c = self.place.c
        if self.crossed:
            return at["z"], c * at["p"] + (1 - c) * at["q"], c * at["q"] + (1 - c) * at["p"]
        return at["z"], at["q"], at["p"]

    def device(self, shifts):
        z, y, x = self.shifted(shifts)
        return self.place.device(z=z, y=y, x=x)

    def chip(self, shifts):
        z, y, x = self.shifted(shifts)
        return (z * 2 + y) * 2 + x

    def offsets(self, upto):
        found = [()]
        for stage, size in enumerate(self.sizes):
            found = [f + (o,) for f in found for o in range(size if stage < upto else 1)]
        return found

    def index(self, offset):
        flat = 0
        for o, size in zip(offset, self.sizes):
            flat = flat * size + o
        return flat


class Gather:
    def __init__(self, place, route, shard, joined, full, local, sends, recvs):
        self.place, self.route = place, route
        self.shard, self.joined, self.full = shard, joined, full
        self.local, self.sends, self.recvs = local, sends, recvs
        self.rows = shard.shape[0]
        self.half = joined.shape[1]
        self.count = 0

    def columns(self, c):
        return pl.ds(pl.multiple_of(c * self.half, 128), self.half)

    def region(self, chip, c):
        rows = 2 * self.rows
        return self.full.at[pl.ds(pl.multiple_of(chip * rows, 16), rows), self.columns(c)]

    def ship(self, src, dst, recv, device):
        remote(src, dst, self.sends.at[self.count], recv, device).start()
        self.count += 1

    def join(self):
        place = self.place
        own = pl.ds(pl.multiple_of(place.c * self.rows, 8), self.rows)
        self.mine = pltpu.make_async_copy(
            self.shard.at[:, self.columns(place.c)], self.joined.at[own], self.local
        )
        self.mine.start()
        self.pair = self.recvs.at[0]
        self.ship(
            self.shard.at[:, self.columns(1 - place.c)],
            self.joined.at[own],
            self.recvs.at[0],
            place.device(c=1 - place.c),
        )

    def arrive(self, offset, stage):
        route, place = self.route, self.place
        chip = route.chip([-o for o in offset])
        block = self.region(chip, place.c)
        for later in range(stage + 1, 3):
            for d in range(1, route.sizes[later]):
                shifts = [0, 0, 0]
                shifts[later] = d
                seen = list(offset)
                seen[later] = d
                self.ship(block, block, self.recvs.at[1 + route.index(seen)], route.device(shifts))
        total = math.prod(route.sizes)
        self.ship(
            block,
            block,
            self.recvs.at[1 + total + route.index(offset)],
            place.device(c=1 - place.c),
        )

    def first(self):
        place = self.place
        self.mine.wait()
        own = pl.ds(pl.multiple_of((1 - place.c) * self.rows, 8), self.rows)
        remote(
            self.joined.at[own], self.joined.at[own], self.sends.at[0], self.recvs.at[0], place.device(c=1 - place.c)
        ).wait()
        chip = self.route.chip([0, 0, 0])
        self.region(chip, place.c)[...] = self.joined[...].astype(BF)
        self.arrive((0, 0, 0), -1)

    def stage(self, stage, some=slice(None)):
        route = self.route
        for offset in [o for o in route.offsets(stage + 1) if o[stage] > 0][some]:
            block = self.region(route.chip([-o for o in offset]), self.place.c)
            remote(
                block, block, self.sends.at[0], self.recvs.at[1 + route.index(offset)], self.place.device()
            ).wait_recv()
            self.arrive(offset, stage)

    def finish(self):
        route = self.route
        total = math.prod(route.sizes)
        for offset in route.offsets(3):
            block = self.region(route.chip([-o for o in offset]), 1 - self.place.c)
            remote(
                block,
                block,
                self.sends.at[0],
                self.recvs.at[1 + total + route.index(offset)],
                self.place.device(),
            ).wait_recv()

    def drain(self):
        block = self.region(self.route.chip([0, 0, 0]), self.place.c)
        for n in range(1, self.count):
            remote(block, block, self.sends.at[n], self.recvs.at[0], self.place.device()).wait_send()


class VectorSum:
    def __init__(self, place, held, slots, sends, recvs):
        self.held, self.slots = held, slots
        stages = [
            [place.device(c=1 - place.c)],
            [place.device(x=1 - place.x)],
            [place.device(y=1 - place.y)],
            [place.device(z=(place.z + d) % place.deep) for d in range(1, place.deep)],
        ]
        self.copies, slot = [], 0
        for stage, others in enumerate(stages):
            self.copies.append([])
            for other in others:
                copy = remote(held.at[stage], slots.at[slot], sends.at[slot], recvs.at[slot], other)
                self.copies[-1].append((copy, slot))
                slot += 1

    def send(self, stage):
        for copy, _ in self.copies[stage]:
            copy.start()

    def add(self, stage):
        total = self.held[stage]
        for copy, slot in self.copies[stage]:
            copy.wait()
            total = total + self.slots[slot]
        self.held[stage + 1] = total


def fill_vectors(block, mask_embed, norm_gain, norm_shift, qv_bias, branch_bias, up_bias):
    block[...] = jnp.zeros_like(block)
    piece = mask_embed.shape[1]
    row = 0
    for part in (mask_embed, norm_gain, norm_shift, qv_bias):
        block[row : row + part.shape[0], 0:piece] = part[...]
        row += part.shape[0]
    block[row : row + 1, 0:piece] = branch_bias[0:1, :]
    block[0:1, 128 : 128 + piece] = branch_bias[1:2, :]
    block[1:2, 128 : 128 + up_bias.shape[1]] = up_bias[...]


def spread_vectors(blocks, vectors):
    width = vectors.shape[1]
    devices = blocks.shape[0] // 8
    piece = width // devices
    table = blocks[...].astype(F32)
    vectors[...] = jnp.zeros_like(vectors)

    def put(rows, at, start):
        window = min(start // 128 * 128, width - 256)
        wide = jnp.concatenate([rows, jnp.zeros_like(rows)], 1)
        wide = pltpu.roll(wide, start - window, 1)
        vectors[at, window : window + 256] = vectors[at, window : window + 256] + wide

    for d in range(devices):
        block = table[8 * d : 8 * d + 8]
        put(block[:, :128], slice(0, 8), piece * d)
        put(block[0:1, 128:], slice(8, 9), piece * d)
        up = 4 * piece * d
        put(block[1:2, 128:], slice(9 + up // width, 10 + up // width), up % width)


def column_of(table, source, row):
    line = table[source, pl.ds(row, 1), :].astype(F32)
    tall = jnp.broadcast_to(line, (8, line.shape[1]))
    return jnp.concatenate([tall[:, n : n + 128].T[:, 0:1] for n in range(0, line.shape[1], 128)], 0)


def forward_kernel(
    deep,
    patches,
    cotangent,
    flags_in,
    clips_in,
    mask_embed,
    norm_gain,
    norm_shift,
    qv_bias,
    branch_bias,
    up_bias,
    shard_qkv,
    shard_out,
    shard_up,
    shard_down,
    o_qkv,
    o_out,
    o_up,
    o_down,
    o_small,
    o_x,
    o_cot,
    o_flags,
    o_first,
    o_q,
    o_k,
    o_v,
    o_mixed,
    o_second,
    o_rate,
    o_middle,
    o_act,
    o_slope,
    o_expon,
    o_result,
    w_qkv,
    w_out,
    w_up,
    w_down,
    j_qkv,
    j_out,
    j_up,
    j_down,
    j_vector,
    shard_vector,
    w_vector,
    small,
    x,
    flags_all,
    clips_all,
    first,
    q,
    k,
    v,
    mixed,
    second,
    rate,
    middle,
    expon,
    slope,
    result,
    q_code,
    k_code,
    join_sems,
    gather_sends,
    gather_recvs,
    row_sends,
    row_recvs,
    local_sems,
    expon_sems,
    act_sems,
):
    place = Place(deep)
    span, width = patches.shape[1:]
    rows = x.shape[0]
    sources = rows // span
    half = width // HEADS
    pairs = HEADS // 2
    inner = w_up.shape[1]
    chunks = inner // width

    fill_vectors(shard_vector, mask_embed, norm_gain, norm_shift, qv_bias, branch_bias, up_bias)
    place.enter()

    kinds = ((patches, x), (flags_in, flags_all), (clips_in, clips_all), (cotangent, o_cot))

    def landing(kind, source):
        dst = kinds[kind][1]
        if kind in (1, 2):
            return dst.at[source]
        return dst.at[pl.ds(pl.multiple_of(source * span, span), span)]

    def leaving(kind, to):
        src = kinds[kind][0]
        return src if kind in (1, 2) else src.at[to]

    def own_part(kind):
        return pltpu.make_async_copy(
            leaving(kind, place.tm), landing(kind, place.tm), local_sems.at[kind]
        )

    def row_copy(kind, step, to):
        return remote(
            leaving(kind, to),
            landing(kind, place.tm),
            row_sends.at[kind, step],
            row_recvs.at[kind, step],
            (place.batch, to),
        )

    def row_wait(kind, step):
        source = place.mate(step)
        there = landing(kind, source)
        remote(
            there, there, row_sends.at[kind, step], row_recvs.at[kind, step], (place.batch, source)
        ).wait_recv()

    zpq = Route(place, "zpq", True)
    zxy = Route(place, "zpq", False)
    pzq = Route(place, "pzq", True)
    xzy = Route(place, "pzq", False)
    named = {}
    for i, (name, route, shard, joined, full) in enumerate(
        (
            (VECTOR, zpq, shard_vector, j_vector, w_vector),
            (QKV, zxy, shard_qkv, j_qkv, w_qkv),
            (OUT, zpq, shard_out, j_out, w_out),
            (UP, zxy, shard_up, j_up, w_up),
            (DOWN, pzq, shard_down, j_down, w_down),
        )
    ):
        named[name] = Gather(
            place, route, shard, joined, full, join_sems.at[i], gather_sends.at[i], gather_recvs.at[i]
        )
    gathers = list(named.values())
    for gather in gathers:
        gather.join()
    def send_rows(kinds):
        for kind in kinds:
            for step in range(1, sources):
                row_copy(kind, step, place.mate(step)).start()

    def run(steps):
        for what, *which in steps:
            if what == ROWS:
                send_rows((1, 2, 0))
            elif what == COTANGENT:
                send_rows((3,))
            elif what == SPREAD:
                spread_vectors(w_vector, small)
            elif what == FIRST:
                named[which[0]].first()
            elif what == FINISH:
                named[which[0]].finish()
            else:
                named[which[0]].stage(which[1], slice(which[2], which[3]))

    def after(loop, index):
        for when, steps in FORWARD_STEPS.get(loop, {}).items():
            if isinstance(index, int):
                if index == when:
                    run(steps)
            else:
                pl.when(index == when)(functools.partial(run, steps))

    for kind in (1, 2, 0):
        own_part(kind).start()
    run(FORWARD_STEPS[START][0])
    keeping = []

    def keep(src, dst):
        copy = pltpu.make_async_copy(src, dst, local_sems.at[4 + len(keeping)])
        copy.start()
        keeping.append(copy)


    vectors = small
    lane = lax.broadcasted_iota(jnp.int32, (1, 2 * half), 1)
    low = lane < half
    own_lanes = [low.astype(F32), 1.0 - low.astype(F32)]

    for kind in (1, 2, 0):
        own_part(kind).wait()

    @pl.loop(0, sources)
    def _(step):
        @pl.when(step > 0)
        def _():
            for kind in (1, 2, 0):
                row_wait(kind, step)

        source = place.mate(step)
        at = pl.ds(pl.multiple_of(source * span, span), span)
        flags = column_of(flags_all, source, place.tm)
        clips = column_of(clips_all, source, place.tm)
        start = jnp.where(flags == 1.0, vectors[0:1, :], x[at, :].astype(F32))
        middle[at, :] = start
        center, speed = moments(start)
        normed = (center * speed * vectors[1:2, :] + vectors[3:4, :]).astype(BF)
        first[at, :] = normed
        q[at, :] = (nn(normed, w_qkv[:, 0:width]) + vectors[5:6, :]).astype(BF) * (1.0 / math.sqrt(half))
        k[at, :] = nn(normed, w_qkv[:, width : 2 * width]).astype(BF)
        v[at, :] = (nn(normed, w_qkv[:, 2 * width :]) + vectors[6:7, :]).astype(BF)
        clip_lane = lax.broadcasted_iota(jnp.int32, (span, 2 * half), 1).astype(F32)
        for h in range(2):
            base = float(half * (1 - h))
            same = clip_lane - base == clips
            coded = jnp.logical_and(clip_lane >= base, clip_lane < base + 5.0)
            q_code[h, at, :] = jnp.where(same, 1.0, 0.0).astype(BF)
            k_code[h, at, :] = jnp.where(jnp.logical_and(coded, jnp.logical_not(same)), FAR, 0.0).astype(BF)
        after(PROJECT, step)

    for src, dst in ((w_qkv, o_qkv), (small, o_small), (x, o_x), (flags_all, o_flags), (first, o_first), (q, o_q), (k, o_k), (v, o_v)):
        keep(src, dst)

    block = min(rows, 512)

    def expon_copy(p):
        return pltpu.make_async_copy(expon.at[p % 2], o_expon.at[pl.ds(2 * p, 2)], expon_sems.at[p % 2])

    def attend(p):
        lanes = pl.ds(pl.multiple_of(p * 2 * half, 128), 2 * half)

        @pl.when(p >= 2)
        def _():
            expon_copy(p - 2).wait()

        slot = p % 2
        keys, values = [], []
        for h in range(2):
            mask = own_lanes[h].astype(BF)
            keys.append(k[:, lanes] * mask + k_code[h])
            values.append(v[:, lanes] * mask + own_lanes[1 - h].astype(BF))
        for part in range(rows // block):
            at = pl.ds(part * block, block)
            mixes = []
            for h in range(2):
                query = q[at, lanes] * own_lanes[h].astype(BF) + q_code[h, at, :]
                scores = nt(query, keys[h])
                peak = jnp.max(scores, -1, keepdims=True)
                weights = jnp.exp2((scores - peak) * LOG2E).astype(BF)
                expon[slot, h, at, :] = weights
                mixes.append(nn(weights, values[h]))
            top = jnp.where(low, mixes[0], mixes[1])
            totals = pltpu.roll(jnp.where(low, mixes[1], mixes[0]), half, 1)
            speed = 1.0 / totals
            rate[at, lanes] = speed
            mixed[at, lanes] = (top * speed).astype(BF)
        expon_copy(p).start()
        after(ATTEND, p)

    pl.loop(0, pairs)(attend)
    for src, dst in ((w_out, o_out), (w_up, o_up), (mixed, o_mixed), (rate, o_rate)):
        keep(src, dst)
    for p in (pairs - 2, pairs - 1):
        expon_copy(p).wait()

    def act(j, at):
        return expon.at[j // 2, j % 2, at, pl.ds(0, width)]

    def slope_copies(step):
        at = pl.ds(pl.multiple_of(step * span, span), span)
        return [
            pltpu.make_async_copy(slope.at[step % 2, j], o_slope.at[j, at], act_sems.at[step % 2, j])
            for j in range(chunks)
        ]

    def act_copies(step):
        at = pl.ds(pl.multiple_of(step * span, span), span)
        return [pltpu.make_async_copy(act(j, at), o_act.at[j, at], act_sems.at[2, j]) for j in range(chunks)]

    def rise(step):
        @pl.when(step >= 2)
        def _():
            for copy in slope_copies(step - 2):
                copy.wait()

        at = pl.ds(pl.multiple_of(step * span, span), span)
        hidden = middle[at, :] + nn(mixed[at, :], w_out[...]) + vectors[7:8, :]
        middle[at, :] = hidden
        center, speed = moments(hidden)
        normed = (center * speed * vectors[2:3, :] + vectors[4:5, :]).astype(BF)
        second[at, :] = normed
        for j in range(chunks):
            pre = nn(normed, w_up[:, j * width : (j + 1) * width]) + vectors[9 + j : 10 + j, :]
            value, steep = gelu_and_slope(pre)
            expon[j // 2, j % 2, at, 0:width] = value.astype(BF)
            slope[step % 2, j] = steep.astype(BF)
        for copy in slope_copies(step) + act_copies(step):
            copy.start()
        after(RISE, step)

    def fall(step):
        at = pl.ds(pl.multiple_of(step * span, span), span)
        total = middle[at, :] + vectors[8:9, :]
        for j in range(chunks):
            total = total + nn(expon[j // 2, j % 2, at, 0:width], w_down[j * width : (j + 1) * width, :])
        result[at, :] = total.astype(BF)

    pl.loop(0, sources)(rise)
    keep(second, o_second)
    keep(middle, o_middle)
    keep(w_down, o_down)
    pl.loop(0, sources)(fall)
    keep(result, o_result)
    for step in range(sources):
        for copy in act_copies(step):
            copy.wait()
    for step in (sources - 2, sources - 1):
        for copy in slope_copies(step):
            copy.wait()
    for step in range(1, sources):
        row_wait(3, step)
        for kind in range(4):
            row_copy(kind, step, place.mate(step)).wait_send()
    for copy in keeping:
        copy.wait()
    for gather in gathers:
        gather.drain()


def forward(deep, patches, cotangent, flags, clips, vectors, shards):
    sources, span, width = patches.shape
    qkv, out, up, down = shards
    rows = sources * span
    chips = deep * 4
    inner = up.shape[1]
    chunks = inner // width
    shape = jax.ShapeDtypeStruct
    fulls = [(2 * chips * s.shape[0], s.shape[1]) for s in shards]
    plane = (rows, width)
    outs = [shape(f, BF) for f in fulls]
    outs += [shape((16, width), F32), shape(plane, BF), shape(plane, BF)]
    outs += [shape((sources,) + flags.shape, jnp.int32)]
    outs += [shape(plane, BF)] * 6 + [shape(plane, F32)] * 2
    outs += [shape((chunks, rows, width), BF)] * 2
    outs += [shape((HEADS, rows, rows), BF), shape(plane, BF)]
    scratch = [pltpu.VMEM(f, BF) for f in fulls]
    scratch += [pltpu.VMEM((2 * s.shape[0], s.shape[1] // 2), F32) for s in shards]
    scratch += [
        pltpu.VMEM((16, 128), F32),
        pltpu.VMEM((8, 256), F32),
        pltpu.VMEM((16 * chips, 256), BF),
        pltpu.VMEM((16, width), F32),
        pltpu.VMEM(plane, BF),
        pltpu.VMEM((sources,) + flags.shape, jnp.int32),
        pltpu.VMEM((sources,) + flags.shape, jnp.int32),
    ]
    scratch += [pltpu.VMEM(plane, BF)] * 6 + [pltpu.VMEM(plane, F32)] * 2
    scratch += [
        pltpu.VMEM((2, 2, rows, rows), BF),
        pltpu.VMEM((2, chunks, span, width), BF),
        pltpu.VMEM(plane, BF),
        pltpu.VMEM((2, rows, 128), BF),
        pltpu.VMEM((2, rows, 128), BF),
    ]
    dma = pltpu.SemaphoreType.DMA
    scratch += [
        dma((5,)),
        dma((5, 1 + 2 * chips)),
        dma((5, 1 + 2 * chips)),
        dma((4, sources)),
        dma((4, sources)),
        dma((20,)),
        dma((2,)),
        dma((3, chunks)),
    ]
    return pl.pallas_call(
        functools.partial(forward_kernel, deep),
        out_shape=outs,
        in_specs=[HBM] * 4 + [pl.BlockSpec(memory_space=pltpu.VMEM)] * 6 + [HBM] * 4,
        out_specs=[HBM] * len(outs),
        scratch_shapes=scratch,
        compiler_params=pltpu.CompilerParams(
            collective_id=0, has_side_effects=True, vmem_limit_bytes=62 * 2**20
        ),
        name="forward",
    )(patches, cotangent, flags, clips, *vectors, *shards)


class Scatter:
    def __init__(self, place, route, held, slots, final, sends, recvs, piece=None):
        self.place, self.route = place, route
        self.held, self.slots, self.final = held, slots, final
        self.sends, self.recvs = sends, recvs
        self.rows = slots.shape[1]
        self.width = piece
        self.sent = []

    def region(self, shifts):
        return pl.ds(pl.multiple_of(self.route.chip(shifts) * self.rows, 16), self.rows)

    def columns(self, piece):
        if piece is None:
            return pl.ds(0, self.held.shape[1])
        return pl.ds(pl.multiple_of(piece * self.width, 128), self.width)

    def parts(self, stage):
        route = self.route
        for d in range(1, route.sizes[stage]):
            for earlier in route.offsets(stage):
                offset = list(earlier)
                offset[stage] = d
                yield d, [-o for o in earlier], route.index(offset) - 1

    def copy(self, stage, d, back, slot, piece):
        shifts, to = list(back), [0, 0, 0]
        shifts[stage] = to[stage] = d
        columns = self.columns(piece)
        n = 0 if piece is None else piece
        return remote(
            self.held.at[self.region(shifts), columns],
            self.slots.at[slot, :, columns],
            self.sends.at[n, slot],
            self.recvs.at[n, slot],
            self.route.device(to),
        )

    def send(self, stage, piece=None):
        self.sent.append((stage, piece))
        for d, back, slot in self.parts(stage):
            self.copy(stage, d, back, slot, piece).start()

    def add(self, stage, piece=None):
        found = {}
        columns = self.columns(piece)
        for d, back, slot in self.parts(stage):
            self.copy(stage, d, back, slot, piece).wait_recv()
            found.setdefault(tuple(back), []).append(slot)
        for back, slots in found.items():
            at = self.region(back)
            total = self.held[at, columns].astype(F32)
            for slot in slots:
                total = total + self.slots[slot, :, columns].astype(F32)
            if stage == 0:
                self.final[:, columns] = total
            else:
                self.held[at, columns] = total.astype(BF)

    def drain(self):
        for stage, piece in self.sent:
            for d, back, slot in self.parts(stage):
                self.copy(stage, d, back, slot, piece).wait_send()


class RowScatter(Scatter):
    def part_q(self, z, p):
        place = self.place
        behind = (place.z - z + place.deep) % place.deep
        return [p, (place.deep - behind) % place.deep, 0], (p * place.deep + behind) * 2

    def copy_q(self, z, p):
        shifts, slot = self.part_q(z, p)
        return self.copy(2, 1, shifts, slot, None)

    def send_q(self, z):
        for p in range(2):
            self.copy_q(z, p).start()

    def add_q(self, z):
        for p in range(2):
            shifts, slot = self.part_q(z, p)
            self.copy_q(z, p).wait_recv()
            at = self.region(shifts)
            self.held[at, :] = (self.held[at, :].astype(F32) + self.slots[slot].astype(F32)).astype(BF)

    def copy_z(self, z, p):
        place = self.place
        ahead = (z - place.z + place.deep) % place.deep
        return self.copy(1, ahead, [p, 0, 0], (p * place.deep + ahead) * 2 - 1, None)

    def send_z(self, z):
        @pl.when(self.place.z != z)
        def _():
            for p in range(2):
                self.copy_z(z, p).start()

    def drain(self):
        place = self.place
        for z in range(place.deep):
            for p in range(2):
                self.copy_q(z, p).wait_send()
        for d, back, slot in self.parts(1):
            self.copy(1, d, back, slot, None).wait_send()
        super().drain()


def backward_kernel(
    deep,
    i_qkv,
    i_out,
    i_up,
    i_down,
    i_small,
    i_x,
    i_cot,
    i_flags,
    i_first,
    i_q,
    i_k,
    i_v,
    i_mixed,
    i_second,
    i_rate,
    i_middle,
    i_act,
    i_slope,
    i_expon,
    i_result,
    i_own_cot,
    o_qkv,
    o_out,
    o_up,
    o_down,
    o_small,
    o_patch,
    o_result,
    w_qkv,
    w_out,
    w_up,
    w_down,
    upstream,
    second,
    gathered,
    middle,
    expon,
    score_grad,
    trio,
    rate,
    mixed,
    staged,
    h_qkv,
    h_out,
    h_up,
    h_down,
    s_qkv,
    s_out,
    s_up,
    s_down,
    f_qkv,
    f_out,
    f_up,
    f_down,
    vectors,
    flags_all,
    small,
    small_slots,
    patch,
    load_sems,
    chunk_sems,
    pair_sems,
    hand_sends,
    hand_recvs,
    scatter_sends,
    scatter_recvs,
    final_sends,
    final_recvs,
    small_sends,
    small_recvs,
    row_sends,
    row_recvs,
    local_sems,
):
    place = Place(deep)
    rows, width = upstream.shape
    sources, span = patch.shape[:2]
    half = width // HEADS
    pairs = HEADS // 2
    chunks = i_act.shape[0]
    part = width // 2
    first = second
    mixed_grad = upstream
    first_grad = gathered

    loads = [
        pltpu.make_async_copy(src, dst, load_sems.at[i])
        for i, (src, dst) in enumerate(
            (
                (i_second, second),
                (i_middle, middle),
                (i_small, vectors),
                (i_flags, flags_all),
                (i_out, w_out),
                (i_qkv, w_qkv),
            )
        )
    ]

    def chunk_loads(j):
        slot = j % 2
        columns = pl.ds(pl.multiple_of(j * width, 128), width)
        moves = (
            (i_down.at[columns], w_down.at[slot]),
            (i_up.at[:, columns], w_up.at[slot]),
            (i_act.at[j], expon.at[slot, 0, :, pl.ds(0, width)]),
            (i_slope.at[j], expon.at[slot, 1, :, pl.ds(0, width)]),
        )
        return [pltpu.make_async_copy(src, dst, chunk_sems.at[slot, n]) for n, (src, dst) in enumerate(moves)]

    def pair_loads(p):
        slot = p % 2
        lanes = pl.ds(pl.multiple_of(p * 2 * half, 128), 2 * half)
        moves = (
            (i_expon.at[pl.ds(2 * p, 2)], expon.at[slot]),
            (i_q.at[:, lanes], trio.at[slot, 0]),
            (i_k.at[:, lanes], trio.at[slot, 1]),
            (i_v.at[:, lanes], trio.at[slot, 2]),
            (i_rate.at[:, lanes], rate.at[slot]),
            (i_mixed.at[:, lanes], mixed.at[slot]),
        )
        return [pltpu.make_async_copy(src, dst, pair_sems.at[slot, n]) for n, (src, dst) in enumerate(moves)]

    for step in range(sources):
        source = place.mate(step)
        at = pl.ds(pl.multiple_of(source * span, span), span)
        loads.insert(
            step,
            pltpu.make_async_copy(
                i_own_cot.at[place.tm] if step == 0 else i_cot.at[at], upstream.at[at], load_sems.at[6 + step]
            ),
        )
    early = sources + 1
    for copy in loads[:early] + chunk_loads(0) + loads[early:]:
        copy.start()
    place.enter()

    def result_copy(step):
        to = place.mate(step)
        return remote(
            i_result.at[pl.ds(pl.multiple_of(to * span, span), span)],
            o_result.at[place.tm],
            row_sends.at[1, step],
            row_recvs.at[1, step],
            (place.batch, to),
        )

    result_in = pltpu.make_async_copy(
        i_result.at[pl.ds(pl.multiple_of(place.tm * span, span), span)], patch.at[sources - 1], local_sems.at[5]
    )
    result_in.start()
    result_out = pltpu.make_async_copy(patch.at[sources - 1], o_result.at[place.tm], local_sems.at[5])
    for step in range(1, sources):
        result_copy(step).start()

    zpq = Route(place, "zpq", True)
    pzq = Route(place, "pzq", True)
    xzy = Route(place, "pzq", False)
    zxy = Route(place, "zpq", False)
    by_qkv = Scatter(place, xzy, h_qkv, s_qkv, f_qkv, scatter_sends.at[0], scatter_recvs.at[0], part)
    by_out = Scatter(place, zxy, h_out, s_out, f_out, scatter_sends.at[1], scatter_recvs.at[1], part)
    by_up = Scatter(place, zpq, h_up, s_up, f_up, scatter_sends.at[2], scatter_recvs.at[2], part)
    by_down = RowScatter(place, pzq, h_down, s_down, f_down, scatter_sends.at[3], scatter_recvs.at[3])
    scatters = [by_qkv, by_out, by_up, by_down]

    def columns(c):
        return pl.ds(pl.multiple_of(c * part, 128), part)

    def hand(slot, held, n):
        return remote(
            staged.at[slot, :, columns(1 - place.c)],
            held,
            hand_sends.at[n],
            hand_recvs.at[n],
            place.device(c=1 - place.c),
        )

    def settle(slot, held, n):
        copy = hand(slot, held, n)
        copy.wait_recv()
        held[...] = (held[...].astype(F32) + staged[slot, :, columns(place.c)].astype(F32)).astype(BF)
        copy.wait_send()

    def down_chunk(j):
        return (2 * (j % 2), h_down.at[pl.ds(pl.multiple_of(j * width, 128), width)], j)

    def up_chunk(j):
        return (2 * (j % 2) + 1, h_up.at[:, pl.ds(pl.multiple_of(j * part, 128), part)], chunks + j)

    def qkv_chunk(i):
        return (1 + i, h_qkv.at[:, pl.ds(pl.multiple_of(i * part, 128), part)], 2 * chunks + 1 + i)

    def out_chunk(i):
        return (0, h_out, 2 * chunks)

    named = {
        QKV: (by_qkv, qkv_chunk),
        OUT: (by_out, out_chunk),
        UP: (by_up, up_chunk),
        DOWN: (by_down, down_chunk),
    }
    summed = VectorSum(place, small, small_slots, small_sends, small_recvs)

    def run(steps):
        for what, *which in steps:
            if what == VECTOR_SEND:
                summed.send(which[0])
            elif what == VECTOR_ADD:
                summed.add(which[0])
            elif what == TURN:
                by_down.add_q(which[0])
                by_down.send_z(which[0])
            elif what == DELIVER:
                deliver(*deliveries[which[0]])
            elif what == SETTLE:
                scatter, chunk = named[which[0]]
                settle(*chunk(which[1]))
                if scatter is by_down:
                    scatter.send_q(which[1])
                else:
                    scatter.send(2, which[1])
            else:
                scatter = named[which[0]][0]
                stage = which[1]
                piece = None if scatter is by_down else which[2]
                scatter.add(stage, piece)
                if stage > 0:
                    scatter.send(stage - 1, piece)

    def after(loop, index):
        for when, steps in BACKWARD_STEPS.get(loop, {}).items():
            if isinstance(index, int):
                if index == when:
                    run(steps)
            else:
                pl.when(index == when)(functools.partial(run, steps))

    for copy in loads[:early]:
        copy.wait()

    def feed(j):
        @pl.when(j < chunks - 1)
        def _():
            for copy in chunk_loads(j + 1):
                copy.start()

        for copy in chunk_loads(j):
            copy.wait()
        slot = j % 2
        act_grad = nt(upstream[...], w_down[slot]).astype(BF).astype(F32)
        pre_grad = (act_grad * expon[slot, 1, :, 0:width].astype(F32)).astype(BF)
        small[0, pl.ds(9 + j, 1), :] = column_sum(pre_grad.astype(F32))
        staged[down_chunk(j)[0]] = tn(expon[slot, 0, :, 0:width], upstream[...]).astype(BF)
        hand(*down_chunk(j)).start()
        staged[up_chunk(j)[0]] = tn(second[...], pre_grad).astype(BF)
        hand(*up_chunk(j)).start()
        grown = nt(pre_grad, w_up[slot])

        gathered[...] = gathered[...] + grown

        after(FEED, j)

    gathered[...] = jnp.zeros_like(gathered)
    pl.loop(0, chunks)(feed)
    whole_mixed = pltpu.make_async_copy(i_mixed, expon.at[1, 1, :, pl.ds(0, width)], local_sems.at[0])
    whole_mixed.start()
    for copy in pair_loads(0):
        copy.start()
    load_first = pltpu.make_async_copy(i_first, first, local_sems.at[1])
    load_first.start()
    for copy in loads[early:]:
        copy.wait()
    for row in (0, 1, 2, 3, 4, 5, 6, 7, 8, 13, 14, 15):
        small[0, row : row + 1, :] = jnp.zeros((1, width), F32)

    def bend(n):
        at = pl.ds(pl.multiple_of(n * span, span), span)
        center, speed = moments(middle[at, :])
        normed = center * speed
        grad = gathered[at, :]
        small[0, 2:3, :] = small[0, 2:3, :] + column_sum(grad * normed)
        small[0, 4:5, :] = small[0, 4:5, :] + column_sum(grad)
        above = upstream[at, :].astype(F32)
        small[0, 8:9, :] = small[0, 8:9, :] + column_sum(above)
        total = above + norm_back(normed, speed, vectors[2:3, :], grad)
        middle[at, :] = total
        low_total = total.astype(BF)
        small[0, 7:8, :] = small[0, 7:8, :] + column_sum(low_total.astype(F32))
        mixed_grad[at, :] = nt(low_total, w_out[...]).astype(BF)

    pl.loop(0, sources)(bend)
    after(BEND, 0)
    whole_mixed.wait()
    staged[0] = tn(expon[1, 1, :, 0:width], middle[...].astype(BF)).astype(BF)
    hand(*out_chunk(0)).start()
    after(MIX, 0)
    load_first.wait()
    result_in.wait()
    result_out.start()

    lane = lax.broadcasted_iota(jnp.int32, (1, 2 * half), 1)
    low = lane < half
    own_lanes = [low.astype(F32), 1.0 - low.astype(F32)]
    block = min(rows, 512)

    def attend(p):
        slot = p % 2
        lanes = pl.ds(pl.multiple_of(p * 2 * half, 128), 2 * half)

        @pl.when(p < pairs - 1)
        def _():
            for copy in pair_loads(p + 1):
                copy.start()

        for copy in pair_loads(p):
            copy.wait()
        scaled = (mixed_grad[:, lanes].astype(F32) * rate[slot]).astype(BF)
        product = scaled.astype(F32) * mixed[slot].astype(F32)
        query, key, value = trio[slot, 0], trio[slot, 1], trio[slot, 2]
        key_grads, value_grads, query_grads = [], [], []
        for h in range(2):
            inner = jnp.sum(product * own_lanes[h], -1, keepdims=True)
            lone = scaled * own_lanes[h].astype(BF)
            query_parts = []
            for n in range(rows // block):
                at = slice(n * block, (n + 1) * block)
                grad = nt(lone[at], value)
                weights = expon[slot, h, at, :].astype(F32)
                grad = (weights * (grad - inner[at])).astype(BF)
                score_grad[h, at, :] = grad
                query_parts.append(nn(grad, key))
            query_grads.append(jnp.concatenate(query_parts, 0))
            key_grads.append(tn(query, score_grad[h]))
            value_grads.append(tn(scaled, expon[slot, h]))
        query_grad = (jnp.where(low, query_grads[0], query_grads[1]) * (1.0 / math.sqrt(half))).astype(BF)
        key_grad = jnp.concatenate([key_grads[0][:half], key_grads[1][half:]], 0).T.astype(BF)
        value_grad = jnp.concatenate([value_grads[0][:half], value_grads[1][half:]], 0).T.astype(BF)
        small[0, 5:6, lanes] = column_sum(query_grad.astype(F32))
        small[0, 6:7, lanes] = column_sum(value_grad.astype(F32))
        grads = jnp.concatenate([query_grad, key_grad, value_grad], 1)
        where = pl.ds(pl.multiple_of(slot * part, 128), part)
        staged[1 + p // 2, :, where] = tn(first[...], grads).astype(BF)
        weight = jnp.concatenate(
            [w_qkv[:, pl.ds(pl.multiple_of(p * 2 * half + n * width, 128), 2 * half)] for n in range(3)], 1
        )
        grown = nt(grads, weight)

        first_grad[...] = first_grad[...] + grown

        @pl.when(p % 2 == 1)
        def _():
            hand(*qkv_chunk(p // 2)).start()

        after(ATTEND, p)

    first_grad[...] = jnp.zeros_like(first_grad)
    pl.loop(0, pairs)(attend)
    load_x = pltpu.make_async_copy(i_x, expon.at[0, 0, :, pl.ds(0, width)], local_sems.at[2])
    load_x.start()
    load_x.wait()
    result_out.wait()

    def close(step):
        source = place.mate(sources - 1 - step)
        at = pl.ds(pl.multiple_of(source * span, span), span)
        flags = column_of(flags_all, source, place.tm) == 1.0
        start = jnp.where(flags, vectors[0:1, :], expon[0, 0, at, 0:width].astype(F32))
        center, speed = moments(start)
        normed = center * speed
        grad = first_grad[at, :]
        small[0, 1:2, :] = small[0, 1:2, :] + column_sum(grad * normed)
        small[0, 3:4, :] = small[0, 3:4, :] + column_sum(grad)
        total = middle[at, :] + norm_back(normed, speed, vectors[1:2, :], grad)
        small[0, 0:1, :] = small[0, 0:1, :] + column_sum(jnp.where(flags, total, 0.0))
        patch[step] = jnp.where(flags, 0.0, total).astype(BF)

        @pl.when(step < sources - 1)
        def _():
            remote(
                patch.at[step],
                o_patch.at[place.tm],
                row_sends.at[0, sources - 1 - step],
                row_recvs.at[0, sources - 1 - step],
                (place.batch, source),
            ).start()

        after(CLOSE, step)

    pl.loop(0, sources)(close)
    own_patch = pltpu.make_async_copy(patch.at[sources - 1], o_patch.at[place.tm], local_sems.at[3])
    own_patch.start()
    moves = []

    def deliver(final, target, pieces):
        shard = target.shape[0]
        for near, far, jump, size in pieces:
            to = pl.ds(pl.multiple_of(far + place.c * jump, 128), size)
            mine = pl.ds(pl.multiple_of(place.c * shard, 8), shard)
            theirs = pl.ds(pl.multiple_of((1 - place.c) * shard, 8), shard)
            n = len(moves) // 2
            moves.append(
                pltpu.make_async_copy(final.at[mine, pl.ds(near, size)], target.at[:, to], local_sems.at[6 + n])
            )
            moves.append(
                remote(
                    final.at[theirs, pl.ds(near, size)],
                    target.at[:, to],
                    final_sends.at[n],
                    final_recvs.at[n],
                    place.device(c=1 - place.c),
                )
            )
            moves[-2].start()
            moves[-1].start()

    deliveries = {
        DOWN: (f_down, o_down, [(0, 0, part, part)]),
        UP: (f_up, o_up, [(j * part, j * width, part, part) for j in range(chunks)]),
        OUT: (f_out, o_out, [(0, 0, part, part)]),
        QKV: (
            f_qkv,
            o_qkv,
            [
                (i * part + n * 2 * half, n * width + i * 4 * half, 2 * half, 2 * half)
                for i in range(3)
                for n in range(3)
            ],
        ),
    }
    after(TAIL, 0)
    own_small = pltpu.make_async_copy(small.at[4], o_small, local_sems.at[4])
    own_small.start()
    for move in moves:
        move.wait()
    for step in range(1, sources):
        copy = remote(
            patch.at[0], o_patch.at[place.mate(step)], row_sends.at[0, step], row_recvs.at[0, step], place.device()
        )
        copy.wait_recv()
        copy.wait_send()
        result_copy(step).wait()
    own_patch.wait()
    own_small.wait()
    for scatter in scatters:
        scatter.drain()


def backward(deep, saved, shards, cotangent):
    sources, span, width = cotangent.shape
    rows = sources * span
    chips = deep * 4
    chunks = shards[2].shape[1] // width
    shape = jax.ShapeDtypeStruct
    plane = (rows, width)
    small = saved[4]
    flags = saved[7]
    halves = [(2 * chips * s.shape[0], s.shape[1] // 2) for s in shards]
    outs = [shape(s.shape, F32) for s in shards] + [shape(small.shape, F32)] + [shape(cotangent.shape, BF)] * 2
    scratch = [
        pltpu.VMEM(saved[0].shape, BF),
        pltpu.VMEM(saved[1].shape, BF),
        pltpu.VMEM((2, width, width), BF),
        pltpu.VMEM((2, width, width), BF),
        pltpu.VMEM(plane, BF),
        pltpu.VMEM(plane, BF),
        pltpu.VMEM(plane, F32),
        pltpu.VMEM(plane, F32),
        pltpu.VMEM((2, 2, rows, rows), BF),
        pltpu.VMEM((2, rows, rows), BF),
        pltpu.VMEM((2, 3, rows, 2 * width // HEADS), BF),
        pltpu.VMEM((2, rows, 2 * width // HEADS), F32),
        pltpu.VMEM((2, rows, 2 * width // HEADS), BF),
        pltpu.VMEM((4, width, width), BF),
    ]
    scratch += [pltpu.VMEM(h, BF) for h in halves]
    scratch += [pltpu.VMEM((chips - 1, 2 * s.shape[0], s.shape[1] // 2), BF) for s in shards]
    scratch += [pltpu.VMEM((2 * s.shape[0], s.shape[1] // 2), F32) for s in shards]
    scratch += [
        pltpu.VMEM(small.shape, F32),
        pltpu.VMEM(flags.shape, jnp.int32),
        pltpu.VMEM((5,) + small.shape, F32),
        pltpu.VMEM((2 + deep,) + small.shape, F32),
        pltpu.VMEM(cotangent.shape, BF),
    ]
    dma = pltpu.SemaphoreType.DMA
    scratch += [
        dma((6 + sources,)),
        dma((2, 4)),
        dma((2, 6)),
        dma((2 * chunks + 4,)),
        dma((2 * chunks + 4,)),
        dma((4, chunks, chips - 1)),
        dma((4, chunks, chips - 1)),
        dma((11 + chunks,)),
        dma((11 + chunks,)),
        dma((2 + deep,)),
        dma((2 + deep,)),
        dma((2, sources)),
        dma((2, sources)),
        dma((17 + chunks,)),
    ]
    return pl.pallas_call(
        functools.partial(backward_kernel, deep),
        out_shape=outs,
        in_specs=[HBM] * (len(saved) + 1),
        out_specs=[HBM] * len(outs),
        scratch_shapes=scratch,
        compiler_params=pltpu.CompilerParams(
            collective_id=1, has_side_effects=True, vmem_limit_bytes=63 * 2**20
        ),
        name="backward",
    )(*saved, cotangent)


def finish_kernel(result, patch, sums, *refs):
    grads, outs = refs[:4], refs[4:]
    o_result, o_patch, embed, gain, shift, g_qkv, qv, g_out, branch, g_up, up, g_down = outs
    o_result[...] = result[...].astype(F32)
    o_patch[...] = patch[...].astype(F32)

    @pl.when(pl.program_id(0) == 0)
    def _():
        device = lax.axis_index("batch") * 4 + lax.axis_index("tm")
        width = sums.shape[1]
        piece, up_piece = embed.shape[1], up.shape[1]
        own = pltpu.roll(sums[...], lax.rem(width - device * piece, width), 1)
        row = 0
        for out in (embed, gain, shift, qv, branch):
            out[...] = own[row : row + out.shape[0], :piece]
            row += out.shape[0]
        lines = width // up_piece
        line = jnp.broadcast_to(sums[pl.ds(row + device // lines, 1), :], (8, width))
        at = lax.rem(width - lax.rem(device, lines) * up_piece, width)
        up[...] = pltpu.roll(line, at, 1)[0:1, :up_piece]
        for grad, out in zip(grads, (g_qkv, g_out, g_up, g_down)):
            out[...] = grad[...]


def finish(result, patch_grad, sums, grads, parts):
    sources, span, width = result.shape
    shape = jax.ShapeDtypeStruct
    rows = pl.BlockSpec((2, span, width), lambda i: (i, 0, 0))

    def whole(array):
        return pl.BlockSpec(array.shape, lambda i: (0, 0))

    vectors = [shape(p.shape, F32) for p in parts]
    embed, gain, shift, qv, branch, up = vectors
    outs = [embed, gain, shift, grads[0], qv, grads[1], branch, grads[2], up, grads[3]]
    outs = [shape(o.shape, F32) for o in outs]
    return pl.pallas_call(
        finish_kernel,
        grid=(sources // 2,),
        out_shape=[shape(result.shape, F32)] * 2 + outs,
        in_specs=[rows, rows, whole(sums)] + [whole(g) for g in grads],
        out_specs=[rows, rows] + [whole(o) for o in outs],
        name="finish",
    )(result, patch_grad, sums, *grads)


def by_rows(
    deep,
    patches,
    segment_ids,
    mask_flags,
    cotangent,
    mask_embed,
    norm_gain,
    norm_shift,
    qkv_weight,
    qv_bias,
    out_weight,
    branch_bias,
    up_weight,
    up_bias,
    down_weight,
):
    sources, span, width = patches.shape
    shards = (qkv_weight, out_weight, up_weight, down_weight)
    vectors = (mask_embed[None], norm_gain, norm_shift, qv_bias, branch_bias, up_bias[None])
    saved = forward(deep, patches, cotangent, mask_flags, segment_ids, vectors, shards)
    *grads, sums, patch_grad, result = backward(deep, saved, shards, cotangent)
    result, patch_grad, embed, gain, shift, g_qkv, qv, g_out, branch, g_up, up, g_down = finish(
        result, patch_grad, sums, grads, vectors
    )
    return result, patch_grad, embed[0], gain, shift, g_qkv, qv, g_out, branch, g_up, up[0], g_down


def layer_norm(hidden, gain, shift):
    center = hidden - jnp.mean(hidden, -1, keepdims=True)
    spread = jnp.mean(center * center, -1, keepdims=True)
    return center * lax.rsqrt(spread + EPS) * gain + shift


def gelu_exact(values):
    return jax.nn.gelu(values, approximate=False)


def outer_sum(left, right):
    return lax.dot_general(
        left, right, (((0,), (0,)), ((), ())), preferred_element_type=jnp.float32
    )


def back_product(grad, weight):
    return lax.dot_general(
        grad, weight, (((1,), (1,)), ((), ())), preferred_element_type=jnp.float32
    )


def by_patches(
    patches,
    segment_ids,
    mask_flags,
    cotangent,
    mask_embed,
    norm_gain,
    norm_shift,
    qkv_weight,
    qv_bias,
    out_weight,
    branch_bias,
    up_weight,
    up_bias,
    down_weight,
):
    rows, span, width = patches.shape
    head_dim = width // HEADS
    scale = 1.0 / math.sqrt(head_dim)
    count = rows * span
    block = min(rows, max(1, 512 // span))
    groups = rows // block
    (
        whole_embed,
        whole_gain,
        whole_shift,
        whole_qkv,
        whole_qvbias,
        whole_out,
        whole_bias,
        whole_up,
        whole_upbias,
        whole_down,
    ) = (
        lax.all_gather(mask_embed.astype(jnp.bfloat16), ("batch", "tm"), axis=0, tiled=True),
        lax.all_gather(norm_gain.astype(jnp.bfloat16), ("batch", "tm"), axis=1, tiled=True),
        lax.all_gather(norm_shift.astype(jnp.bfloat16), ("batch", "tm"), axis=1, tiled=True),
        lax.all_gather(qkv_weight.astype(jnp.bfloat16), ("batch", "tm"), axis=0, tiled=True),
        lax.all_gather(qv_bias.astype(jnp.bfloat16), ("batch", "tm"), axis=1, tiled=True),
        lax.all_gather(out_weight.astype(jnp.bfloat16), ("batch", "tm"), axis=0, tiled=True),
        lax.all_gather(branch_bias.astype(jnp.bfloat16), ("batch", "tm"), axis=1, tiled=True),
        lax.all_gather(up_weight.astype(jnp.bfloat16), ("batch", "tm"), axis=0, tiled=True),
        lax.all_gather(up_bias.astype(jnp.bfloat16), ("batch", "tm"), axis=0, tiled=True),
        lax.all_gather(down_weight.astype(jnp.bfloat16), ("batch", "tm"), axis=0, tiled=True),
    )
    gains = whole_gain.astype(jnp.float32)
    shifts = whole_shift.astype(jnp.float32)
    biases = whole_bias.astype(jnp.float32)
    qv_terms = whole_qvbias.astype(jnp.float32)
    masked = (mask_flags == 1)[..., None]
    start = jnp.where(masked, whole_embed.astype(jnp.float32), patches.astype(jnp.float32))
    first_in = layer_norm(start, gains[0], shifts[0]).astype(jnp.bfloat16).reshape(count, width)
    projected = jnp.dot(first_in, whole_qkv, preferred_element_type=jnp.float32)
    queries = (projected[:, :width] + qv_terms[0]).astype(jnp.bfloat16)
    keys_local = projected[:, width : 2 * width].astype(jnp.bfloat16)
    values_local = (projected[:, 2 * width :] + qv_terms[1]).astype(jnp.bfloat16)
    pairs = jnp.concatenate([keys_local, values_local], 1).reshape(rows, span, 2 * width)
    all_pairs, all_segments = (
        lax.all_gather(pairs, "tm", axis=1, tiled=True),
        lax.all_gather(segment_ids, "tm", axis=1, tiled=True),
    )
    total_keys = all_pairs.shape[1]
    query_blocks = queries.reshape(groups, block, span, width)
    pair_blocks = all_pairs.reshape(groups, block, total_keys, 2 * width)
    own_segments = segment_ids.reshape(groups, block, span)
    far_segments = all_segments.reshape(groups, block, total_keys)

    def masked_scores(query_blk, key_blk, query_seg, key_seg):
        lead = query_blk.shape[1]
        trail = key_blk.shape[1]
        query_heads = query_blk.reshape(block, lead, HEADS, head_dim)
        key_heads = key_blk.reshape(block, trail, HEADS, head_dim)
        scores = (
            jnp.einsum(
                "bqhd,bkhd->bhqk", query_heads, key_heads, preferred_element_type=jnp.float32
            )
            * scale
        )
        allowed = (query_seg[:, :, None] == key_seg[:, None, :])[:, None]
        return jnp.where(allowed, scores, FAR)

    def attend(items):
        query_blk, pair_blk, own_seg, far_seg = items
        scores = masked_scores(query_blk, pair_blk[..., :width], own_seg, far_seg)
        peak = jnp.max(scores, -1, keepdims=True)
        expon = jnp.exp(scores - peak)
        totals = jnp.sum(expon, -1, keepdims=True)
        probs_low = (expon / totals).astype(jnp.bfloat16)
        value_heads = pair_blk[..., width:].reshape(block, total_keys, HEADS, head_dim)
        mixed_blk = jnp.einsum(
            "bhqk,bkhd->bqhd", probs_low, value_heads, preferred_element_type=jnp.float32
        )
        return (mixed_blk.reshape(block, span, width), peak + jnp.log(totals))

    mixed, log_totals = lax.map(attend, (query_blocks, pair_blocks, own_segments, far_segments))
    mixed_low = mixed.reshape(count, width).astype(jnp.bfloat16)
    branch = jnp.dot(mixed_low, whole_out, preferred_element_type=jnp.float32) + biases[0]
    middle = start + branch.reshape(rows, span, width)
    second_in = layer_norm(middle, gains[1], shifts[1]).astype(jnp.bfloat16).reshape(count, width)
    hidden_pre = jnp.dot(
        second_in, whole_up, preferred_element_type=jnp.float32
    ) + whole_upbias.astype(jnp.float32)
    hidden_act = gelu_exact(hidden_pre).astype(jnp.bfloat16)
    result = jnp.dot(hidden_act, whole_down, preferred_element_type=jnp.float32) + biases[1]
    output = middle + result.reshape(rows, span, width)
    back_qkv, back_out, back_up, back_down = (
        lax.all_gather(qkv_weight.astype(jnp.bfloat16), ("batch", "tm"), axis=0, tiled=True),
        lax.all_gather(out_weight.astype(jnp.bfloat16), ("batch", "tm"), axis=0, tiled=True),
        lax.all_gather(up_weight.astype(jnp.bfloat16), ("batch", "tm"), axis=0, tiled=True),
        lax.all_gather(down_weight.astype(jnp.bfloat16), ("batch", "tm"), axis=0, tiled=True),
    )
    upstream = cotangent.astype(jnp.float32)
    result_grad = upstream.reshape(count, width).astype(jnp.bfloat16)
    down_bias_grad = jnp.sum(result_grad.astype(jnp.float32), 0)
    down_weight_grad = outer_sum(hidden_act, result_grad)
    act_grad = back_product(result_grad, back_down).astype(jnp.bfloat16)
    gelu_pull = jax.vjp(gelu_exact, hidden_pre)[1]
    pre_grad = gelu_pull(act_grad.astype(jnp.float32))[0].astype(jnp.bfloat16)
    up_bias_grad = jnp.sum(pre_grad.astype(jnp.float32), 0)
    up_weight_grad = outer_sum(second_in, pre_grad)
    second_grad = back_product(pre_grad, back_up).reshape(rows, span, width)
    norm_pull_two = jax.vjp(layer_norm, middle, gains[1], shifts[1])[1]
    middle_norm_grad, gain_two_grad, shift_two_grad = norm_pull_two(second_grad)
    middle_grad = upstream + middle_norm_grad
    branch_grad = middle_grad.reshape(count, width).astype(jnp.bfloat16)
    out_bias_grad = jnp.sum(branch_grad.astype(jnp.float32), 0)
    out_weight_grad = outer_sum(mixed_low, branch_grad)
    mixed_grad = back_product(branch_grad, back_out).astype(jnp.bfloat16)
    mixed_blocks = mixed_grad.reshape(groups, block, span, width)

    def query_back(items):
        query_blk, pair_blk, own_seg, far_seg, log_total, grad_blk = items
        scores = masked_scores(query_blk, pair_blk[..., :width], own_seg, far_seg)
        probs = jnp.exp(scores - log_total)
        probs_low = probs.astype(jnp.bfloat16)
        query_heads = query_blk.reshape(block, span, HEADS, head_dim)
        key_heads = pair_blk[..., :width].reshape(block, total_keys, HEADS, head_dim)
        value_heads = pair_blk[..., width:].reshape(block, total_keys, HEADS, head_dim)
        grad_heads = grad_blk.reshape(block, span, HEADS, head_dim)
        prob_grad = jnp.einsum(
            "bqhd,bkhd->bhqk", grad_heads, value_heads, preferred_element_type=jnp.float32
        )
        inner = jnp.sum(probs * prob_grad, -1, keepdims=True)
        score_grad = (probs * (prob_grad - inner)).astype(jnp.bfloat16)
        query_grad = (
            jnp.einsum("bhqk,bkhd->bqhd", score_grad, key_heads, preferred_element_type=jnp.float32)
            * scale
        )
        key_grad = (
            jnp.einsum(
                "bhqk,bqhd->bkhd", score_grad, query_heads, preferred_element_type=jnp.float32
            )
            * scale
        )
        value_grad = jnp.einsum(
            "bhqk,bqhd->bkhd", probs_low, grad_heads, preferred_element_type=jnp.float32
        )
        pair_grad = jnp.concatenate(
            [
                key_grad.reshape(block, total_keys, width),
                value_grad.reshape(block, total_keys, width),
            ],
            -1,
        )
        return (query_grad.reshape(block, span, width), pair_grad, inner)

    query_grads, pair_grads, unused_inner = lax.map(
        query_back,
        (query_blocks, pair_blocks, own_segments, far_segments, log_totals, mixed_blocks),
    )
    pair_grads = pair_grads.reshape(rows, total_keys, 2 * width)
    local_pair_grads = lax.psum_scatter(pair_grads, "tm", scatter_dimension=1, tiled=True).astype(
        jnp.bfloat16
    )
    query_low = query_grads.reshape(count, width).astype(jnp.bfloat16)
    local_pair_grads = local_pair_grads.reshape(count, 2 * width)
    qkv_grad = jnp.concatenate([query_low, local_pair_grads], 1)
    qkv_weight_grad = outer_sum(first_in, qkv_grad)
    qv_bias_grad = jnp.stack(
        [
            jnp.sum(query_low.astype(jnp.float32), 0),
            jnp.sum(local_pair_grads[:, width:].astype(jnp.float32), 0),
        ]
    )
    first_grad = back_product(qkv_grad, back_qkv).reshape(rows, span, width)
    norm_pull_one = jax.vjp(layer_norm, start, gains[0], shifts[0])[1]
    start_norm_grad, gain_one_grad, shift_one_grad = norm_pull_one(first_grad)
    start_grad = middle_grad + start_norm_grad
    embed_grad = jnp.sum(jnp.where(masked, start_grad, 0.0), (0, 1))
    patch_grad = jnp.where(masked, 0.0, start_grad)
    (
        embed_sum,
        gain_sum,
        shift_sum,
        qkv_sum,
        qv_sum,
        out_sum,
        branch_sum,
        up_sum,
        up_bias_sum,
        down_sum,
    ) = (
        lax.psum_scatter(embed_grad, ("batch", "tm"), scatter_dimension=0, tiled=True),
        lax.psum_scatter(
            jnp.stack([gain_one_grad, gain_two_grad]),
            ("batch", "tm"),
            scatter_dimension=1,
            tiled=True,
        ),
        lax.psum_scatter(
            jnp.stack([shift_one_grad, shift_two_grad]),
            ("batch", "tm"),
            scatter_dimension=1,
            tiled=True,
        ),
        lax.psum_scatter(qkv_weight_grad, ("batch", "tm"), scatter_dimension=0, tiled=True),
        lax.psum_scatter(qv_bias_grad, ("batch", "tm"), scatter_dimension=1, tiled=True),
        lax.psum_scatter(out_weight_grad, ("batch", "tm"), scatter_dimension=0, tiled=True),
        lax.psum_scatter(
            jnp.stack([out_bias_grad, down_bias_grad]),
            ("batch", "tm"),
            scatter_dimension=1,
            tiled=True,
        ),
        lax.psum_scatter(up_weight_grad, ("batch", "tm"), scatter_dimension=0, tiled=True),
        lax.psum_scatter(up_bias_grad, ("batch", "tm"), scatter_dimension=0, tiled=True),
        lax.psum_scatter(down_weight_grad, ("batch", "tm"), scatter_dimension=0, tiled=True),
    )
    return (
        output,
        patch_grad,
        embed_sum,
        gain_sum,
        shift_sum,
        qkv_sum,
        qv_sum,
        out_sum,
        branch_sum,
        up_sum,
        up_bias_sum,
        down_sum,
    )


def solution(mesh):
    wide, deep = mesh.shape["batch"] * mesh.shape["tm"], mesh.shape["batch"] // 2

    def on_device(patches, *rest):
        width = patches.shape[-1]
        fits = mesh.shape["tm"] == patches.shape[0] == 4 and width % (8 * wide) == 0 and patches.shape[1] == 256
        return by_rows(deep, patches, *rest) if fits else by_patches(patches, *rest)

    return jax.shard_map(
        on_device,
        mesh=mesh,
        in_specs=(
            P("batch", "tm", None),
            P("batch", "tm"),
            P("batch", "tm"),
            P("batch", "tm", None),
            P(("batch", "tm")),
            P(None, ("batch", "tm")),
            P(None, ("batch", "tm")),
            P(("batch", "tm"), None),
            P(None, ("batch", "tm")),
            P(("batch", "tm"), None),
            P(None, ("batch", "tm")),
            P(("batch", "tm"), None),
            P(("batch", "tm")),
            P(("batch", "tm"), None),
        ),
        out_specs=(
            P("batch", "tm", None),
            P("batch", "tm", None),
            P(("batch", "tm")),
            P(None, ("batch", "tm")),
            P(None, ("batch", "tm")),
            P(("batch", "tm"), None),
            P(None, ("batch", "tm")),
            P(("batch", "tm"), None),
            P(None, ("batch", "tm")),
            P(("batch", "tm"), None),
            P(("batch", "tm")),
            P(("batch", "tm"), None),
        ),
        check_vma=False,
    )
```

```python
import functools
import math

import jax
import jax.numpy as jnp
from jax import lax
from jax.experimental import pallas as pl
from jax.experimental.pallas import tpu as pltpu
from jax.sharding import PartitionSpec as P

HEADS = 12
EPS = 1e-06
FAR = -1e30
LOG2E = math.log2(math.e)
BF = jnp.bfloat16
F32 = jnp.float32
MESH = pl.DeviceIdType.MESH
HBM = pl.BlockSpec(memory_space=pl.ANY)
SLOPE = 0.36
COEFFICIENTS = (
    0.14371305209487725,
    0.14177235930704382,
    0.1397197719471602,
    0.026547986328787306,
    0.18095585464885458,
    -0.1797659534284226,
    0.04705662553510592,
)


VECTOR, QKV, OUT, UP, DOWN = range(5)
START, PROJECT, ATTEND, RISE, FALL, FEED, BEND, MIX, CLOSE, TAIL = range(10)
FIRST, STAGE, FINISH, ROWS, COTANGENT, SPREAD = range(6)
SETTLE, TURN, ADD, VECTOR_SEND, VECTOR_ADD, DELIVER = range(6)

FORWARD_STEPS = {
    START: {
        0: [
            (FIRST, VECTOR),
            (FIRST, QKV),
            (FIRST, UP),
            (STAGE, VECTOR, 0, 0, 3),
            (FIRST, OUT),
            (STAGE, VECTOR, 1, 0, 4),
            (STAGE, QKV, 0, 0, 3),
            (STAGE, VECTOR, 2, 0, 8),
            (FINISH, VECTOR),
            (ROWS,),
            (STAGE, QKV, 1, 0, 4),
            (STAGE, QKV, 2, 0, 4),
            (SPREAD,),
            (STAGE, QKV, 2, 4, 8),
            (FINISH, QKV),
            (STAGE, UP, 0, 0, 3),
        ],
    },
    PROJECT: {
        1: [
            (FIRST, DOWN),
        ],
        3: [
            (STAGE, OUT, 0, 0, 3),
        ],
    },
    ATTEND: {
        1: [
            (STAGE, UP, 1, 0, 4),
        ],
        2: [
            (STAGE, OUT, 1, 0, 4),
            (STAGE, DOWN, 0, 0, 1),
        ],
        3: [
            (STAGE, UP, 2, 0, 4),
            (STAGE, DOWN, 1, 0, 3),
        ],
        5: [
            (STAGE, OUT, 2, 0, 4),
            (STAGE, OUT, 2, 4, 8),
            (STAGE, UP, 2, 4, 8),
            (FINISH, OUT),
            (FINISH, UP),
            (STAGE, DOWN, 1, 3, 6),
        ],
    },
    RISE: {
        0: [
            (STAGE, DOWN, 2, 0, 4),
            (COTANGENT,),
        ],
        1: [
            (STAGE, DOWN, 2, 4, 8),
        ],
        2: [
            (FINISH, DOWN),
        ],
    },
}


BACKWARD_STEPS = {
    FEED: {
        0: [
            (SETTLE, DOWN, 0),
            (SETTLE, UP, 0),
        ],
        1: [
            (SETTLE, DOWN, 1),
        ],
        2: [
            (SETTLE, UP, 1),
            (SETTLE, DOWN, 2),
            (TURN, 0),
        ],
        3: [
            (TURN, 1),
            (SETTLE, DOWN, 3),
            (TURN, 2),
            (SETTLE, UP, 3),
        ],
    },
    MIX: {
        0: [
            (SETTLE, UP, 2),
            (TURN, 3),
        ],
    },
    ATTEND: {
        0: [
            (SETTLE, OUT, 0),
        ],
        1: [
            (ADD, UP, 2, 0),
            (ADD, UP, 2, 2),
            (ADD, UP, 2, 3),
        ],
        2: [
            (ADD, UP, 2, 1),
        ],
        3: [
            (ADD, OUT, 2, 0),
            (ADD, UP, 1, 2),
            (ADD, UP, 1, 1),
            (ADD, UP, 1, 3),
        ],
        4: [
            (SETTLE, QKV, 0),
            (ADD, OUT, 1, 0),
            (ADD, DOWN, 1, 0),
            (ADD, UP, 1, 0),
        ],
    },
    CLOSE: {
        1: [
            (ADD, OUT, 0, 0),
            (ADD, QKV, 2, 0),
            (ADD, UP, 0, 2),
            (ADD, UP, 0, 1),
        ],
        2: [
            (SETTLE, QKV, 1),
        ],
    },
    TAIL: {
        0: [
            (VECTOR_SEND, 0),
            (DELIVER, OUT),
            (ADD, DOWN, 0, 0),
            (ADD, QKV, 2, 1),
            (VECTOR_ADD, 0),
            (ADD, UP, 0, 3),
            (SETTLE, QKV, 2),
            (VECTOR_SEND, 1),
            (ADD, UP, 0, 0),
            (ADD, QKV, 2, 2),
            (ADD, QKV, 1, 0),
            (DELIVER, DOWN),
            (VECTOR_ADD, 1),
            (VECTOR_SEND, 2),
            (VECTOR_ADD, 2),
            (ADD, QKV, 1, 1),
            (VECTOR_SEND, 3),
            (ADD, QKV, 1, 2),
            (ADD, QKV, 0, 2),
            (ADD, QKV, 0, 0),
            (DELIVER, UP),
            (ADD, QKV, 0, 1),
            (DELIVER, QKV),
            (VECTOR_ADD, 3),
        ],
    },
}


def nn(left, right):
    return jnp.dot(left, right, preferred_element_type=F32)


def nt(left, right):
    return lax.dot_general(left, right, (((1,), (1,)), ((), ())), preferred_element_type=F32)


def tn(left, right):
    return lax.dot_general(left, right, (((0,), (0,)), ((), ())), preferred_element_type=F32)


def gelu_and_slope(pre):
    size = jnp.abs(pre)
    t = 1.0 / (1.0 + SLOPE * size)
    poly = jnp.full_like(t, COEFFICIENTS[-1])
    for term in COEFFICIENTS[-2::-1]:
        poly = poly * t + term
    bell = jnp.exp2(pre * pre * (-0.5 * LOG2E))
    lower = poly * t * bell
    cdf = jnp.where(pre >= 0, 1.0 - lower, lower)
    return pre * cdf, cdf + pre * bell * (1.0 / math.sqrt(2.0 * math.pi))


def moments(hidden):
    center = hidden - jnp.mean(hidden, -1, keepdims=True)
    return center, lax.rsqrt(jnp.mean(center * center, -1, keepdims=True) + EPS)


def norm_back(normed, rate, gain, grad):
    scaled = grad * gain
    shared = jnp.mean(scaled * normed, -1, keepdims=True)
    return rate * (scaled - jnp.mean(scaled, -1, keepdims=True) - normed * shared)


def column_sum(values):
    return jnp.sum(values, 0, keepdims=True)


class Place:
    def __init__(self, deep):
        batch, tm = lax.axis_index("batch"), lax.axis_index("tm")
        self.deep = deep
        self.batch, self.tm = batch, tm
        self.z, self.y = batch // 2, batch % 2
        self.x, self.c = tm // 2, tm % 2

    def device(self, z=None, y=None, x=None, c=None):
        z = self.z if z is None else z
        y = self.y if y is None else y
        x = self.x if x is None else x
        c = self.c if c is None else c
        return (z * 2 + y, x * 2 + c)

    def mate(self, k):
        return (self.x + k // 2) % 2 * 2 + (self.c + k % 2) % 2

    def enter(self):
        barrier = pltpu.get_barrier_semaphore()
        others = [self.device(c=1 - self.c), self.device(x=1 - self.x), self.device(y=1 - self.y)]
        others.append(self.device(x=1 - self.x, c=1 - self.c))
        others += [self.device(z=(self.z + d) % self.deep) for d in range(1, self.deep)]
        for other in others:
            pl.semaphore_signal(barrier, inc=1, device_id=other, device_id_type=MESH)
        pl.semaphore_wait(barrier, len(others))


def remote(src, dst, send, recv, device):
    return pltpu.make_async_remote_copy(
        src_ref=src, dst_ref=dst, send_sem=send, recv_sem=recv, device_id=device, device_id_type=MESH
    )


class Route:
    def __init__(self, place, order, crossed):
        self.place, self.order, self.crossed = place, order, crossed
        c = place.c
        self.own = {
            "z": place.z,
            "p": c * place.y + (1 - c) * place.x if crossed else place.x,
            "q": c * place.x + (1 - c) * place.y if crossed else place.y,
        }
        self.size = {"z": place.deep, "p": 2, "q": 2}
        self.sizes = [self.size[axis] for axis in order]

    def shifted(self, shifts):
        at = {a: (self.own[a] + s % self.size[a]) % self.size[a] for a, s in zip(self.order, shifts)}
        c = self.place.c
        if self.crossed:
            return at["z"], c * at["p"] + (1 - c) * at["q"], c * at["q"] + (1 - c) * at["p"]
        return at["z"], at["q"], at["p"]

    def device(self, shifts):
        z, y, x = self.shifted(shifts)
        return self.place.device(z=z, y=y, x=x)

    def chip(self, shifts):
        z, y, x = self.shifted(shifts)
        return (z * 2 + y) * 2 + x

    def offsets(self, upto):
        found = [()]
        for stage, size in enumerate(self.sizes):
            found = [f + (o,) for f in found for o in range(size if stage < upto else 1)]
        return found

    def index(self, offset):
        flat = 0
        for o, size in zip(offset, self.sizes):
            flat = flat * size + o
        return flat


class Gather:
    def __init__(self, place, route, shard, joined, full, local, sends, recvs):
        self.place, self.route = place, route
        self.shard, self.joined, self.full = shard, joined, full
        self.local, self.sends, self.recvs = local, sends, recvs
        self.rows = shard.shape[0]
        self.half = joined.shape[1]
        self.count = 0

    def columns(self, c):
        return pl.ds(pl.multiple_of(c * self.half, 128), self.half)

    def region(self, chip, c):
        rows = 2 * self.rows
        return self.full.at[pl.ds(pl.multiple_of(chip * rows, 16), rows), self.columns(c)]

    def ship(self, src, dst, recv, device):
        remote(src, dst, self.sends.at[self.count], recv, device).start()
        self.count += 1

    def join(self):
        place = self.place
        own = pl.ds(pl.multiple_of(place.c * self.rows, 8), self.rows)
        self.mine = pltpu.make_async_copy(
            self.shard.at[:, self.columns(place.c)], self.joined.at[own], self.local
        )
        self.mine.start()
        self.pair = self.recvs.at[0]
        self.ship(
            self.shard.at[:, self.columns(1 - place.c)],
            self.joined.at[own],
            self.recvs.at[0],
            place.device(c=1 - place.c),
        )

    def arrive(self, offset, stage):
        route, place = self.route, self.place
        chip = route.chip([-o for o in offset])
        block = self.region(chip, place.c)
        for later in range(stage + 1, 3):
            for d in range(1, route.sizes[later]):
                shifts = [0, 0, 0]
                shifts[later] = d
                seen = list(offset)
                seen[later] = d
                self.ship(block, block, self.recvs.at[1 + route.index(seen)], route.device(shifts))
        total = math.prod(route.sizes)
        self.ship(
            block,
            block,
            self.recvs.at[1 + total + route.index(offset)],
            place.device(c=1 - place.c),
        )

    def first(self):
        place = self.place
        self.mine.wait()
        own = pl.ds(pl.multiple_of((1 - place.c) * self.rows, 8), self.rows)
        remote(
            self.joined.at[own], self.joined.at[own], self.sends.at[0], self.recvs.at[0], place.device(c=1 - place.c)
        ).wait()
        chip = self.route.chip([0, 0, 0])
        self.region(chip, place.c)[...] = self.joined[...].astype(BF)
        self.arrive((0, 0, 0), -1)

    def stage(self, stage, some=slice(None)):
        route = self.route
        for offset in [o for o in route.offsets(stage + 1) if o[stage] > 0][some]:
            block = self.region(route.chip([-o for o in offset]), self.place.c)
            remote(
                block, block, self.sends.at[0], self.recvs.at[1 + route.index(offset)], self.place.device()
            ).wait_recv()
            self.arrive(offset, stage)

    def finish(self):
        route = self.route
        total = math.prod(route.sizes)
        for offset in route.offsets(3):
            block = self.region(route.chip([-o for o in offset]), 1 - self.place.c)
            remote(
                block,
                block,
                self.sends.at[0],
                self.recvs.at[1 + total + route.index(offset)],
                self.place.device(),
            ).wait_recv()

    def drain(self):
        block = self.region(self.route.chip([0, 0, 0]), self.place.c)
        for n in range(1, self.count):
            remote(block, block, self.sends.at[n], self.recvs.at[0], self.place.device()).wait_send()


class VectorSum:
    def __init__(self, place, held, slots, sends, recvs):
        self.held, self.slots = held, slots
        stages = [
            [place.device(c=1 - place.c)],
            [place.device(x=1 - place.x)],
            [place.device(y=1 - place.y)],
            [place.device(z=(place.z + d) % place.deep) for d in range(1, place.deep)],
        ]
        self.copies, slot = [], 0
        for stage, others in enumerate(stages):
            self.copies.append([])
            for other in others:
                copy = remote(held.at[stage], slots.at[slot], sends.at[slot], recvs.at[slot], other)
                self.copies[-1].append((copy, slot))
                slot += 1

    def send(self, stage):
        for copy, _ in self.copies[stage]:
            copy.start()

    def add(self, stage):
        total = self.held[stage]
        for copy, slot in self.copies[stage]:
            copy.wait()
            total = total + self.slots[slot]
        self.held[stage + 1] = total


def fill_vectors(block, mask_embed, norm_gain, norm_shift, qv_bias, branch_bias, up_bias):
    block[...] = jnp.zeros_like(block)
    piece = mask_embed.shape[1]
    row = 0
    for part in (mask_embed, norm_gain, norm_shift, qv_bias):
        block[row : row + part.shape[0], 0:piece] = part[...]
        row += part.shape[0]
    block[row : row + 1, 0:piece] = branch_bias[0:1, :]
    block[0:1, 128 : 128 + piece] = branch_bias[1:2, :]
    block[1:2, 128 : 128 + up_bias.shape[1]] = up_bias[...]


def spread_vectors(blocks, vectors):
    width = vectors.shape[1]
    devices = blocks.shape[0] // 8
    piece = width // devices
    table = blocks[...].astype(F32)
    vectors[...] = jnp.zeros_like(vectors)

    def put(rows, at, start):
        window = min(start // 128 * 128, width - 256)
        wide = jnp.concatenate([rows, jnp.zeros_like(rows)], 1)
        wide = pltpu.roll(wide, start - window, 1)
        vectors[at, window : window + 256] = vectors[at, window : window + 256] + wide

    for d in range(devices):
        block = table[8 * d : 8 * d + 8]
        put(block[:, :128], slice(0, 8), piece * d)
        put(block[0:1, 128:], slice(8, 9), piece * d)
        up = 4 * piece * d
        put(block[1:2, 128:], slice(9 + up // width, 10 + up // width), up % width)


def column_of(table, source, row):
    line = table[source, pl.ds(row, 1), :].astype(F32)
    tall = jnp.broadcast_to(line, (8, line.shape[1]))
    return jnp.concatenate([tall[:, n : n + 128].T[:, 0:1] for n in range(0, line.shape[1], 128)], 0)


def forward_kernel(
    deep,
    patches,
    cotangent,
    flags_in,
    clips_in,
    mask_embed,
    norm_gain,
    norm_shift,
    qv_bias,
    branch_bias,
    up_bias,
    shard_qkv,
    shard_out,
    shard_up,
    shard_down,
    o_qkv,
    o_out,
    o_up,
    o_down,
    o_small,
    o_x,
    o_cot,
    o_flags,
    o_first,
    o_q,
    o_k,
    o_v,
    o_mixed,
    o_second,
    o_rate,
    o_middle,
    o_act,
    o_slope,
    o_expon,
    o_result,
    w_qkv,
    w_out,
    w_up,
    w_down,
    j_qkv,
    j_out,
    j_up,
    j_down,
    j_vector,
    shard_vector,
    w_vector,
    small,
    x,
    flags_all,
    clips_all,
    first,
    q,
    k,
    v,
    mixed,
    second,
    rate,
    middle,
    expon,
    slope,
    result,
    q_code,
    k_code,
    join_sems,
    gather_sends,
    gather_recvs,
    row_sends,
    row_recvs,
    local_sems,
    expon_sems,
    act_sems,
):
    place = Place(deep)
    span, width = patches.shape[1:]
    rows = x.shape[0]
    sources = rows // span
    half = width // HEADS
    pairs = HEADS // 2
    inner = w_up.shape[1]
    chunks = inner // width

    fill_vectors(shard_vector, mask_embed, norm_gain, norm_shift, qv_bias, branch_bias, up_bias)
    place.enter()

    kinds = ((patches, x), (flags_in, flags_all), (clips_in, clips_all), (cotangent, o_cot))

    def landing(kind, source):
        dst = kinds[kind][1]
        if kind in (1, 2):
            return dst.at[source]
        return dst.at[pl.ds(pl.multiple_of(source * span, span), span)]

    def leaving(kind, to):
        src = kinds[kind][0]
        return src if kind in (1, 2) else src.at[to]

    def own_part(kind):
        return pltpu.make_async_copy(
            leaving(kind, place.tm), landing(kind, place.tm), local_sems.at[kind]
        )

    def row_copy(kind, step, to):
        return remote(
            leaving(kind, to),
            landing(kind, place.tm),
            row_sends.at[kind, step],
            row_recvs.at[kind, step],
            (place.batch, to),
        )

    def row_wait(kind, step):
        source = place.mate(step)
        there = landing(kind, source)
        remote(
            there, there, row_sends.at[kind, step], row_recvs.at[kind, step], (place.batch, source)
        ).wait_recv()

    zpq = Route(place, "zpq", True)
    zxy = Route(place, "zpq", False)
    pzq = Route(place, "pzq", True)
    xzy = Route(place, "pzq", False)
    named = {}
    for i, (name, route, shard, joined, full) in enumerate(
        (
            (VECTOR, zpq, shard_vector, j_vector, w_vector),
            (QKV, zxy, shard_qkv, j_qkv, w_qkv),
            (OUT, zpq, shard_out, j_out, w_out),
            (UP, zxy, shard_up, j_up, w_up),
            (DOWN, pzq, shard_down, j_down, w_down),
        )
    ):
        named[name] = Gather(
            place, route, shard, joined, full, join_sems.at[i], gather_sends.at[i], gather_recvs.at[i]
        )
    gathers = list(named.values())
    for gather in gathers:
        gather.join()
    def send_rows(kinds):
        for kind in kinds:
            for step in range(1, sources):
                row_copy(kind, step, place.mate(step)).start()

    def run(steps):
        for what, *which in steps:
            if what == ROWS:
                send_rows((1, 2, 0))
            elif what == COTANGENT:
                send_rows((3,))
            elif what == SPREAD:
                spread_vectors(w_vector, small)
            elif what == FIRST:
                named[which[0]].first()
            elif what == FINISH:
                named[which[0]].finish()
            else:
                named[which[0]].stage(which[1], slice(which[2], which[3]))

    def after(loop, index):
        for when, steps in FORWARD_STEPS.get(loop, {}).items():
            if isinstance(index, int):
                if index == when:
                    run(steps)
            else:
                pl.when(index == when)(functools.partial(run, steps))

    for kind in (1, 2, 0):
        own_part(kind).start()
    run(FORWARD_STEPS[START][0])
    keeping = []

    def keep(src, dst):
        copy = pltpu.make_async_copy(src, dst, local_sems.at[4 + len(keeping)])
        copy.start()
        keeping.append(copy)


    vectors = small
    lane = lax.broadcasted_iota(jnp.int32, (1, 2 * half), 1)
    low = lane < half
    own_lanes = [low.astype(F32), 1.0 - low.astype(F32)]

    for kind in (1, 2, 0):
        own_part(kind).wait()

    @pl.loop(0, sources)
    def _(step):
        @pl.when(step > 0)
        def _():
            for kind in (1, 2, 0):
                row_wait(kind, step)

        source = place.mate(step)
        at = pl.ds(pl.multiple_of(source * span, span), span)
        flags = column_of(flags_all, source, place.tm)
        clips = column_of(clips_all, source, place.tm)
        start = jnp.where(flags == 1.0, vectors[0:1, :], x[at, :].astype(F32))
        middle[at, :] = start
        center, speed = moments(start)
        normed = (center * speed * vectors[1:2, :] + vectors[3:4, :]).astype(BF)
        first[at, :] = normed
        q[at, :] = (nn(normed, w_qkv[:, 0:width]) + vectors[5:6, :]).astype(BF) * (1.0 / math.sqrt(half))
        k[at, :] = nn(normed, w_qkv[:, width : 2 * width]).astype(BF)
        v[at, :] = (nn(normed, w_qkv[:, 2 * width :]) + vectors[6:7, :]).astype(BF)
        clip_lane = lax.broadcasted_iota(jnp.int32, (span, 2 * half), 1).astype(F32)
        for h in range(2):
            base = float(half * (1 - h))
            same = clip_lane - base == clips
            coded = jnp.logical_and(clip_lane >= base, clip_lane < base + 5.0)
            q_code[h, at, :] = jnp.where(same, 1.0, 0.0).astype(BF)
            k_code[h, at, :] = jnp.where(jnp.logical_and(coded, jnp.logical_not(same)), FAR, 0.0).astype(BF)
        after(PROJECT, step)

    for src, dst in ((w_qkv, o_qkv), (small, o_small), (x, o_x), (flags_all, o_flags), (first, o_first), (q, o_q), (k, o_k), (v, o_v)):
        keep(src, dst)

    block = min(rows, 512)

    def expon_copy(p):
        return pltpu.make_async_copy(expon.at[p % 2], o_expon.at[pl.ds(2 * p, 2)], expon_sems.at[p % 2])

    def attend(p):
        lanes = pl.ds(pl.multiple_of(p * 2 * half, 128), 2 * half)

        @pl.when(p >= 2)
        def _():
            expon_copy(p - 2).wait()

        slot = p % 2
        keys, values = [], []
        for h in range(2):
            mask = own_lanes[h].astype(BF)
            keys.append(k[:, lanes] * mask + k_code[h])
            values.append(v[:, lanes] * mask + own_lanes[1 - h].astype(BF))
        for part in range(rows // block):
            at = pl.ds(part * block, block)
            mixes = []
            for h in range(2):
                query = q[at, lanes] * own_lanes[h].astype(BF) + q_code[h, at, :]
                scores = nt(query, keys[h])
                peak = jnp.max(scores, -1, keepdims=True)
                weights = jnp.exp2((scores - peak) * LOG2E).astype(BF)
                expon[slot, h, at, :] = weights
                mixes.append(nn(weights, values[h]))
            top = jnp.where(low, mixes[0], mixes[1])
            totals = pltpu.roll(jnp.where(low, mixes[1], mixes[0]), half, 1)
            speed = 1.0 / totals
            rate[at, lanes] = speed
            mixed[at, lanes] = (top * speed).astype(BF)
        expon_copy(p).start()
        after(ATTEND, p)

    pl.loop(0, pairs)(attend)
    for src, dst in ((w_out, o_out), (w_up, o_up), (mixed, o_mixed), (rate, o_rate)):
        keep(src, dst)
    for p in (pairs - 2, pairs - 1):
        expon_copy(p).wait()

    def act(j, at):
        return expon.at[j // 2, j % 2, at, pl.ds(0, width)]

    def slope_copies(step):
        at = pl.ds(pl.multiple_of(step * span, span), span)
        return [
            pltpu.make_async_copy(slope.at[step % 2, j], o_slope.at[j, at], act_sems.at[step % 2, j])
            for j in range(chunks)
        ]

    def act_copies(step):
        at = pl.ds(pl.multiple_of(step * span, span), span)
        return [pltpu.make_async_copy(act(j, at), o_act.at[j, at], act_sems.at[2, j]) for j in range(chunks)]

    def rise(step):
        @pl.when(step >= 2)
        def _():
            for copy in slope_copies(step - 2):
                copy.wait()

        at = pl.ds(pl.multiple_of(step * span, span), span)
        hidden = middle[at, :] + nn(mixed[at, :], w_out[...]) + vectors[7:8, :]
        middle[at, :] = hidden
        center, speed = moments(hidden)
        normed = (center * speed * vectors[2:3, :] + vectors[4:5, :]).astype(BF)
        second[at, :] = normed
        for j in range(chunks):
            pre = nn(normed, w_up[:, j * width : (j + 1) * width]) + vectors[9 + j : 10 + j, :]
            value, steep = gelu_and_slope(pre)
            expon[j // 2, j % 2, at, 0:width] = value.astype(BF)
            slope[step % 2, j] = steep.astype(BF)
        for copy in slope_copies(step) + act_copies(step):
            copy.start()
        after(RISE, step)

    def fall(step):
        at = pl.ds(pl.multiple_of(step * span, span), span)
        total = middle[at, :] + vectors[8:9, :]
        for j in range(chunks):
            total = total + nn(expon[j // 2, j % 2, at, 0:width], w_down[j * width : (j + 1) * width, :])
        result[at, :] = total.astype(BF)

    pl.loop(0, sources)(rise)
    keep(second, o_second)
    keep(middle, o_middle)
    keep(w_down, o_down)
    pl.loop(0, sources)(fall)
    keep(result, o_result)
    for step in range(sources):
        for copy in act_copies(step):
            copy.wait()
    for step in (sources - 2, sources - 1):
        for copy in slope_copies(step):
            copy.wait()
    for step in range(1, sources):
        row_wait(3, step)
        for kind in range(4):
            row_copy(kind, step, place.mate(step)).wait_send()
    for copy in keeping:
        copy.wait()
    for gather in gathers:
        gather.drain()


def forward(deep, patches, cotangent, flags, clips, vectors, shards):
    sources, span, width = patches.shape
    qkv, out, up, down = shards
    rows = sources * span
    chips = deep * 4
    inner = up.shape[1]
    chunks = inner // width
    shape = jax.ShapeDtypeStruct
    fulls = [(2 * chips * s.shape[0], s.shape[1]) for s in shards]
    plane = (rows, width)
    outs = [shape(f, BF) for f in fulls]
    outs += [shape((16, width), F32), shape(plane, BF), shape(plane, BF)]
    outs += [shape((sources,) + flags.shape, jnp.int32)]
    outs += [shape(plane, BF)] * 6 + [shape(plane, F32)] * 2
    outs += [shape((chunks, rows, width), BF)] * 2
    outs += [shape((HEADS, rows, rows), BF), shape(plane, BF)]
    scratch = [pltpu.VMEM(f, BF) for f in fulls]
    scratch += [pltpu.VMEM((2 * s.shape[0], s.shape[1] // 2), F32) for s in shards]
    scratch += [
        pltpu.VMEM((16, 128), F32),
        pltpu.VMEM((8, 256), F32),
        pltpu.VMEM((16 * chips, 256), BF),
        pltpu.VMEM((16, width), F32),
        pltpu.VMEM(plane, BF),
        pltpu.VMEM((sources,) + flags.shape, jnp.int32),
        pltpu.VMEM((sources,) + flags.shape, jnp.int32),
    ]
    scratch += [pltpu.VMEM(plane, BF)] * 6 + [pltpu.VMEM(plane, F32)] * 2
    scratch += [
        pltpu.VMEM((2, 2, rows, rows), BF),
        pltpu.VMEM((2, chunks, span, width), BF),
        pltpu.VMEM(plane, BF),
        pltpu.VMEM((2, rows, 128), BF),
        pltpu.VMEM((2, rows, 128), BF),
    ]
    dma = pltpu.SemaphoreType.DMA
    scratch += [
        dma((5,)),
        dma((5, 1 + 2 * chips)),
        dma((5, 1 + 2 * chips)),
        dma((4, sources)),
        dma((4, sources)),
        dma((20,)),
        dma((2,)),
        dma((3, chunks)),
    ]
    return pl.pallas_call(
        functools.partial(forward_kernel, deep),
        out_shape=outs,
        in_specs=[HBM] * 4 + [pl.BlockSpec(memory_space=pltpu.VMEM)] * 6 + [HBM] * 4,
        out_specs=[HBM] * len(outs),
        scratch_shapes=scratch,
        compiler_params=pltpu.CompilerParams(
            collective_id=0, has_side_effects=True, vmem_limit_bytes=62 * 2**20
        ),
        name="forward",
    )(patches, cotangent, flags, clips, *vectors, *shards)


class Scatter:
    def __init__(self, place, route, held, slots, final, sends, recvs, piece=None):
        self.place, self.route = place, route
        self.held, self.slots, self.final = held, slots, final
        self.sends, self.recvs = sends, recvs
        self.rows = slots.shape[1]
        self.width = piece
        self.sent = []

    def region(self, shifts):
        return pl.ds(pl.multiple_of(self.route.chip(shifts) * self.rows, 16), self.rows)

    def columns(self, piece):
        if piece is None:
            return pl.ds(0, self.held.shape[1])
        return pl.ds(pl.multiple_of(piece * self.width, 128), self.width)

    def parts(self, stage):
        route = self.route
        for d in range(1, route.sizes[stage]):
            for earlier in route.offsets(stage):
                offset = list(earlier)
                offset[stage] = d
                yield d, [-o for o in earlier], route.index(offset) - 1

    def copy(self, stage, d, back, slot, piece):
        shifts, to = list(back), [0, 0, 0]
        shifts[stage] = to[stage] = d
        columns = self.columns(piece)
        n = 0 if piece is None else piece
        return remote(
            self.held.at[self.region(shifts), columns],
            self.slots.at[slot, :, columns],
            self.sends.at[n, slot],
            self.recvs.at[n, slot],
            self.route.device(to),
        )

    def send(self, stage, piece=None):
        self.sent.append((stage, piece))
        for d, back, slot in self.parts(stage):
            self.copy(stage, d, back, slot, piece).start()

    def add(self, stage, piece=None):
        found = {}
        columns = self.columns(piece)
        for d, back, slot in self.parts(stage):
            self.copy(stage, d, back, slot, piece).wait_recv()
            found.setdefault(tuple(back), []).append(slot)
        for back, slots in found.items():
            at = self.region(back)
            total = self.held[at, columns].astype(F32)
            for slot in slots:
                total = total + self.slots[slot, :, columns].astype(F32)
            if stage == 0:
                self.final[:, columns] = total
            else:
                self.held[at, columns] = total.astype(BF)

    def drain(self):
        for stage, piece in self.sent:
            for d, back, slot in self.parts(stage):
                self.copy(stage, d, back, slot, piece).wait_send()


class RowScatter(Scatter):
    def part_q(self, z, p):
        place = self.place
        behind = (place.z - z + place.deep) % place.deep
        return [p, (place.deep - behind) % place.deep, 0], (p * place.deep + behind) * 2

    def copy_q(self, z, p):
        shifts, slot = self.part_q(z, p)
        return self.copy(2, 1, shifts, slot, None)

    def send_q(self, z):
        for p in range(2):
            self.copy_q(z, p).start()

    def add_q(self, z):
        for p in range(2):
            shifts, slot = self.part_q(z, p)
            self.copy_q(z, p).wait_recv()
            at = self.region(shifts)
            self.held[at, :] = (self.held[at, :].astype(F32) + self.slots[slot].astype(F32)).astype(BF)

    def copy_z(self, z, p):
        place = self.place
        ahead = (z - place.z + place.deep) % place.deep
        return self.copy(1, ahead, [p, 0, 0], (p * place.deep + ahead) * 2 - 1, None)

    def send_z(self, z):
        @pl.when(self.place.z != z)
        def _():
            for p in range(2):
                self.copy_z(z, p).start()

    def drain(self):
        place = self.place
        for z in range(place.deep):
            for p in range(2):
                self.copy_q(z, p).wait_send()
        for d, back, slot in self.parts(1):
            self.copy(1, d, back, slot, None).wait_send()
        super().drain()


def backward_kernel(
    deep,
    i_qkv,
    i_out,
    i_up,
    i_down,
    i_small,
    i_x,
    i_cot,
    i_flags,
    i_first,
    i_q,
    i_k,
    i_v,
    i_mixed,
    i_second,
    i_rate,
    i_middle,
    i_act,
    i_slope,
    i_expon,
    i_result,
    i_own_cot,
    o_qkv,
    o_out,
    o_up,
    o_down,
    o_small,
    o_patch,
    o_result,
    w_qkv,
    w_out,
    w_up,
    w_down,
    upstream,
    second,
    gathered,
    middle,
    expon,
    score_grad,
    trio,
    rate,
    mixed,
    staged,
    h_qkv,
    h_out,
    h_up,
    h_down,
    s_qkv,
    s_out,
    s_up,
    s_down,
    f_qkv,
    f_out,
    f_up,
    f_down,
    vectors,
    flags_all,
    small,
    small_slots,
    patch,
    load_sems,
    chunk_sems,
    pair_sems,
    hand_sends,
    hand_recvs,
    scatter_sends,
    scatter_recvs,
    final_sends,
    final_recvs,
    small_sends,
    small_recvs,
    row_sends,
    row_recvs,
    local_sems,
):
    place = Place(deep)
    rows, width = upstream.shape
    sources, span = patch.shape[:2]
    half = width // HEADS
    pairs = HEADS // 2
    chunks = i_act.shape[0]
    part = width // 2
    first = second
    mixed_grad = upstream
    first_grad = gathered

    loads = [
        pltpu.make_async_copy(src, dst, load_sems.at[i])
        for i, (src, dst) in enumerate(
            (
                (i_second, second),
                (i_middle, middle),
                (i_small, vectors),
                (i_flags, flags_all),
                (i_out, w_out),
                (i_qkv, w_qkv),
            )
        )
    ]

    def chunk_loads(j):
        slot = j % 2
        columns = pl.ds(pl.multiple_of(j * width, 128), width)
        moves = (
            (i_down.at[columns], w_down.at[slot]),
            (i_up.at[:, columns], w_up.at[slot]),
            (i_act.at[j], expon.at[slot, 0, :, pl.ds(0, width)]),
            (i_slope.at[j], expon.at[slot, 1, :, pl.ds(0, width)]),
        )
        return [pltpu.make_async_copy(src, dst, chunk_sems.at[slot, n]) for n, (src, dst) in enumerate(moves)]

    def pair_loads(p):
        slot = p % 2
        lanes = pl.ds(pl.multiple_of(p * 2 * half, 128), 2 * half)
        moves = (
            (i_expon.at[pl.ds(2 * p, 2)], expon.at[slot]),
            (i_q.at[:, lanes], trio.at[slot, 0]),
            (i_k.at[:, lanes], trio.at[slot, 1]),
            (i_v.at[:, lanes], trio.at[slot, 2]),
            (i_rate.at[:, lanes], rate.at[slot]),
            (i_mixed.at[:, lanes], mixed.at[slot]),
        )
        return [pltpu.make_async_copy(src, dst, pair_sems.at[slot, n]) for n, (src, dst) in enumerate(moves)]

    for step in range(sources):
        source = place.mate(step)
        at = pl.ds(pl.multiple_of(source * span, span), span)
        loads.insert(
            step,
            pltpu.make_async_copy(
                i_own_cot.at[place.tm] if step == 0 else i_cot.at[at], upstream.at[at], load_sems.at[6 + step]
            ),
        )
    early = sources + 1
    for copy in loads[:early] + chunk_loads(0) + loads[early:]:
        copy.start()
    place.enter()

    def result_copy(step):
        to = place.mate(step)
        return remote(
            i_result.at[pl.ds(pl.multiple_of(to * span, span), span)],
            o_result.at[place.tm],
            row_sends.at[1, step],
            row_recvs.at[1, step],
            (place.batch, to),
        )

    result_in = pltpu.make_async_copy(
        i_result.at[pl.ds(pl.multiple_of(place.tm * span, span), span)], patch.at[sources - 1], local_sems.at[5]
    )
    result_in.start()
    result_out = pltpu.make_async_copy(patch.at[sources - 1], o_result.at[place.tm], local_sems.at[5])
    for step in range(1, sources):
        result_copy(step).start()

    zpq = Route(place, "zpq", True)
    pzq = Route(place, "pzq", True)
    xzy = Route(place, "pzq", False)
    zxy = Route(place, "zpq", False)
    by_qkv = Scatter(place, xzy, h_qkv, s_qkv, f_qkv, scatter_sends.at[0], scatter_recvs.at[0], part)
    by_out = Scatter(place, zxy, h_out, s_out, f_out, scatter_sends.at[1], scatter_recvs.at[1], part)
    by_up = Scatter(place, zpq, h_up, s_up, f_up, scatter_sends.at[2], scatter_recvs.at[2], part)
    by_down = RowScatter(place, pzq, h_down, s_down, f_down, scatter_sends.at[3], scatter_recvs.at[3])
    scatters = [by_qkv, by_out, by_up, by_down]

    def columns(c):
        return pl.ds(pl.multiple_of(c * part, 128), part)

    def hand(slot, held, n):
        return remote(
            staged.at[slot, :, columns(1 - place.c)],
            held,
            hand_sends.at[n],
            hand_recvs.at[n],
            place.device(c=1 - place.c),
        )

    def settle(slot, held, n):
        copy = hand(slot, held, n)
        copy.wait_recv()
        held[...] = (held[...].astype(F32) + staged[slot, :, columns(place.c)].astype(F32)).astype(BF)
        copy.wait_send()

    def down_chunk(j):
        return (2 * (j % 2), h_down.at[pl.ds(pl.multiple_of(j * width, 128), width)], j)

    def up_chunk(j):
        return (2 * (j % 2) + 1, h_up.at[:, pl.ds(pl.multiple_of(j * part, 128), part)], chunks + j)

    def qkv_chunk(i):
        return (1 + i, h_qkv.at[:, pl.ds(pl.multiple_of(i * part, 128), part)], 2 * chunks + 1 + i)

    def out_chunk(i):
        return (0, h_out, 2 * chunks)

    named = {
        QKV: (by_qkv, qkv_chunk),
        OUT: (by_out, out_chunk),
        UP: (by_up, up_chunk),
        DOWN: (by_down, down_chunk),
    }
    summed = VectorSum(place, small, small_slots, small_sends, small_recvs)

    def run(steps):
        for what, *which in steps:
            if what == VECTOR_SEND:
                summed.send(which[0])
            elif what == VECTOR_ADD:
                summed.add(which[0])
            elif what == TURN:
                by_down.add_q(which[0])
                by_down.send_z(which[0])
            elif what == DELIVER:
                deliver(*deliveries[which[0]])
            elif what == SETTLE:
                scatter, chunk = named[which[0]]
                settle(*chunk(which[1]))
                if scatter is by_down:
                    scatter.send_q(which[1])
                else:
                    scatter.send(2, which[1])
            else:
                scatter = named[which[0]][0]
                stage = which[1]
                piece = None if scatter is by_down else which[2]
                scatter.add(stage, piece)
                if stage > 0:
                    scatter.send(stage - 1, piece)

    def after(loop, index):
        for when, steps in BACKWARD_STEPS.get(loop, {}).items():
            if isinstance(index, int):
                if index == when:
                    run(steps)
            else:
                pl.when(index == when)(functools.partial(run, steps))

    for copy in loads[:early]:
        copy.wait()

    def feed(j):
        @pl.when(j < chunks - 1)
        def _():
            for copy in chunk_loads(j + 1):
                copy.start()

        for copy in chunk_loads(j):
            copy.wait()
        slot = j % 2
        act_grad = nt(upstream[...], w_down[slot]).astype(BF).astype(F32)
        pre_grad = (act_grad * expon[slot, 1, :, 0:width].astype(F32)).astype(BF)
        small[0, pl.ds(9 + j, 1), :] = column_sum(pre_grad.astype(F32))
        staged[down_chunk(j)[0]] = tn(expon[slot, 0, :, 0:width], upstream[...]).astype(BF)
        hand(*down_chunk(j)).start()
        staged[up_chunk(j)[0]] = tn(second[...], pre_grad).astype(BF)
        hand(*up_chunk(j)).start()
        grown = nt(pre_grad, w_up[slot])

        gathered[...] = gathered[...] + grown

        after(FEED, j)

    gathered[...] = jnp.zeros_like(gathered)
    pl.loop(0, chunks)(feed)
    whole_mixed = pltpu.make_async_copy(i_mixed, expon.at[1, 1, :, pl.ds(0, width)], local_sems.at[0])
    whole_mixed.start()
    for copy in pair_loads(0):
        copy.start()
    load_first = pltpu.make_async_copy(i_first, first, local_sems.at[1])
    load_first.start()
    for copy in loads[early:]:
        copy.wait()
    for row in (0, 1, 2, 3, 4, 5, 6, 7, 8, 13, 14, 15):
        small[0, row : row + 1, :] = jnp.zeros((1, width), F32)

    def bend(n):
        at = pl.ds(pl.multiple_of(n * span, span), span)
        center, speed = moments(middle[at, :])
        normed = center * speed
        grad = gathered[at, :]
        small[0, 2:3, :] = small[0, 2:3, :] + column_sum(grad * normed)
        small[0, 4:5, :] = small[0, 4:5, :] + column_sum(grad)
        above = upstream[at, :].astype(F32)
        small[0, 8:9, :] = small[0, 8:9, :] + column_sum(above)
        total = above + norm_back(normed, speed, vectors[2:3, :], grad)
        middle[at, :] = total
        low_total = total.astype(BF)
        small[0, 7:8, :] = small[0, 7:8, :] + column_sum(low_total.astype(F32))
        mixed_grad[at, :] = nt(low_total, w_out[...]).astype(BF)

    pl.loop(0, sources)(bend)
    after(BEND, 0)
    whole_mixed.wait()
    staged[0] = tn(expon[1, 1, :, 0:width], middle[...].astype(BF)).astype(BF)
    hand(*out_chunk(0)).start()
    after(MIX, 0)
    load_first.wait()
    result_in.wait()
    result_out.start()

    lane = lax.broadcasted_iota(jnp.int32, (1, 2 * half), 1)
    low = lane < half
    own_lanes = [low.astype(F32), 1.0 - low.astype(F32)]
    block = min(rows, 512)

    def attend(p):
        slot = p % 2
        lanes = pl.ds(pl.multiple_of(p * 2 * half, 128), 2 * half)

        @pl.when(p < pairs - 1)
        def _():
            for copy in pair_loads(p + 1):
                copy.start()

        for copy in pair_loads(p):
            copy.wait()
        scaled = (mixed_grad[:, lanes].astype(F32) * rate[slot]).astype(BF)
        product = scaled.astype(F32) * mixed[slot].astype(F32)
        query, key, value = trio[slot, 0], trio[slot, 1], trio[slot, 2]
        key_grads, value_grads, query_grads = [], [], []
        for h in range(2):
            inner = jnp.sum(product * own_lanes[h], -1, keepdims=True)
            lone = scaled * own_lanes[h].astype(BF)
            query_parts = []
            for n in range(rows // block):
                at = slice(n * block, (n + 1) * block)
                grad = nt(lone[at], value)
                weights = expon[slot, h, at, :].astype(F32)
                grad = (weights * (grad - inner[at])).astype(BF)
                score_grad[h, at, :] = grad
                query_parts.append(nn(grad, key))
            query_grads.append(jnp.concatenate(query_parts, 0))
            key_grads.append(tn(query, score_grad[h]))
            value_grads.append(tn(scaled, expon[slot, h]))
        query_grad = (jnp.where(low, query_grads[0], query_grads[1]) * (1.0 / math.sqrt(half))).astype(BF)
        key_grad = jnp.concatenate([key_grads[0][:half], key_grads[1][half:]], 0).T.astype(BF)
        value_grad = jnp.concatenate([value_grads[0][:half], value_grads[1][half:]], 0).T.astype(BF)
        small[0, 5:6, lanes] = column_sum(query_grad.astype(F32))
        small[0, 6:7, lanes] = column_sum(value_grad.astype(F32))
        grads = jnp.concatenate([query_grad, key_grad, value_grad], 1)
        where = pl.ds(pl.multiple_of(slot * part, 128), part)
        staged[1 + p // 2, :, where] = tn(first[...], grads).astype(BF)
        weight = jnp.concatenate(
            [w_qkv[:, pl.ds(pl.multiple_of(p * 2 * half + n * width, 128), 2 * half)] for n in range(3)], 1
        )
        grown = nt(grads, weight)

        first_grad[...] = first_grad[...] + grown

        @pl.when(p % 2 == 1)
        def _():
            hand(*qkv_chunk(p // 2)).start()

        after(ATTEND, p)

    first_grad[...] = jnp.zeros_like(first_grad)
    pl.loop(0, pairs)(attend)
    load_x = pltpu.make_async_copy(i_x, expon.at[0, 0, :, pl.ds(0, width)], local_sems.at[2])
    load_x.start()
    load_x.wait()
    result_out.wait()

    def close(step):
        source = place.mate(sources - 1 - step)
        at = pl.ds(pl.multiple_of(source * span, span), span)
        flags = column_of(flags_all, source, place.tm) == 1.0
        start = jnp.where(flags, vectors[0:1, :], expon[0, 0, at, 0:width].astype(F32))
        center, speed = moments(start)
        normed = center * speed
        grad = first_grad[at, :]
        small[0, 1:2, :] = small[0, 1:2, :] + column_sum(grad * normed)
        small[0, 3:4, :] = small[0, 3:4, :] + column_sum(grad)
        total = middle[at, :] + norm_back(normed, speed, vectors[1:2, :], grad)
        small[0, 0:1, :] = small[0, 0:1, :] + column_sum(jnp.where(flags, total, 0.0))
        patch[step] = jnp.where(flags, 0.0, total).astype(BF)

        @pl.when(step < sources - 1)
        def _():
            remote(
                patch.at[step],
                o_patch.at[place.tm],
                row_sends.at[0, sources - 1 - step],
                row_recvs.at[0, sources - 1 - step],
                (place.batch, source),
            ).start()

        after(CLOSE, step)

    pl.loop(0, sources)(close)
    own_patch = pltpu.make_async_copy(patch.at[sources - 1], o_patch.at[place.tm], local_sems.at[3])
    own_patch.start()
    moves = []

    def deliver(final, target, pieces):
        shard = target.shape[0]
        for near, far, jump, size in pieces:
            to = pl.ds(pl.multiple_of(far + place.c * jump, 128), size)
            mine = pl.ds(pl.multiple_of(place.c * shard, 8), shard)
            theirs = pl.ds(pl.multiple_of((1 - place.c) * shard, 8), shard)
            n = len(moves) // 2
            moves.append(
                pltpu.make_async_copy(final.at[mine, pl.ds(near, size)], target.at[:, to], local_sems.at[6 + n])
            )
            moves.append(
                remote(
                    final.at[theirs, pl.ds(near, size)],
                    target.at[:, to],
                    final_sends.at[n],
                    final_recvs.at[n],
                    place.device(c=1 - place.c),
                )
            )
            moves[-2].start()
            moves[-1].start()

    deliveries = {
        DOWN: (f_down, o_down, [(0, 0, part, part)]),
        UP: (f_up, o_up, [(j * part, j * width, part, part) for j in range(chunks)]),
        OUT: (f_out, o_out, [(0, 0, part, part)]),
        QKV: (
            f_qkv,
            o_qkv,
            [
                (i * part + n * 2 * half, n * width + i * 4 * half, 2 * half, 2 * half)
                for i in range(3)
                for n in range(3)
            ],
        ),
    }
    after(TAIL, 0)
    own_small = pltpu.make_async_copy(small.at[4], o_small, local_sems.at[4])
    own_small.start()
    for move in moves:
        move.wait()
    for step in range(1, sources):
        copy = remote(
            patch.at[0], o_patch.at[place.mate(step)], row_sends.at[0, step], row_recvs.at[0, step], place.device()
        )
        copy.wait_recv()
        copy.wait_send()
        result_copy(step).wait()
    own_patch.wait()
    own_small.wait()
    for scatter in scatters:
        scatter.drain()


def backward(deep, saved, shards, cotangent):
    sources, span, width = cotangent.shape
    rows = sources * span
    chips = deep * 4
    chunks = shards[2].shape[1] // width
    shape = jax.ShapeDtypeStruct
    plane = (rows, width)
    small = saved[4]
    flags = saved[7]
    halves = [(2 * chips * s.shape[0], s.shape[1] // 2) for s in shards]
    outs = [shape(s.shape, F32) for s in shards] + [shape(small.shape, F32)] + [shape(cotangent.shape, BF)] * 2
    scratch = [
        pltpu.VMEM(saved[0].shape, BF),
        pltpu.VMEM(saved[1].shape, BF),
        pltpu.VMEM((2, width, width), BF),
        pltpu.VMEM((2, width, width), BF),
        pltpu.VMEM(plane, BF),
        pltpu.VMEM(plane, BF),
        pltpu.VMEM(plane, F32),
        pltpu.VMEM(plane, F32),
        pltpu.VMEM((2, 2, rows, rows), BF),
        pltpu.VMEM((2, rows, rows), BF),
        pltpu.VMEM((2, 3, rows, 2 * width // HEADS), BF),
        pltpu.VMEM((2, rows, 2 * width // HEADS), F32),
        pltpu.VMEM((2, rows, 2 * width // HEADS), BF),
        pltpu.VMEM((4, width, width), BF),
    ]
    scratch += [pltpu.VMEM(h, BF) for h in halves]
    scratch += [pltpu.VMEM((chips - 1, 2 * s.shape[0], s.shape[1] // 2), BF) for s in shards]
    scratch += [pltpu.VMEM((2 * s.shape[0], s.shape[1] // 2), F32) for s in shards]
    scratch += [
        pltpu.VMEM(small.shape, F32),
        pltpu.VMEM(flags.shape, jnp.int32),
        pltpu.VMEM((5,) + small.shape, F32),
        pltpu.VMEM((2 + deep,) + small.shape, F32),
        pltpu.VMEM(cotangent.shape, BF),
    ]
    dma = pltpu.SemaphoreType.DMA
    scratch += [
        dma((6 + sources,)),
        dma((2, 4)),
        dma((2, 6)),
        dma((2 * chunks + 4,)),
        dma((2 * chunks + 4,)),
        dma((4, chunks, chips - 1)),
        dma((4, chunks, chips - 1)),
        dma((11 + chunks,)),
        dma((11 + chunks,)),
        dma((2 + deep,)),
        dma((2 + deep,)),
        dma((2, sources)),
        dma((2, sources)),
        dma((17 + chunks,)),
    ]
    return pl.pallas_call(
        functools.partial(backward_kernel, deep),
        out_shape=outs,
        in_specs=[HBM] * (len(saved) + 1),
        out_specs=[HBM] * len(outs),
        scratch_shapes=scratch,
        compiler_params=pltpu.CompilerParams(
            collective_id=1, has_side_effects=True, vmem_limit_bytes=63 * 2**20
        ),
        name="backward",
    )(*saved, cotangent)


def finish_kernel(result, patch, sums, *refs):
    grads, outs = refs[:4], refs[4:]
    o_result, o_patch, embed, gain, shift, g_qkv, qv, g_out, branch, g_up, up, g_down = outs
    o_result[...] = result[...].astype(F32)
    o_patch[...] = patch[...].astype(F32)

    for grad, out in zip(grads, (g_qkv, g_out, g_up, g_down)):
        out[...] = grad[...]

    device = lax.axis_index("batch") * 4 + lax.axis_index("tm")
    width = sums.shape[1]
    piece, up_piece = embed.shape[1], up.shape[1]
    own = pltpu.roll(sums[...], lax.rem(width - device * piece, width), 1)
    row = 0
    for out in (embed, gain, shift, qv, branch):
        out[...] = own[row : row + out.shape[0], :piece]
        row += out.shape[0]
    lines = width // up_piece
    line = jnp.broadcast_to(sums[pl.ds(row + device // lines, 1), :], (8, width))
    at = lax.rem(width - lax.rem(device, lines) * up_piece, width)
    up[...] = pltpu.roll(line, at, 1)[0:1, :up_piece]


def finish(result, patch_grad, sums, grads, parts):
    shape = jax.ShapeDtypeStruct
    rows = pl.BlockSpec(result.shape, lambda i: (0, 0, 0))

    def whole(array):
        return pl.BlockSpec(array.shape, lambda i: (0, 0))

    vectors = [shape(p.shape, F32) for p in parts]
    embed, gain, shift, qv, branch, up = vectors
    outs = [embed, gain, shift, grads[0], qv, grads[1], branch, grads[2], up, grads[3]]
    outs = [shape(o.shape, F32) for o in outs]
    return pl.pallas_call(
        finish_kernel,
        grid=(1,),
        out_shape=[shape(result.shape, F32)] * 2 + outs,
        in_specs=[rows, rows, whole(sums)] + [whole(g) for g in grads],
        out_specs=[rows, rows] + [whole(o) for o in outs],
        compiler_params=pltpu.CompilerParams(vmem_limit_bytes=40 * 2**20),
        name="finish",
    )(result, patch_grad, sums, *grads)


def by_rows(
    deep,
    patches,
    segment_ids,
    mask_flags,
    cotangent,
    mask_embed,
    norm_gain,
    norm_shift,
    qkv_weight,
    qv_bias,
    out_weight,
    branch_bias,
    up_weight,
    up_bias,
    down_weight,
):
    sources, span, width = patches.shape
    shards = (qkv_weight, out_weight, up_weight, down_weight)
    vectors = (mask_embed[None], norm_gain, norm_shift, qv_bias, branch_bias, up_bias[None])
    saved = forward(deep, patches, cotangent, mask_flags, segment_ids, vectors, shards)
    *grads, sums, patch_grad, result = backward(deep, saved, shards, cotangent)
    result, patch_grad, embed, gain, shift, g_qkv, qv, g_out, branch, g_up, up, g_down = finish(
        result, patch_grad, sums, grads, vectors
    )
    return result, patch_grad, embed[0], gain, shift, g_qkv, qv, g_out, branch, g_up, up[0], g_down


def layer_norm(hidden, gain, shift):
    center = hidden - jnp.mean(hidden, -1, keepdims=True)
    spread = jnp.mean(center * center, -1, keepdims=True)
    return center * lax.rsqrt(spread + EPS) * gain + shift


def gelu_exact(values):
    return jax.nn.gelu(values, approximate=False)


def outer_sum(left, right):
    return lax.dot_general(
        left, right, (((0,), (0,)), ((), ())), preferred_element_type=jnp.float32
    )


def back_product(grad, weight):
    return lax.dot_general(
        grad, weight, (((1,), (1,)), ((), ())), preferred_element_type=jnp.float32
    )


def by_patches(
    patches,
    segment_ids,
    mask_flags,
    cotangent,
    mask_embed,
    norm_gain,
    norm_shift,
    qkv_weight,
    qv_bias,
    out_weight,
    branch_bias,
    up_weight,
    up_bias,
    down_weight,
):
    rows, span, width = patches.shape
    head_dim = width // HEADS
    scale = 1.0 / math.sqrt(head_dim)
    count = rows * span
    block = min(rows, max(1, 512 // span))
    groups = rows // block
    (
        whole_embed,
        whole_gain,
        whole_shift,
        whole_qkv,
        whole_qvbias,
        whole_out,
        whole_bias,
        whole_up,
        whole_upbias,
        whole_down,
    ) = (
        lax.all_gather(mask_embed.astype(jnp.bfloat16), ("batch", "tm"), axis=0, tiled=True),
        lax.all_gather(norm_gain.astype(jnp.bfloat16), ("batch", "tm"), axis=1, tiled=True),
        lax.all_gather(norm_shift.astype(jnp.bfloat16), ("batch", "tm"), axis=1, tiled=True),
        lax.all_gather(qkv_weight.astype(jnp.bfloat16), ("batch", "tm"), axis=0, tiled=True),
        lax.all_gather(qv_bias.astype(jnp.bfloat16), ("batch", "tm"), axis=1, tiled=True),
        lax.all_gather(out_weight.astype(jnp.bfloat16), ("batch", "tm"), axis=0, tiled=True),
        lax.all_gather(branch_bias.astype(jnp.bfloat16), ("batch", "tm"), axis=1, tiled=True),
        lax.all_gather(up_weight.astype(jnp.bfloat16), ("batch", "tm"), axis=0, tiled=True),
        lax.all_gather(up_bias.astype(jnp.bfloat16), ("batch", "tm"), axis=0, tiled=True),
        lax.all_gather(down_weight.astype(jnp.bfloat16), ("batch", "tm"), axis=0, tiled=True),
    )
    gains = whole_gain.astype(jnp.float32)
    shifts = whole_shift.astype(jnp.float32)
    biases = whole_bias.astype(jnp.float32)
    qv_terms = whole_qvbias.astype(jnp.float32)
    masked = (mask_flags == 1)[..., None]
    start = jnp.where(masked, whole_embed.astype(jnp.float32), patches.astype(jnp.float32))
    first_in = layer_norm(start, gains[0], shifts[0]).astype(jnp.bfloat16).reshape(count, width)
    projected = jnp.dot(first_in, whole_qkv, preferred_element_type=jnp.float32)
    queries = (projected[:, :width] + qv_terms[0]).astype(jnp.bfloat16)
    keys_local = projected[:, width : 2 * width].astype(jnp.bfloat16)
    values_local = (projected[:, 2 * width :] + qv_terms[1]).astype(jnp.bfloat16)
    pairs = jnp.concatenate([keys_local, values_local], 1).reshape(rows, span, 2 * width)
    all_pairs, all_segments = (
        lax.all_gather(pairs, "tm", axis=1, tiled=True),
        lax.all_gather(segment_ids, "tm", axis=1, tiled=True),
    )
    total_keys = all_pairs.shape[1]
    query_blocks = queries.reshape(groups, block, span, width)
    pair_blocks = all_pairs.reshape(groups, block, total_keys, 2 * width)
    own_segments = segment_ids.reshape(groups, block, span)
    far_segments = all_segments.reshape(groups, block, total_keys)

    def masked_scores(query_blk, key_blk, query_seg, key_seg):
        lead = query_blk.shape[1]
        trail = key_blk.shape[1]
        query_heads = query_blk.reshape(block, lead, HEADS, head_dim)
        key_heads = key_blk.reshape(block, trail, HEADS, head_dim)
        scores = (
            jnp.einsum(
                "bqhd,bkhd->bhqk", query_heads, key_heads, preferred_element_type=jnp.float32
            )
            * scale
        )
        allowed = (query_seg[:, :, None] == key_seg[:, None, :])[:, None]
        return jnp.where(allowed, scores, FAR)

    def attend(items):
        query_blk, pair_blk, own_seg, far_seg = items
        scores = masked_scores(query_blk, pair_blk[..., :width], own_seg, far_seg)
        peak = jnp.max(scores, -1, keepdims=True)
        expon = jnp.exp(scores - peak)
        totals = jnp.sum(expon, -1, keepdims=True)
        probs_low = (expon / totals).astype(jnp.bfloat16)
        value_heads = pair_blk[..., width:].reshape(block, total_keys, HEADS, head_dim)
        mixed_blk = jnp.einsum(
            "bhqk,bkhd->bqhd", probs_low, value_heads, preferred_element_type=jnp.float32
        )
        return (mixed_blk.reshape(block, span, width), peak + jnp.log(totals))

    mixed, log_totals = lax.map(attend, (query_blocks, pair_blocks, own_segments, far_segments))
    mixed_low = mixed.reshape(count, width).astype(jnp.bfloat16)
    branch = jnp.dot(mixed_low, whole_out, preferred_element_type=jnp.float32) + biases[0]
    middle = start + branch.reshape(rows, span, width)
    second_in = layer_norm(middle, gains[1], shifts[1]).astype(jnp.bfloat16).reshape(count, width)
    hidden_pre = jnp.dot(
        second_in, whole_up, preferred_element_type=jnp.float32
    ) + whole_upbias.astype(jnp.float32)
    hidden_act = gelu_exact(hidden_pre).astype(jnp.bfloat16)
    result = jnp.dot(hidden_act, whole_down, preferred_element_type=jnp.float32) + biases[1]
    output = middle + result.reshape(rows, span, width)
    back_qkv, back_out, back_up, back_down = (
        lax.all_gather(qkv_weight.astype(jnp.bfloat16), ("batch", "tm"), axis=0, tiled=True),
        lax.all_gather(out_weight.astype(jnp.bfloat16), ("batch", "tm"), axis=0, tiled=True),
        lax.all_gather(up_weight.astype(jnp.bfloat16), ("batch", "tm"), axis=0, tiled=True),
        lax.all_gather(down_weight.astype(jnp.bfloat16), ("batch", "tm"), axis=0, tiled=True),
    )
    upstream = cotangent.astype(jnp.float32)
    result_grad = upstream.reshape(count, width).astype(jnp.bfloat16)
    down_bias_grad = jnp.sum(result_grad.astype(jnp.float32), 0)
    down_weight_grad = outer_sum(hidden_act, result_grad)
    act_grad = back_product(result_grad, back_down).astype(jnp.bfloat16)
    gelu_pull = jax.vjp(gelu_exact, hidden_pre)[1]
    pre_grad = gelu_pull(act_grad.astype(jnp.float32))[0].astype(jnp.bfloat16)
    up_bias_grad = jnp.sum(pre_grad.astype(jnp.float32), 0)
    up_weight_grad = outer_sum(second_in, pre_grad)
    second_grad = back_product(pre_grad, back_up).reshape(rows, span, width)
    norm_pull_two = jax.vjp(layer_norm, middle, gains[1], shifts[1])[1]
    middle_norm_grad, gain_two_grad, shift_two_grad = norm_pull_two(second_grad)
    middle_grad = upstream + middle_norm_grad
    branch_grad = middle_grad.reshape(count, width).astype(jnp.bfloat16)
    out_bias_grad = jnp.sum(branch_grad.astype(jnp.float32), 0)
    out_weight_grad = outer_sum(mixed_low, branch_grad)
    mixed_grad = back_product(branch_grad, back_out).astype(jnp.bfloat16)
    mixed_blocks = mixed_grad.reshape(groups, block, span, width)

    def query_back(items):
        query_blk, pair_blk, own_seg, far_seg, log_total, grad_blk = items
        scores = masked_scores(query_blk, pair_blk[..., :width], own_seg, far_seg)
        probs = jnp.exp(scores - log_total)
        probs_low = probs.astype(jnp.bfloat16)
        query_heads = query_blk.reshape(block, span, HEADS, head_dim)
        key_heads = pair_blk[..., :width].reshape(block, total_keys, HEADS, head_dim)
        value_heads = pair_blk[..., width:].reshape(block, total_keys, HEADS, head_dim)
        grad_heads = grad_blk.reshape(block, span, HEADS, head_dim)
        prob_grad = jnp.einsum(
            "bqhd,bkhd->bhqk", grad_heads, value_heads, preferred_element_type=jnp.float32
        )
        inner = jnp.sum(probs * prob_grad, -1, keepdims=True)
        score_grad = (probs * (prob_grad - inner)).astype(jnp.bfloat16)
        query_grad = (
            jnp.einsum("bhqk,bkhd->bqhd", score_grad, key_heads, preferred_element_type=jnp.float32)
            * scale
        )
        key_grad = (
            jnp.einsum(
                "bhqk,bqhd->bkhd", score_grad, query_heads, preferred_element_type=jnp.float32
            )
            * scale
        )
        value_grad = jnp.einsum(
            "bhqk,bqhd->bkhd", probs_low, grad_heads, preferred_element_type=jnp.float32
        )
        pair_grad = jnp.concatenate(
            [
                key_grad.reshape(block, total_keys, width),
                value_grad.reshape(block, total_keys, width),
            ],
            -1,
        )
        return (query_grad.reshape(block, span, width), pair_grad, inner)

    query_grads, pair_grads, unused_inner = lax.map(
        query_back,
        (query_blocks, pair_blocks, own_segments, far_segments, log_totals, mixed_blocks),
    )
    pair_grads = pair_grads.reshape(rows, total_keys, 2 * width)
    local_pair_grads = lax.psum_scatter(pair_grads, "tm", scatter_dimension=1, tiled=True).astype(
        jnp.bfloat16
    )
    query_low = query_grads.reshape(count, width).astype(jnp.bfloat16)
    local_pair_grads = local_pair_grads.reshape(count, 2 * width)
    qkv_grad = jnp.concatenate([query_low, local_pair_grads], 1)
    qkv_weight_grad = outer_sum(first_in, qkv_grad)
    qv_bias_grad = jnp.stack(
        [
            jnp.sum(query_low.astype(jnp.float32), 0),
            jnp.sum(local_pair_grads[:, width:].astype(jnp.float32), 0),
        ]
    )
    first_grad = back_product(qkv_grad, back_qkv).reshape(rows, span, width)
    norm_pull_one = jax.vjp(layer_norm, start, gains[0], shifts[0])[1]
    start_norm_grad, gain_one_grad, shift_one_grad = norm_pull_one(first_grad)
    start_grad = middle_grad + start_norm_grad
    embed_grad = jnp.sum(jnp.where(masked, start_grad, 0.0), (0, 1))
    patch_grad = jnp.where(masked, 0.0, start_grad)
    (
        embed_sum,
        gain_sum,
        shift_sum,
        qkv_sum,
        qv_sum,
        out_sum,
        branch_sum,
        up_sum,
        up_bias_sum,
        down_sum,
    ) = (
        lax.psum_scatter(embed_grad, ("batch", "tm"), scatter_dimension=0, tiled=True),
        lax.psum_scatter(
            jnp.stack([gain_one_grad, gain_two_grad]),
            ("batch", "tm"),
            scatter_dimension=1,
            tiled=True,
        ),
        lax.psum_scatter(
            jnp.stack([shift_one_grad, shift_two_grad]),
            ("batch", "tm"),
            scatter_dimension=1,
            tiled=True,
        ),
        lax.psum_scatter(qkv_weight_grad, ("batch", "tm"), scatter_dimension=0, tiled=True),
        lax.psum_scatter(qv_bias_grad, ("batch", "tm"), scatter_dimension=1, tiled=True),
        lax.psum_scatter(out_weight_grad, ("batch", "tm"), scatter_dimension=0, tiled=True),
        lax.psum_scatter(
            jnp.stack([out_bias_grad, down_bias_grad]),
            ("batch", "tm"),
            scatter_dimension=1,
            tiled=True,
        ),
        lax.psum_scatter(up_weight_grad, ("batch", "tm"), scatter_dimension=0, tiled=True),
        lax.psum_scatter(up_bias_grad, ("batch", "tm"), scatter_dimension=0, tiled=True),
        lax.psum_scatter(down_weight_grad, ("batch", "tm"), scatter_dimension=0, tiled=True),
    )
    return (
        output,
        patch_grad,
        embed_sum,
        gain_sum,
        shift_sum,
        qkv_sum,
        qv_sum,
        out_sum,
        branch_sum,
        up_sum,
        up_bias_sum,
        down_sum,
    )


def solution(mesh):
    wide, deep = mesh.shape["batch"] * mesh.shape["tm"], mesh.shape["batch"] // 2

    def on_device(patches, *rest):
        width = patches.shape[-1]
        fits = mesh.shape["tm"] == patches.shape[0] == 4 and width % (8 * wide) == 0 and patches.shape[1] == 256
        return by_rows(deep, patches, *rest) if fits else by_patches(patches, *rest)

    return jax.shard_map(
        on_device,
        mesh=mesh,
        in_specs=(
            P("batch", "tm", None),
            P("batch", "tm"),
            P("batch", "tm"),
            P("batch", "tm", None),
            P(("batch", "tm")),
            P(None, ("batch", "tm")),
            P(None, ("batch", "tm")),
            P(("batch", "tm"), None),
            P(None, ("batch", "tm")),
            P(("batch", "tm"), None),
            P(None, ("batch", "tm")),
            P(("batch", "tm"), None),
            P(("batch", "tm")),
            P(("batch", "tm"), None),
        ),
        out_specs=(
            P("batch", "tm", None),
            P("batch", "tm", None),
            P(("batch", "tm")),
            P(None, ("batch", "tm")),
            P(None, ("batch", "tm")),
            P(("batch", "tm"), None),
            P(None, ("batch", "tm")),
            P(("batch", "tm"), None),
            P(None, ("batch", "tm")),
            P(("batch", "tm"), None),
            P(("batch", "tm")),
            P(("batch", "tm"), None),
        ),
        check_vma=False,
    )
```

```python
import functools
import math

import jax
import jax.numpy as jnp
from jax import lax
from jax.experimental import pallas as pl
from jax.experimental.pallas import tpu as pltpu
from jax.sharding import PartitionSpec as P

HEADS = 12
EPS = 1e-06
FAR = -1e30
LOG2E = math.log2(math.e)
BF = jnp.bfloat16
F32 = jnp.float32
MESH = pl.DeviceIdType.MESH
HBM = pl.BlockSpec(memory_space=pl.ANY)
SLOPE = 0.36
COEFFICIENTS = (
    0.14371305209487725,
    0.14177235930704382,
    0.1397197719471602,
    0.026547986328787306,
    0.18095585464885458,
    -0.1797659534284226,
    0.04705662553510592,
)


VECTOR, QKV, OUT, UP, DOWN = range(5)
START, PROJECT, ATTEND, RISE, FALL, FEED, BEND, MIX, CLOSE, TAIL = range(10)
FIRST, STAGE, FINISH, ROWS, COTANGENT, SPREAD = range(6)
SETTLE, TURN, ADD, VECTOR_SEND, VECTOR_ADD, DELIVER = range(6)

FORWARD_STEPS = {
    START: {
        0: [
            (FIRST, VECTOR),
            (FIRST, QKV),
            (FIRST, UP),
            (STAGE, VECTOR, 0, 0, 3),
            (FIRST, OUT),
            (STAGE, VECTOR, 1, 0, 4),
            (STAGE, QKV, 0, 0, 3),
            (STAGE, VECTOR, 2, 0, 8),
            (FINISH, VECTOR),
            (ROWS,),
            (STAGE, QKV, 1, 0, 4),
            (STAGE, QKV, 2, 0, 4),
            (SPREAD,),
            (STAGE, QKV, 2, 4, 8),
            (FINISH, QKV),
            (STAGE, UP, 0, 0, 3),
        ],
    },
    PROJECT: {
        1: [
            (FIRST, DOWN),
        ],
        3: [
            (STAGE, OUT, 0, 0, 3),
        ],
    },
    ATTEND: {
        1: [
            (STAGE, UP, 1, 0, 4),
        ],
        2: [
            (STAGE, OUT, 1, 0, 4),
            (STAGE, DOWN, 0, 0, 1),
        ],
        3: [
            (STAGE, UP, 2, 0, 4),
            (STAGE, DOWN, 1, 0, 3),
        ],
        5: [
            (STAGE, OUT, 2, 0, 4),
            (STAGE, OUT, 2, 4, 8),
            (STAGE, UP, 2, 4, 8),
            (FINISH, OUT),
            (FINISH, UP),
            (STAGE, DOWN, 1, 3, 6),
        ],
    },
    RISE: {
        0: [
            (STAGE, DOWN, 2, 0, 4),
            (COTANGENT,),
        ],
        1: [
            (STAGE, DOWN, 2, 4, 8),
        ],
        2: [
            (FINISH, DOWN),
        ],
    },
}


BACKWARD_STEPS = {
    FEED: {
        0: [
            (SETTLE, DOWN, 0),
            (SETTLE, UP, 0),
        ],
        1: [
            (SETTLE, DOWN, 1),
        ],
        2: [
            (SETTLE, UP, 1),
            (SETTLE, DOWN, 2),
            (TURN, 0),
        ],
        3: [
            (TURN, 1),
            (SETTLE, DOWN, 3),
            (TURN, 2),
            (SETTLE, UP, 3),
        ],
    },
    MIX: {
        0: [
            (SETTLE, UP, 2),
            (TURN, 3),
        ],
    },
    ATTEND: {
        0: [
            (SETTLE, OUT, 0),
        ],
        1: [
            (ADD, UP, 2, 0),
            (ADD, UP, 2, 2),
            (ADD, UP, 2, 3),
        ],
        2: [
            (ADD, UP, 2, 1),
        ],
        3: [
            (ADD, OUT, 2, 0),
            (ADD, UP, 1, 2),
            (ADD, UP, 1, 1),
            (ADD, UP, 1, 3),
        ],
        4: [
            (SETTLE, QKV, 0),
            (ADD, OUT, 1, 0),
            (ADD, DOWN, 1, 0),
            (ADD, UP, 1, 0),
        ],
    },
    CLOSE: {
        1: [
            (ADD, OUT, 0, 0),
            (ADD, QKV, 2, 0),
            (ADD, UP, 0, 2),
            (ADD, UP, 0, 1),
        ],
        2: [
            (SETTLE, QKV, 1),
        ],
    },
    TAIL: {
        0: [
            (VECTOR_SEND, 0),
            (DELIVER, OUT),
            (ADD, DOWN, 0, 0),
            (ADD, QKV, 2, 1),
            (VECTOR_ADD, 0),
            (ADD, UP, 0, 3),
            (SETTLE, QKV, 2),
            (VECTOR_SEND, 1),
            (ADD, UP, 0, 0),
            (ADD, QKV, 2, 2),
            (ADD, QKV, 1, 0),
            (DELIVER, DOWN),
            (VECTOR_ADD, 1),
            (VECTOR_SEND, 2),
            (VECTOR_ADD, 2),
            (ADD, QKV, 1, 1),
            (VECTOR_SEND, 3),
            (ADD, QKV, 1, 2),
            (ADD, QKV, 0, 2),
            (ADD, QKV, 0, 0),
            (DELIVER, UP),
            (ADD, QKV, 0, 1),
            (DELIVER, QKV),
            (VECTOR_ADD, 3),
        ],
    },
}


def nn(left, right):
    return jnp.dot(left, right, preferred_element_type=F32)


def nt(left, right):
    return lax.dot_general(left, right, (((1,), (1,)), ((), ())), preferred_element_type=F32)


def tn(left, right):
    return lax.dot_general(left, right, (((0,), (0,)), ((), ())), preferred_element_type=F32)


def gelu_and_slope(pre):
    size = jnp.abs(pre)
    t = 1.0 / (1.0 + SLOPE * size)
    poly = jnp.full_like(t, COEFFICIENTS[-1])
    for term in COEFFICIENTS[-2::-1]:
        poly = poly * t + term
    bell = jnp.exp2(pre * pre * (-0.5 * LOG2E))
    lower = poly * t * bell
    cdf = jnp.where(pre >= 0, 1.0 - lower, lower)
    return pre * cdf, cdf + pre * bell * (1.0 / math.sqrt(2.0 * math.pi))


def moments(hidden):
    center = hidden - jnp.mean(hidden, -1, keepdims=True)
    return center, lax.rsqrt(jnp.mean(center * center, -1, keepdims=True) + EPS)


def norm_back(normed, rate, gain, grad):
    scaled = grad * gain
    shared = jnp.mean(scaled * normed, -1, keepdims=True)
    return rate * (scaled - jnp.mean(scaled, -1, keepdims=True) - normed * shared)


def column_sum(values):
    return jnp.sum(values, 0, keepdims=True)


class Place:
    def __init__(self, deep):
        batch, tm = lax.axis_index("batch"), lax.axis_index("tm")
        self.deep = deep
        self.batch, self.tm = batch, tm
        self.z, self.y = batch // 2, batch % 2
        self.x, self.c = tm // 2, tm % 2

    def device(self, z=None, y=None, x=None, c=None):
        z = self.z if z is None else z
        y = self.y if y is None else y
        x = self.x if x is None else x
        c = self.c if c is None else c
        return (z * 2 + y, x * 2 + c)

    def mate(self, k):
        return (self.x + k // 2) % 2 * 2 + (self.c + k % 2) % 2

    def enter(self):
        barrier = pltpu.get_barrier_semaphore()
        others = [self.device(c=1 - self.c), self.device(x=1 - self.x), self.device(y=1 - self.y)]
        others.append(self.device(x=1 - self.x, c=1 - self.c))
        others += [self.device(z=(self.z + d) % self.deep) for d in range(1, self.deep)]
        for other in others:
            pl.semaphore_signal(barrier, inc=1, device_id=other, device_id_type=MESH)
        pl.semaphore_wait(barrier, len(others))


def remote(src, dst, send, recv, device):
    return pltpu.make_async_remote_copy(
        src_ref=src, dst_ref=dst, send_sem=send, recv_sem=recv, device_id=device, device_id_type=MESH
    )


class Route:
    def __init__(self, place, order, crossed):
        self.place, self.order, self.crossed = place, order, crossed
        c = place.c
        self.own = {
            "z": place.z,
            "p": c * place.y + (1 - c) * place.x if crossed else place.x,
            "q": c * place.x + (1 - c) * place.y if crossed else place.y,
        }
        self.size = {"z": place.deep, "p": 2, "q": 2}
        self.sizes = [self.size[axis] for axis in order]

    def shifted(self, shifts):
        at = {a: (self.own[a] + s % self.size[a]) % self.size[a] for a, s in zip(self.order, shifts)}
        c = self.place.c
        if self.crossed:
            return at["z"], c * at["p"] + (1 - c) * at["q"], c * at["q"] + (1 - c) * at["p"]
        return at["z"], at["q"], at["p"]

    def device(self, shifts):
        z, y, x = self.shifted(shifts)
        return self.place.device(z=z, y=y, x=x)

    def chip(self, shifts):
        z, y, x = self.shifted(shifts)
        return (z * 2 + y) * 2 + x

    def offsets(self, upto):
        found = [()]
        for stage, size in enumerate(self.sizes):
            found = [f + (o,) for f in found for o in range(size if stage < upto else 1)]
        return found

    def index(self, offset):
        flat = 0
        for o, size in zip(offset, self.sizes):
            flat = flat * size + o
        return flat


class Gather:
    def __init__(self, place, route, shard, joined, full, local, sends, recvs):
        self.place, self.route = place, route
        self.shard, self.joined, self.full = shard, joined, full
        self.local, self.sends, self.recvs = local, sends, recvs
        self.rows = shard.shape[0]
        self.half = joined.shape[1]
        self.count = 0

    def columns(self, c):
        return pl.ds(pl.multiple_of(c * self.half, 128), self.half)

    def region(self, chip, c):
        rows = 2 * self.rows
        return self.full.at[pl.ds(pl.multiple_of(chip * rows, 16), rows), self.columns(c)]

    def ship(self, src, dst, recv, device):
        remote(src, dst, self.sends.at[self.count], recv, device).start()
        self.count += 1

    def join(self):
        place = self.place
        own = pl.ds(pl.multiple_of(place.c * self.rows, 8), self.rows)
        self.mine = pltpu.make_async_copy(
            self.shard.at[:, self.columns(place.c)], self.joined.at[own], self.local
        )
        self.mine.start()
        self.pair = self.recvs.at[0]
        self.ship(
            self.shard.at[:, self.columns(1 - place.c)],
            self.joined.at[own],
            self.recvs.at[0],
            place.device(c=1 - place.c),
        )

    def arrive(self, offset, stage):
        route, place = self.route, self.place
        chip = route.chip([-o for o in offset])
        block = self.region(chip, place.c)
        for later in range(stage + 1, 3):
            for d in range(1, route.sizes[later]):
                shifts = [0, 0, 0]
                shifts[later] = d
                seen = list(offset)
                seen[later] = d
                self.ship(block, block, self.recvs.at[1 + route.index(seen)], route.device(shifts))
        total = math.prod(route.sizes)
        self.ship(
            block,
            block,
            self.recvs.at[1 + total + route.index(offset)],
            place.device(c=1 - place.c),
        )

    def first(self):
        place = self.place
        self.mine.wait()
        own = pl.ds(pl.multiple_of((1 - place.c) * self.rows, 8), self.rows)
        remote(
            self.joined.at[own], self.joined.at[own], self.sends.at[0], self.recvs.at[0], place.device(c=1 - place.c)
        ).wait()
        chip = self.route.chip([0, 0, 0])
        self.region(chip, place.c)[...] = self.joined[...].astype(BF)
        self.arrive((0, 0, 0), -1)

    def stage(self, stage, some=slice(None)):
        route = self.route
        for offset in [o for o in route.offsets(stage + 1) if o[stage] > 0][some]:
            block = self.region(route.chip([-o for o in offset]), self.place.c)
            remote(
                block, block, self.sends.at[0], self.recvs.at[1 + route.index(offset)], self.place.device()
            ).wait_recv()
            self.arrive(offset, stage)

    def finish(self):
        route = self.route
        total = math.prod(route.sizes)
        for offset in route.offsets(3):
            block = self.region(route.chip([-o for o in offset]), 1 - self.place.c)
            remote(
                block,
                block,
                self.sends.at[0],
                self.recvs.at[1 + total + route.index(offset)],
                self.place.device(),
            ).wait_recv()

    def drain(self):
        block = self.region(self.route.chip([0, 0, 0]), self.place.c)
        for n in range(1, self.count):
            remote(block, block, self.sends.at[n], self.recvs.at[0], self.place.device()).wait_send()


class VectorSum:
    def __init__(self, place, held, slots, sends, recvs):
        self.held, self.slots = held, slots
        stages = [
            [place.device(c=1 - place.c)],
            [place.device(x=1 - place.x)],
            [place.device(y=1 - place.y)],
            [place.device(z=(place.z + d) % place.deep) for d in range(1, place.deep)],
        ]
        self.copies, slot = [], 0
        for stage, others in enumerate(stages):
            self.copies.append([])
            for other in others:
                copy = remote(held.at[stage], slots.at[slot], sends.at[slot], recvs.at[slot], other)
                self.copies[-1].append((copy, slot))
                slot += 1

    def send(self, stage):
        for copy, _ in self.copies[stage]:
            copy.start()

    def add(self, stage):
        total = self.held[stage]
        for copy, slot in self.copies[stage]:
            copy.wait()
            total = total + self.slots[slot]
        self.held[stage + 1] = total


def fill_vectors(block, mask_embed, norm_gain, norm_shift, qv_bias, branch_bias, up_bias):
    block[...] = jnp.zeros_like(block)
    piece = mask_embed.shape[1]
    row = 0
    for part in (mask_embed, norm_gain, norm_shift, qv_bias):
        block[row : row + part.shape[0], 0:piece] = part[...]
        row += part.shape[0]
    block[row : row + 1, 0:piece] = branch_bias[0:1, :]
    block[0:1, 128 : 128 + piece] = branch_bias[1:2, :]
    block[1:2, 128 : 128 + up_bias.shape[1]] = up_bias[...]


def spread_vectors(blocks, vectors):
    width = vectors.shape[1]
    devices = blocks.shape[0] // 8
    piece = width // devices
    table = blocks[...].astype(F32)
    vectors[...] = jnp.zeros_like(vectors)

    def put(rows, at, start):
        window = min(start // 128 * 128, width - 256)
        wide = jnp.concatenate([rows, jnp.zeros_like(rows)], 1)
        wide = pltpu.roll(wide, start - window, 1)
        vectors[at, window : window + 256] = vectors[at, window : window + 256] + wide

    for d in range(devices):
        block = table[8 * d : 8 * d + 8]
        put(block[:, :128], slice(0, 8), piece * d)
        put(block[0:1, 128:], slice(8, 9), piece * d)
        up = 4 * piece * d
        put(block[1:2, 128:], slice(9 + up // width, 10 + up // width), up % width)


def column_of(table, source, row):
    line = table[source, pl.ds(row, 1), :].astype(F32)
    tall = jnp.broadcast_to(line, (8, line.shape[1]))
    return jnp.concatenate([tall[:, n : n + 128].T[:, 0:1] for n in range(0, line.shape[1], 128)], 0)


def forward_kernel(
    deep,
    patches,
    cotangent,
    flags_in,
    clips_in,
    mask_embed,
    norm_gain,
    norm_shift,
    qv_bias,
    branch_bias,
    up_bias,
    shard_qkv,
    shard_out,
    shard_up,
    shard_down,
    o_qkv,
    o_out,
    o_up,
    o_down,
    o_small,
    o_x,
    o_cot,
    o_flags,
    o_first,
    o_q,
    o_k,
    o_v,
    o_mixed,
    o_second,
    o_rate,
    o_middle,
    o_act,
    o_slope,
    o_expon,
    o_result,
    w_qkv,
    w_out,
    w_up,
    w_down,
    j_qkv,
    j_out,
    j_up,
    j_down,
    j_vector,
    shard_vector,
    w_vector,
    small,
    x,
    flags_all,
    clips_all,
    first,
    q,
    k,
    v,
    mixed,
    second,
    rate,
    middle,
    expon,
    slope,
    result,
    q_code,
    k_code,
    join_sems,
    gather_sends,
    gather_recvs,
    row_sends,
    row_recvs,
    local_sems,
    expon_sems,
    act_sems,
):
    place = Place(deep)
    span, width = patches.shape[1:]
    rows = x.shape[0]
    sources = rows // span
    half = width // HEADS
    pairs = HEADS // 2
    inner = w_up.shape[1]
    chunks = inner // width

    fill_vectors(shard_vector, mask_embed, norm_gain, norm_shift, qv_bias, branch_bias, up_bias)
    place.enter()

    kinds = ((patches, x), (flags_in, flags_all), (clips_in, clips_all), (cotangent, o_cot))

    def landing(kind, source):
        dst = kinds[kind][1]
        if kind in (1, 2):
            return dst.at[source]
        return dst.at[pl.ds(pl.multiple_of(source * span, span), span)]

    def leaving(kind, to):
        src = kinds[kind][0]
        return src if kind in (1, 2) else src.at[to]

    def own_part(kind):
        return pltpu.make_async_copy(
            leaving(kind, place.tm), landing(kind, place.tm), local_sems.at[kind]
        )

    def row_copy(kind, step, to):
        return remote(
            leaving(kind, to),
            landing(kind, place.tm),
            row_sends.at[kind, step],
            row_recvs.at[kind, step],
            (place.batch, to),
        )

    def row_wait(kind, step):
        source = place.mate(step)
        there = landing(kind, source)
        remote(
            there, there, row_sends.at[kind, step], row_recvs.at[kind, step], (place.batch, source)
        ).wait_recv()

    zpq = Route(place, "zpq", True)
    zxy = Route(place, "zpq", False)
    pzq = Route(place, "pzq", True)
    xzy = Route(place, "pzq", False)
    named = {}
    for i, (name, route, shard, joined, full) in enumerate(
        (
            (VECTOR, zpq, shard_vector, j_vector, w_vector),
            (QKV, zxy, shard_qkv, j_qkv, w_qkv),
            (OUT, zpq, shard_out, j_out, w_out),
            (UP, zxy, shard_up, j_up, w_up),
            (DOWN, pzq, shard_down, j_down, w_down),
        )
    ):
        named[name] = Gather(
            place, route, shard, joined, full, join_sems.at[i], gather_sends.at[i], gather_recvs.at[i]
        )
    gathers = list(named.values())
    for gather in gathers:
        gather.join()
    def send_rows(kinds):
        for kind in kinds:
            for step in range(1, sources):
                row_copy(kind, step, place.mate(step)).start()

    def run(steps):
        for what, *which in steps:
            if what == ROWS:
                send_rows((1, 2, 0))
            elif what == COTANGENT:
                send_rows((3,))
            elif what == SPREAD:
                spread_vectors(w_vector, small)
            elif what == FIRST:
                named[which[0]].first()
            elif what == FINISH:
                named[which[0]].finish()
            else:
                named[which[0]].stage(which[1], slice(which[2], which[3]))

    def after(loop, index):
        for when, steps in FORWARD_STEPS.get(loop, {}).items():
            if isinstance(index, int):
                if index == when:
                    run(steps)
            else:
                pl.when(index == when)(functools.partial(run, steps))

    for kind in (1, 2, 0):
        own_part(kind).start()
    run(FORWARD_STEPS[START][0])
    keeping = []

    def keep(src, dst):
        copy = pltpu.make_async_copy(src, dst, local_sems.at[4 + len(keeping)])
        copy.start()
        keeping.append(copy)


    vectors = small
    lane = lax.broadcasted_iota(jnp.int32, (1, 2 * half), 1)
    low = lane < half
    own_lanes = [low.astype(F32), 1.0 - low.astype(F32)]

    for kind in (1, 2, 0):
        own_part(kind).wait()

    @pl.loop(0, sources)
    def _(step):
        @pl.when(step > 0)
        def _():
            for kind in (1, 2, 0):
                row_wait(kind, step)

        source = place.mate(step)
        at = pl.ds(pl.multiple_of(source * span, span), span)
        flags = column_of(flags_all, source, place.tm)
        clips = column_of(clips_all, source, place.tm)
        start = jnp.where(flags == 1.0, vectors[0:1, :], x[at, :].astype(F32))
        middle[at, :] = start
        center, speed = moments(start)
        normed = (center * speed * vectors[1:2, :] + vectors[3:4, :]).astype(BF)
        first[at, :] = normed
        q[at, :] = (nn(normed, w_qkv[:, 0:width]) + vectors[5:6, :]).astype(BF) * (1.0 / math.sqrt(half))
        k[at, :] = nn(normed, w_qkv[:, width : 2 * width]).astype(BF)
        v[at, :] = (nn(normed, w_qkv[:, 2 * width :]) + vectors[6:7, :]).astype(BF)
        clip_lane = lax.broadcasted_iota(jnp.int32, (span, 2 * half), 1).astype(F32)
        for h in range(2):
            base = float(half * (1 - h))
            same = clip_lane - base == clips
            coded = jnp.logical_and(clip_lane >= base, clip_lane < base + 5.0)
            q_code[h, at, :] = jnp.where(same, 1.0, 0.0).astype(BF)
            k_code[h, at, :] = jnp.where(jnp.logical_and(coded, jnp.logical_not(same)), FAR, 0.0).astype(BF)
        after(PROJECT, step)

    for src, dst in ((w_qkv, o_qkv), (small, o_small), (x, o_x), (flags_all, o_flags), (first, o_first), (q, o_q), (k, o_k), (v, o_v)):
        keep(src, dst)

    block = min(rows, 512)

    def expon_copy(p):
        return pltpu.make_async_copy(expon.at[p % 2], o_expon.at[pl.ds(2 * p, 2)], expon_sems.at[p % 2])

    def attend(p):
        lanes = pl.ds(pl.multiple_of(p * 2 * half, 128), 2 * half)

        @pl.when(p >= 2)
        def _():
            expon_copy(p - 2).wait()

        slot = p % 2
        keys, values = [], []
        for h in range(2):
            mask = own_lanes[h].astype(BF)
            keys.append(k[:, lanes] * mask + k_code[h])
            values.append(v[:, lanes] * mask + own_lanes[1 - h].astype(BF))
        for part in range(rows // block):
            at = pl.ds(part * block, block)
            mixes = []
            for h in range(2):
                query = q[at, lanes] * own_lanes[h].astype(BF) + q_code[h, at, :]
                scores = nt(query, keys[h])
                peak = jnp.max(scores, -1, keepdims=True)
                weights = jnp.exp2((scores - peak) * LOG2E).astype(BF)
                expon[slot, h, at, :] = weights
                mixes.append(nn(weights, values[h]))
            top = jnp.where(low, mixes[0], mixes[1])
            totals = pltpu.roll(jnp.where(low, mixes[1], mixes[0]), half, 1)
            speed = 1.0 / totals
            rate[at, lanes] = speed
            mixed[at, lanes] = (top * speed).astype(BF)
        expon_copy(p).start()
        after(ATTEND, p)

    pl.loop(0, pairs)(attend)
    for src, dst in ((w_out, o_out), (w_up, o_up), (mixed, o_mixed), (rate, o_rate)):
        keep(src, dst)
    for p in (pairs - 2, pairs - 1):
        expon_copy(p).wait()

    def act(j, at):
        return expon.at[j // 2, j % 2, at, pl.ds(0, width)]

    def slope_copies(step):
        at = pl.ds(pl.multiple_of(step * span, span), span)
        return [
            pltpu.make_async_copy(slope.at[step % 2, j], o_slope.at[j, at], act_sems.at[step % 2, j])
            for j in range(chunks)
        ]

    def act_copies(step):
        at = pl.ds(pl.multiple_of(step * span, span), span)
        return [pltpu.make_async_copy(act(j, at), o_act.at[j, at], act_sems.at[2, j]) for j in range(chunks)]

    def rise(step):
        @pl.when(step >= 2)
        def _():
            for copy in slope_copies(step - 2):
                copy.wait()

        at = pl.ds(pl.multiple_of(step * span, span), span)
        hidden = middle[at, :] + nn(mixed[at, :], w_out[...]) + vectors[7:8, :]
        middle[at, :] = hidden
        center, speed = moments(hidden)
        normed = (center * speed * vectors[2:3, :] + vectors[4:5, :]).astype(BF)
        second[at, :] = normed
        for j in range(chunks):
            pre = nn(normed, w_up[:, j * width : (j + 1) * width]) + vectors[9 + j : 10 + j, :]
            value, steep = gelu_and_slope(pre)
            expon[j // 2, j % 2, at, 0:width] = value.astype(BF)
            slope[step % 2, j] = steep.astype(BF)
        for copy in slope_copies(step) + act_copies(step):
            copy.start()
        after(RISE, step)

    def fall(step):
        at = pl.ds(pl.multiple_of(step * span, span), span)
        total = middle[at, :] + vectors[8:9, :]
        for j in range(chunks):
            total = total + nn(expon[j // 2, j % 2, at, 0:width], w_down[j * width : (j + 1) * width, :])
        result[at, :] = total.astype(BF)

    pl.loop(0, sources)(rise)
    keep(second, o_second)
    keep(middle, o_middle)
    keep(w_down, o_down)
    pl.loop(0, sources)(fall)
    keep(result, o_result)
    for step in range(sources):
        for copy in act_copies(step):
            copy.wait()
    for step in (sources - 2, sources - 1):
        for copy in slope_copies(step):
            copy.wait()
    for step in range(1, sources):
        row_wait(3, step)
        for kind in range(4):
            row_copy(kind, step, place.mate(step)).wait_send()
    for copy in keeping:
        copy.wait()
    for gather in gathers:
        gather.drain()


def forward(deep, patches, cotangent, flags, clips, vectors, shards):
    sources, span, width = patches.shape
    qkv, out, up, down = shards
    rows = sources * span
    chips = deep * 4
    inner = up.shape[1]
    chunks = inner // width
    shape = jax.ShapeDtypeStruct
    fulls = [(2 * chips * s.shape[0], s.shape[1]) for s in shards]
    plane = (rows, width)
    outs = [shape(f, BF) for f in fulls]
    outs += [shape((16, width), F32), shape(plane, BF), shape(plane, BF)]
    outs += [shape((sources,) + flags.shape, jnp.int32)]
    outs += [shape(plane, BF)] * 6 + [shape(plane, F32)] * 2
    outs += [shape((chunks, rows, width), BF)] * 2
    outs += [shape((HEADS, rows, rows), BF), shape(plane, BF)]
    scratch = [pltpu.VMEM(f, BF) for f in fulls]
    scratch += [pltpu.VMEM((2 * s.shape[0], s.shape[1] // 2), F32) for s in shards]
    scratch += [
        pltpu.VMEM((16, 128), F32),
        pltpu.VMEM((8, 256), F32),
        pltpu.VMEM((16 * chips, 256), BF),
        pltpu.VMEM((16, width), F32),
        pltpu.VMEM(plane, BF),
        pltpu.VMEM((sources,) + flags.shape, jnp.int32),
        pltpu.VMEM((sources,) + flags.shape, jnp.int32),
    ]
    scratch += [pltpu.VMEM(plane, BF)] * 6 + [pltpu.VMEM(plane, F32)] * 2
    scratch += [
        pltpu.VMEM((2, 2, rows, rows), BF),
        pltpu.VMEM((2, chunks, span, width), BF),
        pltpu.VMEM(plane, BF),
        pltpu.VMEM((2, rows, 128), BF),
        pltpu.VMEM((2, rows, 128), BF),
    ]
    dma = pltpu.SemaphoreType.DMA
    scratch += [
        dma((5,)),
        dma((5, 1 + 2 * chips)),
        dma((5, 1 + 2 * chips)),
        dma((4, sources)),
        dma((4, sources)),
        dma((20,)),
        dma((2,)),
        dma((3, chunks)),
    ]
    return pl.pallas_call(
        functools.partial(forward_kernel, deep),
        out_shape=outs,
        in_specs=[HBM] * 4 + [pl.BlockSpec(memory_space=pltpu.VMEM)] * 6 + [HBM] * 4,
        out_specs=[HBM] * len(outs),
        scratch_shapes=scratch,
        compiler_params=pltpu.CompilerParams(
            collective_id=0, has_side_effects=True, vmem_limit_bytes=62 * 2**20
        ),
        name="forward",
    )(patches, cotangent, flags, clips, *vectors, *shards)


class Scatter:
    def __init__(self, place, route, held, slots, final, sends, recvs, piece=None):
        self.place, self.route = place, route
        self.held, self.slots, self.final = held, slots, final
        self.sends, self.recvs = sends, recvs
        self.rows = slots.shape[1]
        self.width = piece
        self.sent = []

    def region(self, shifts):
        return pl.ds(pl.multiple_of(self.route.chip(shifts) * self.rows, 16), self.rows)

    def columns(self, piece):
        if piece is None:
            return pl.ds(0, self.held.shape[1])
        return pl.ds(pl.multiple_of(piece * self.width, 128), self.width)

    def parts(self, stage):
        route = self.route
        for d in range(1, route.sizes[stage]):
            for earlier in route.offsets(stage):
                offset = list(earlier)
                offset[stage] = d
                yield d, [-o for o in earlier], route.index(offset) - 1

    def copy(self, stage, d, back, slot, piece):
        shifts, to = list(back), [0, 0, 0]
        shifts[stage] = to[stage] = d
        columns = self.columns(piece)
        n = 0 if piece is None else piece
        return remote(
            self.held.at[self.region(shifts), columns],
            self.slots.at[slot, :, columns],
            self.sends.at[n, slot],
            self.recvs.at[n, slot],
            self.route.device(to),
        )

    def send(self, stage, piece=None):
        self.sent.append((stage, piece))
        for d, back, slot in self.parts(stage):
            self.copy(stage, d, back, slot, piece).start()

    def add(self, stage, piece=None):
        found = {}
        columns = self.columns(piece)
        for d, back, slot in self.parts(stage):
            self.copy(stage, d, back, slot, piece).wait_recv()
            found.setdefault(tuple(back), []).append(slot)
        for back, slots in found.items():
            at = self.region(back)
            total = self.held[at, columns].astype(F32)
            for slot in slots:
                total = total + self.slots[slot, :, columns].astype(F32)
            if stage == 0:
                self.final[:, columns] = total
            else:
                self.held[at, columns] = total.astype(BF)

    def drain(self):
        for stage, piece in self.sent:
            for d, back, slot in self.parts(stage):
                self.copy(stage, d, back, slot, piece).wait_send()


class RowScatter(Scatter):
    def part_q(self, z, p):
        place = self.place
        behind = (place.z - z + place.deep) % place.deep
        return [p, (place.deep - behind) % place.deep, 0], (p * place.deep + behind) * 2

    def copy_q(self, z, p):
        shifts, slot = self.part_q(z, p)
        return self.copy(2, 1, shifts, slot, None)

    def send_q(self, z):
        for p in range(2):
            self.copy_q(z, p).start()

    def add_q(self, z):
        for p in range(2):
            shifts, slot = self.part_q(z, p)
            self.copy_q(z, p).wait_recv()
            at = self.region(shifts)
            self.held[at, :] = (self.held[at, :].astype(F32) + self.slots[slot].astype(F32)).astype(BF)

    def copy_z(self, z, p):
        place = self.place
        ahead = (z - place.z + place.deep) % place.deep
        return self.copy(1, ahead, [p, 0, 0], (p * place.deep + ahead) * 2 - 1, None)

    def send_z(self, z):
        @pl.when(self.place.z != z)
        def _():
            for p in range(2):
                self.copy_z(z, p).start()

    def drain(self):
        place = self.place
        for z in range(place.deep):
            for p in range(2):
                self.copy_q(z, p).wait_send()
        for d, back, slot in self.parts(1):
            self.copy(1, d, back, slot, None).wait_send()
        super().drain()


def backward_kernel(
    deep,
    i_qkv,
    i_out,
    i_up,
    i_down,
    i_small,
    i_x,
    i_cot,
    i_flags,
    i_first,
    i_q,
    i_k,
    i_v,
    i_mixed,
    i_second,
    i_rate,
    i_middle,
    i_act,
    i_slope,
    i_expon,
    i_result,
    i_own_cot,
    o_qkv,
    o_out,
    o_up,
    o_down,
    o_small,
    o_patch,
    o_result,
    w_qkv,
    w_out,
    w_up,
    w_down,
    upstream,
    second,
    gathered,
    middle,
    expon,
    score_grad,
    trio,
    rate,
    mixed,
    staged,
    h_qkv,
    h_out,
    h_up,
    h_down,
    s_qkv,
    s_out,
    s_up,
    s_down,
    f_qkv,
    f_out,
    f_up,
    f_down,
    vectors,
    flags_all,
    small,
    small_slots,
    patch,
    load_sems,
    chunk_sems,
    pair_sems,
    hand_sends,
    hand_recvs,
    scatter_sends,
    scatter_recvs,
    final_sends,
    final_recvs,
    small_sends,
    small_recvs,
    row_sends,
    row_recvs,
    local_sems,
):
    place = Place(deep)
    rows, width = upstream.shape
    sources, span = patch.shape[:2]
    half = width // HEADS
    pairs = HEADS // 2
    chunks = i_act.shape[0]
    part = width // 2
    first = second
    mixed_grad = upstream
    first_grad = gathered

    loads = [
        pltpu.make_async_copy(src, dst, load_sems.at[i])
        for i, (src, dst) in enumerate(
            (
                (i_second, second),
                (i_middle, middle),
                (i_small, vectors),
                (i_flags, flags_all),
                (i_out, w_out),
                (i_qkv, w_qkv),
            )
        )
    ]

    def chunk_loads(j):
        slot = j % 2
        columns = pl.ds(pl.multiple_of(j * width, 128), width)
        moves = (
            (i_down.at[columns], w_down.at[slot]),
            (i_up.at[:, columns], w_up.at[slot]),
            (i_act.at[j], expon.at[slot, 0, :, pl.ds(0, width)]),
            (i_slope.at[j], expon.at[slot, 1, :, pl.ds(0, width)]),
        )
        return [pltpu.make_async_copy(src, dst, chunk_sems.at[slot, n]) for n, (src, dst) in enumerate(moves)]

    def pair_loads(p):
        slot = p % 2
        lanes = pl.ds(pl.multiple_of(p * 2 * half, 128), 2 * half)
        moves = (
            (i_expon.at[pl.ds(2 * p, 2)], expon.at[slot]),
            (i_q.at[:, lanes], trio.at[slot, 0]),
            (i_k.at[:, lanes], trio.at[slot, 1]),
            (i_v.at[:, lanes], trio.at[slot, 2]),
            (i_rate.at[:, lanes], rate.at[slot]),
            (i_mixed.at[:, lanes], mixed.at[slot]),
        )
        return [pltpu.make_async_copy(src, dst, pair_sems.at[slot, n]) for n, (src, dst) in enumerate(moves)]

    for step in range(sources):
        source = place.mate(step)
        at = pl.ds(pl.multiple_of(source * span, span), span)
        loads.insert(
            step,
            pltpu.make_async_copy(
                i_own_cot.at[place.tm] if step == 0 else i_cot.at[at], upstream.at[at], load_sems.at[6 + step]
            ),
        )
    early = sources + 1
    for copy in loads[:early] + chunk_loads(0) + loads[early:]:
        copy.start()
    place.enter()

    def result_copy(step):
        to = place.mate(step)
        return remote(
            i_result.at[pl.ds(pl.multiple_of(to * span, span), span)],
            o_result.at[place.tm],
            row_sends.at[1, step],
            row_recvs.at[1, step],
            (place.batch, to),
        )

    result_in = pltpu.make_async_copy(
        i_result.at[pl.ds(pl.multiple_of(place.tm * span, span), span)], patch.at[sources - 1], local_sems.at[5]
    )
    result_in.start()
    result_out = pltpu.make_async_copy(patch.at[sources - 1], o_result.at[place.tm], local_sems.at[5])
    for step in range(1, sources):
        result_copy(step).start()

    zpq = Route(place, "zpq", True)
    pzq = Route(place, "pzq", True)
    xzy = Route(place, "pzq", False)
    zxy = Route(place, "zpq", False)
    by_qkv = Scatter(place, xzy, h_qkv, s_qkv, f_qkv, scatter_sends.at[0], scatter_recvs.at[0], part)
    by_out = Scatter(place, zxy, h_out, s_out, f_out, scatter_sends.at[1], scatter_recvs.at[1], part)
    by_up = Scatter(place, zpq, h_up, s_up, f_up, scatter_sends.at[2], scatter_recvs.at[2], part)
    by_down = RowScatter(place, pzq, h_down, s_down, f_down, scatter_sends.at[3], scatter_recvs.at[3])
    scatters = [by_qkv, by_out, by_up, by_down]

    def columns(c):
        return pl.ds(pl.multiple_of(c * part, 128), part)

    def hand(slot, held, n):
        return remote(
            staged.at[slot, :, columns(1 - place.c)],
            held,
            hand_sends.at[n],
            hand_recvs.at[n],
            place.device(c=1 - place.c),
        )

    def settle(slot, held, n):
        copy = hand(slot, held, n)
        copy.wait_recv()
        held[...] = (held[...].astype(F32) + staged[slot, :, columns(place.c)].astype(F32)).astype(BF)
        copy.wait_send()

    def down_chunk(j):
        return (2 * (j % 2), h_down.at[pl.ds(pl.multiple_of(j * width, 128), width)], j)

    def up_chunk(j):
        return (2 * (j % 2) + 1, h_up.at[:, pl.ds(pl.multiple_of(j * part, 128), part)], chunks + j)

    def qkv_chunk(i):
        return (1 + i, h_qkv.at[:, pl.ds(pl.multiple_of(i * part, 128), part)], 2 * chunks + 1 + i)

    def out_chunk(i):
        return (0, h_out, 2 * chunks)

    named = {
        QKV: (by_qkv, qkv_chunk),
        OUT: (by_out, out_chunk),
        UP: (by_up, up_chunk),
        DOWN: (by_down, down_chunk),
    }
    summed = VectorSum(place, small, small_slots, small_sends, small_recvs)

    def run(steps):
        for what, *which in steps:
            if what == VECTOR_SEND:
                summed.send(which[0])
            elif what == VECTOR_ADD:
                summed.add(which[0])
            elif what == TURN:
                by_down.add_q(which[0])
                by_down.send_z(which[0])
            elif what == DELIVER:
                deliver(*deliveries[which[0]])
            elif what == SETTLE:
                scatter, chunk = named[which[0]]
                settle(*chunk(which[1]))
                if scatter is by_down:
                    scatter.send_q(which[1])
                else:
                    scatter.send(2, which[1])
            else:
                scatter = named[which[0]][0]
                stage = which[1]
                piece = None if scatter is by_down else which[2]
                scatter.add(stage, piece)
                if stage > 0:
                    scatter.send(stage - 1, piece)

    def after(loop, index):
        for when, steps in BACKWARD_STEPS.get(loop, {}).items():
            if isinstance(index, int):
                if index == when:
                    run(steps)
            else:
                pl.when(index == when)(functools.partial(run, steps))

    for copy in loads[:early]:
        copy.wait()

    def feed(j):
        @pl.when(j < chunks - 1)
        def _():
            for copy in chunk_loads(j + 1):
                copy.start()

        for copy in chunk_loads(j):
            copy.wait()
        slot = j % 2
        act_grad = nt(upstream[...], w_down[slot]).astype(BF).astype(F32)
        pre_grad = (act_grad * expon[slot, 1, :, 0:width].astype(F32)).astype(BF)
        small[0, pl.ds(9 + j, 1), :] = column_sum(pre_grad.astype(F32))
        staged[down_chunk(j)[0]] = tn(expon[slot, 0, :, 0:width], upstream[...]).astype(BF)
        hand(*down_chunk(j)).start()
        staged[up_chunk(j)[0]] = tn(second[...], pre_grad).astype(BF)
        hand(*up_chunk(j)).start()
        grown = nt(pre_grad, w_up[slot])

        gathered[...] = gathered[...] + grown

        after(FEED, j)

    gathered[...] = jnp.zeros_like(gathered)
    pl.loop(0, chunks)(feed)
    whole_mixed = pltpu.make_async_copy(i_mixed, expon.at[1, 1, :, pl.ds(0, width)], local_sems.at[0])
    whole_mixed.start()
    for copy in pair_loads(0):
        copy.start()
    load_first = pltpu.make_async_copy(i_first, first, local_sems.at[1])
    load_first.start()
    for copy in loads[early:]:
        copy.wait()
    for row in (0, 1, 2, 3, 4, 5, 6, 7, 8, 13, 14, 15):
        small[0, row : row + 1, :] = jnp.zeros((1, width), F32)

    def bend(n):
        at = pl.ds(pl.multiple_of(n * span, span), span)
        center, speed = moments(middle[at, :])
        normed = center * speed
        grad = gathered[at, :]
        small[0, 2:3, :] = small[0, 2:3, :] + column_sum(grad * normed)
        small[0, 4:5, :] = small[0, 4:5, :] + column_sum(grad)
        above = upstream[at, :].astype(F32)
        small[0, 8:9, :] = small[0, 8:9, :] + column_sum(above)
        total = above + norm_back(normed, speed, vectors[2:3, :], grad)
        middle[at, :] = total
        low_total = total.astype(BF)
        small[0, 7:8, :] = small[0, 7:8, :] + column_sum(low_total.astype(F32))
        mixed_grad[at, :] = nt(low_total, w_out[...]).astype(BF)

    pl.loop(0, sources)(bend)
    after(BEND, 0)
    whole_mixed.wait()
    staged[0] = tn(expon[1, 1, :, 0:width], middle[...].astype(BF)).astype(BF)
    hand(*out_chunk(0)).start()
    after(MIX, 0)
    load_first.wait()
    result_in.wait()
    result_out.start()

    lane = lax.broadcasted_iota(jnp.int32, (1, 2 * half), 1)
    low = lane < half
    own_lanes = [low.astype(F32), 1.0 - low.astype(F32)]
    block = min(rows, 512)

    def attend(p):
        slot = p % 2
        lanes = pl.ds(pl.multiple_of(p * 2 * half, 128), 2 * half)

        @pl.when(p < pairs - 1)
        def _():
            for copy in pair_loads(p + 1):
                copy.start()

        pl.when(p == pairs - 1)(lambda: load_x.start())

        for copy in pair_loads(p):
            copy.wait()
        scaled = (mixed_grad[:, lanes].astype(F32) * rate[slot]).astype(BF)
        product = scaled.astype(F32) * mixed[slot].astype(F32)
        query, key, value = trio[slot, 0], trio[slot, 1], trio[slot, 2]
        key_grads, value_grads, query_grads = [], [], []
        for h in range(2):
            inner = jnp.sum(product * own_lanes[h], -1, keepdims=True)
            lone = scaled * own_lanes[h].astype(BF)
            query_parts = []
            for n in range(rows // block):
                at = slice(n * block, (n + 1) * block)
                grad = nt(lone[at], value)
                weights = expon[slot, h, at, :].astype(F32)
                grad = (weights * (grad - inner[at])).astype(BF)
                score_grad[h, at, :] = grad
                query_parts.append(nn(grad, key))
            query_grads.append(jnp.concatenate(query_parts, 0))
            key_grads.append(tn(query, score_grad[h]))
            value_grads.append(tn(scaled, expon[slot, h]))
        query_grad = (jnp.where(low, query_grads[0], query_grads[1]) * (1.0 / math.sqrt(half))).astype(BF)
        key_grad = jnp.concatenate([key_grads[0][:half], key_grads[1][half:]], 0).T.astype(BF)
        value_grad = jnp.concatenate([value_grads[0][:half], value_grads[1][half:]], 0).T.astype(BF)
        small[0, 5:6, lanes] = column_sum(query_grad.astype(F32))
        small[0, 6:7, lanes] = column_sum(value_grad.astype(F32))
        grads = jnp.concatenate([query_grad, key_grad, value_grad], 1)
        where = pl.ds(pl.multiple_of(slot * part, 128), part)
        staged[1 + p // 2, :, where] = tn(first[...], grads).astype(BF)
        weight = jnp.concatenate(
            [w_qkv[:, pl.ds(pl.multiple_of(p * 2 * half + n * width, 128), 2 * half)] for n in range(3)], 1
        )
        grown = nt(grads, weight)

        first_grad[...] = first_grad[...] + grown

        @pl.when(p % 2 == 1)
        def _():
            hand(*qkv_chunk(p // 2)).start()

        after(ATTEND, p)

    load_x = pltpu.make_async_copy(i_x, expon.at[0, 0, :, pl.ds(0, width)], local_sems.at[2])
    first_grad[...] = jnp.zeros_like(first_grad)
    pl.loop(0, pairs)(attend)
    load_x.wait()
    result_out.wait()

    def close(step):
        source = place.mate(sources - 1 - step)
        at = pl.ds(pl.multiple_of(source * span, span), span)
        flags = column_of(flags_all, source, place.tm) == 1.0
        start = jnp.where(flags, vectors[0:1, :], expon[0, 0, at, 0:width].astype(F32))
        center, speed = moments(start)
        normed = center * speed
        grad = first_grad[at, :]
        small[0, 1:2, :] = small[0, 1:2, :] + column_sum(grad * normed)
        small[0, 3:4, :] = small[0, 3:4, :] + column_sum(grad)
        total = middle[at, :] + norm_back(normed, speed, vectors[1:2, :], grad)
        small[0, 0:1, :] = small[0, 0:1, :] + column_sum(jnp.where(flags, total, 0.0))
        patch[step] = jnp.where(flags, 0.0, total).astype(BF)

        @pl.when(step < sources - 1)
        def _():
            remote(
                patch.at[step],
                o_patch.at[place.tm],
                row_sends.at[0, sources - 1 - step],
                row_recvs.at[0, sources - 1 - step],
                (place.batch, source),
            ).start()

        after(CLOSE, step)

    pl.loop(0, sources)(close)
    own_patch = pltpu.make_async_copy(patch.at[sources - 1], o_patch.at[place.tm], local_sems.at[3])
    own_patch.start()
    moves = []

    def deliver(final, target, pieces):
        shard = target.shape[0]
        for near, far, jump, size in pieces:
            to = pl.ds(pl.multiple_of(far + place.c * jump, 128), size)
            mine = pl.ds(pl.multiple_of(place.c * shard, 8), shard)
            theirs = pl.ds(pl.multiple_of((1 - place.c) * shard, 8), shard)
            n = len(moves) // 2
            moves.append(
                pltpu.make_async_copy(final.at[mine, pl.ds(near, size)], target.at[:, to], local_sems.at[6 + n])
            )
            moves.append(
                remote(
                    final.at[theirs, pl.ds(near, size)],
                    target.at[:, to],
                    final_sends.at[n],
                    final_recvs.at[n],
                    place.device(c=1 - place.c),
                )
            )
            moves[-2].start()
            moves[-1].start()

    deliveries = {
        DOWN: (f_down, o_down, [(0, 0, part, part)]),
        UP: (f_up, o_up, [(j * part, j * width, part, part) for j in range(chunks)]),
        OUT: (f_out, o_out, [(0, 0, part, part)]),
        QKV: (
            f_qkv,
            o_qkv,
            [
                (i * part + n * 2 * half, n * width + i * 4 * half, 2 * half, 2 * half)
                for i in range(3)
                for n in range(3)
            ],
        ),
    }
    after(TAIL, 0)
    own_small = pltpu.make_async_copy(small.at[4], o_small, local_sems.at[4])
    own_small.start()
    for move in moves:
        move.wait()
    for step in range(1, sources):
        copy = remote(
            patch.at[0], o_patch.at[place.mate(step)], row_sends.at[0, step], row_recvs.at[0, step], place.device()
        )
        copy.wait_recv()
        copy.wait_send()
        result_copy(step).wait()
    own_patch.wait()
    own_small.wait()
    for scatter in scatters:
        scatter.drain()


def backward(deep, saved, shards, cotangent):
    sources, span, width = cotangent.shape
    rows = sources * span
    chips = deep * 4
    chunks = shards[2].shape[1] // width
    shape = jax.ShapeDtypeStruct
    plane = (rows, width)
    small = saved[4]
    flags = saved[7]
    halves = [(2 * chips * s.shape[0], s.shape[1] // 2) for s in shards]
    outs = [shape(s.shape, F32) for s in shards] + [shape(small.shape, F32)] + [shape(cotangent.shape, BF)] * 2
    scratch = [
        pltpu.VMEM(saved[0].shape, BF),
        pltpu.VMEM(saved[1].shape, BF),
        pltpu.VMEM((2, width, width), BF),
        pltpu.VMEM((2, width, width), BF),
        pltpu.VMEM(plane, BF),
        pltpu.VMEM(plane, BF),
        pltpu.VMEM(plane, F32),
        pltpu.VMEM(plane, F32),
        pltpu.VMEM((2, 2, rows, rows), BF),
        pltpu.VMEM((2, rows, rows), BF),
        pltpu.VMEM((2, 3, rows, 2 * width // HEADS), BF),
        pltpu.VMEM((2, rows, 2 * width // HEADS), F32),
        pltpu.VMEM((2, rows, 2 * width // HEADS), BF),
        pltpu.VMEM((4, width, width), BF),
    ]
    scratch += [pltpu.VMEM(h, BF) for h in halves]
    scratch += [pltpu.VMEM((chips - 1, 2 * s.shape[0], s.shape[1] // 2), BF) for s in shards]
    scratch += [pltpu.VMEM((2 * s.shape[0], s.shape[1] // 2), F32) for s in shards]
    scratch += [
        pltpu.VMEM(small.shape, F32),
        pltpu.VMEM(flags.shape, jnp.int32),
        pltpu.VMEM((5,) + small.shape, F32),
        pltpu.VMEM((2 + deep,) + small.shape, F32),
        pltpu.VMEM(cotangent.shape, BF),
    ]
    dma = pltpu.SemaphoreType.DMA
    scratch += [
        dma((6 + sources,)),
        dma((2, 4)),
        dma((2, 6)),
        dma((2 * chunks + 4,)),
        dma((2 * chunks + 4,)),
        dma((4, chunks, chips - 1)),
        dma((4, chunks, chips - 1)),
        dma((11 + chunks,)),
        dma((11 + chunks,)),
        dma((2 + deep,)),
        dma((2 + deep,)),
        dma((2, sources)),
        dma((2, sources)),
        dma((17 + chunks,)),
    ]
    return pl.pallas_call(
        functools.partial(backward_kernel, deep),
        out_shape=outs,
        in_specs=[HBM] * (len(saved) + 1),
        out_specs=[HBM] * len(outs),
        scratch_shapes=scratch,
        compiler_params=pltpu.CompilerParams(
            collective_id=1, has_side_effects=True, vmem_limit_bytes=63 * 2**20
        ),
        name="backward",
    )(*saved, cotangent)


def finish_kernel(result, patch, sums, *refs):
    grads, outs = refs[:4], refs[4:]
    o_result, o_patch, embed, gain, shift, g_qkv, qv, g_out, branch, g_up, up, g_down = outs
    o_result[...] = result[...].astype(F32)
    o_patch[...] = patch[...].astype(F32)

    @pl.when(pl.program_id(0) == 0)
    def _():
        device = lax.axis_index("batch") * 4 + lax.axis_index("tm")
        width = sums.shape[1]
        piece, up_piece = embed.shape[1], up.shape[1]
        own = pltpu.roll(sums[...], lax.rem(width - device * piece, width), 1)
        row = 0
        for out in (embed, gain, shift, qv, branch):
            out[...] = own[row : row + out.shape[0], :piece]
            row += out.shape[0]
        lines = width // up_piece
        line = jnp.broadcast_to(sums[pl.ds(row + device // lines, 1), :], (8, width))
        at = lax.rem(width - lax.rem(device, lines) * up_piece, width)
        up[...] = pltpu.roll(line, at, 1)[0:1, :up_piece]
        for grad, out in zip(grads, (g_qkv, g_out, g_up, g_down)):
            out[...] = grad[...]


def finish(result, patch_grad, sums, grads, parts):
    sources, span, width = result.shape
    shape = jax.ShapeDtypeStruct
    rows = pl.BlockSpec((2, span, width), lambda i: (i, 0, 0))

    def whole(array):
        return pl.BlockSpec(array.shape, lambda i: (0, 0))

    vectors = [shape(p.shape, F32) for p in parts]
    embed, gain, shift, qv, branch, up = vectors
    outs = [embed, gain, shift, grads[0], qv, grads[1], branch, grads[2], up, grads[3]]
    outs = [shape(o.shape, F32) for o in outs]
    return pl.pallas_call(
        finish_kernel,
        grid=(sources // 2,),
        out_shape=[shape(result.shape, F32)] * 2 + outs,
        in_specs=[rows, rows, whole(sums)] + [whole(g) for g in grads],
        out_specs=[rows, rows] + [whole(o) for o in outs],
        name="finish",
    )(result, patch_grad, sums, *grads)


def by_rows(
    deep,
    patches,
    segment_ids,
    mask_flags,
    cotangent,
    mask_embed,
    norm_gain,
    norm_shift,
    qkv_weight,
    qv_bias,
    out_weight,
    branch_bias,
    up_weight,
    up_bias,
    down_weight,
):
    sources, span, width = patches.shape
    shards = (qkv_weight, out_weight, up_weight, down_weight)
    vectors = (mask_embed[None], norm_gain, norm_shift, qv_bias, branch_bias, up_bias[None])
    saved = forward(deep, patches, cotangent, mask_flags, segment_ids, vectors, shards)
    *grads, sums, patch_grad, result = backward(deep, saved, shards, cotangent)
    result, patch_grad, embed, gain, shift, g_qkv, qv, g_out, branch, g_up, up, g_down = finish(
        result, patch_grad, sums, grads, vectors
    )
    return result, patch_grad, embed[0], gain, shift, g_qkv, qv, g_out, branch, g_up, up[0], g_down


def layer_norm(hidden, gain, shift):
    center = hidden - jnp.mean(hidden, -1, keepdims=True)
    spread = jnp.mean(center * center, -1, keepdims=True)
    return center * lax.rsqrt(spread + EPS) * gain + shift


def gelu_exact(values):
    return jax.nn.gelu(values, approximate=False)


def outer_sum(left, right):
    return lax.dot_general(
        left, right, (((0,), (0,)), ((), ())), preferred_element_type=jnp.float32
    )


def back_product(grad, weight):
    return lax.dot_general(
        grad, weight, (((1,), (1,)), ((), ())), preferred_element_type=jnp.float32
    )


def by_patches(
    patches,
    segment_ids,
    mask_flags,
    cotangent,
    mask_embed,
    norm_gain,
    norm_shift,
    qkv_weight,
    qv_bias,
    out_weight,
    branch_bias,
    up_weight,
    up_bias,
    down_weight,
):
    rows, span, width = patches.shape
    head_dim = width // HEADS
    scale = 1.0 / math.sqrt(head_dim)
    count = rows * span
    block = min(rows, max(1, 512 // span))
    groups = rows // block
    (
        whole_embed,
        whole_gain,
        whole_shift,
        whole_qkv,
        whole_qvbias,
        whole_out,
        whole_bias,
        whole_up,
        whole_upbias,
        whole_down,
    ) = (
        lax.all_gather(mask_embed.astype(jnp.bfloat16), ("batch", "tm"), axis=0, tiled=True),
        lax.all_gather(norm_gain.astype(jnp.bfloat16), ("batch", "tm"), axis=1, tiled=True),
        lax.all_gather(norm_shift.astype(jnp.bfloat16), ("batch", "tm"), axis=1, tiled=True),
        lax.all_gather(qkv_weight.astype(jnp.bfloat16), ("batch", "tm"), axis=0, tiled=True),
        lax.all_gather(qv_bias.astype(jnp.bfloat16), ("batch", "tm"), axis=1, tiled=True),
        lax.all_gather(out_weight.astype(jnp.bfloat16), ("batch", "tm"), axis=0, tiled=True),
        lax.all_gather(branch_bias.astype(jnp.bfloat16), ("batch", "tm"), axis=1, tiled=True),
        lax.all_gather(up_weight.astype(jnp.bfloat16), ("batch", "tm"), axis=0, tiled=True),
        lax.all_gather(up_bias.astype(jnp.bfloat16), ("batch", "tm"), axis=0, tiled=True),
        lax.all_gather(down_weight.astype(jnp.bfloat16), ("batch", "tm"), axis=0, tiled=True),
    )
    gains = whole_gain.astype(jnp.float32)
    shifts = whole_shift.astype(jnp.float32)
    biases = whole_bias.astype(jnp.float32)
    qv_terms = whole_qvbias.astype(jnp.float32)
    masked = (mask_flags == 1)[..., None]
    start = jnp.where(masked, whole_embed.astype(jnp.float32), patches.astype(jnp.float32))
    first_in = layer_norm(start, gains[0], shifts[0]).astype(jnp.bfloat16).reshape(count, width)
    projected = jnp.dot(first_in, whole_qkv, preferred_element_type=jnp.float32)
    queries = (projected[:, :width] + qv_terms[0]).astype(jnp.bfloat16)
    keys_local = projected[:, width : 2 * width].astype(jnp.bfloat16)
    values_local = (projected[:, 2 * width :] + qv_terms[1]).astype(jnp.bfloat16)
    pairs = jnp.concatenate([keys_local, values_local], 1).reshape(rows, span, 2 * width)
    all_pairs, all_segments = (
        lax.all_gather(pairs, "tm", axis=1, tiled=True),
        lax.all_gather(segment_ids, "tm", axis=1, tiled=True),
    )
    total_keys = all_pairs.shape[1]
    query_blocks = queries.reshape(groups, block, span, width)
    pair_blocks = all_pairs.reshape(groups, block, total_keys, 2 * width)
    own_segments = segment_ids.reshape(groups, block, span)
    far_segments = all_segments.reshape(groups, block, total_keys)

    def masked_scores(query_blk, key_blk, query_seg, key_seg):
        lead = query_blk.shape[1]
        trail = key_blk.shape[1]
        query_heads = query_blk.reshape(block, lead, HEADS, head_dim)
        key_heads = key_blk.reshape(block, trail, HEADS, head_dim)
        scores = (
            jnp.einsum(
                "bqhd,bkhd->bhqk", query_heads, key_heads, preferred_element_type=jnp.float32
            )
            * scale
        )
        allowed = (query_seg[:, :, None] == key_seg[:, None, :])[:, None]
        return jnp.where(allowed, scores, FAR)

    def attend(items):
        query_blk, pair_blk, own_seg, far_seg = items
        scores = masked_scores(query_blk, pair_blk[..., :width], own_seg, far_seg)
        peak = jnp.max(scores, -1, keepdims=True)
        expon = jnp.exp(scores - peak)
        totals = jnp.sum(expon, -1, keepdims=True)
        probs_low = (expon / totals).astype(jnp.bfloat16)
        value_heads = pair_blk[..., width:].reshape(block, total_keys, HEADS, head_dim)
        mixed_blk = jnp.einsum(
            "bhqk,bkhd->bqhd", probs_low, value_heads, preferred_element_type=jnp.float32
        )
        return (mixed_blk.reshape(block, span, width), peak + jnp.log(totals))

    mixed, log_totals = lax.map(attend, (query_blocks, pair_blocks, own_segments, far_segments))
    mixed_low = mixed.reshape(count, width).astype(jnp.bfloat16)
    branch = jnp.dot(mixed_low, whole_out, preferred_element_type=jnp.float32) + biases[0]
    middle = start + branch.reshape(rows, span, width)
    second_in = layer_norm(middle, gains[1], shifts[1]).astype(jnp.bfloat16).reshape(count, width)
    hidden_pre = jnp.dot(
        second_in, whole_up, preferred_element_type=jnp.float32
    ) + whole_upbias.astype(jnp.float32)
    hidden_act = gelu_exact(hidden_pre).astype(jnp.bfloat16)
    result = jnp.dot(hidden_act, whole_down, preferred_element_type=jnp.float32) + biases[1]
    output = middle + result.reshape(rows, span, width)
    back_qkv, back_out, back_up, back_down = (
        lax.all_gather(qkv_weight.astype(jnp.bfloat16), ("batch", "tm"), axis=0, tiled=True),
        lax.all_gather(out_weight.astype(jnp.bfloat16), ("batch", "tm"), axis=0, tiled=True),
        lax.all_gather(up_weight.astype(jnp.bfloat16), ("batch", "tm"), axis=0, tiled=True),
        lax.all_gather(down_weight.astype(jnp.bfloat16), ("batch", "tm"), axis=0, tiled=True),
    )
    upstream = cotangent.astype(jnp.float32)
    result_grad = upstream.reshape(count, width).astype(jnp.bfloat16)
    down_bias_grad = jnp.sum(result_grad.astype(jnp.float32), 0)
    down_weight_grad = outer_sum(hidden_act, result_grad)
    act_grad = back_product(result_grad, back_down).astype(jnp.bfloat16)
    gelu_pull = jax.vjp(gelu_exact, hidden_pre)[1]
    pre_grad = gelu_pull(act_grad.astype(jnp.float32))[0].astype(jnp.bfloat16)
    up_bias_grad = jnp.sum(pre_grad.astype(jnp.float32), 0)
    up_weight_grad = outer_sum(second_in, pre_grad)
    second_grad = back_product(pre_grad, back_up).reshape(rows, span, width)
    norm_pull_two = jax.vjp(layer_norm, middle, gains[1], shifts[1])[1]
    middle_norm_grad, gain_two_grad, shift_two_grad = norm_pull_two(second_grad)
    middle_grad = upstream + middle_norm_grad
    branch_grad = middle_grad.reshape(count, width).astype(jnp.bfloat16)
    out_bias_grad = jnp.sum(branch_grad.astype(jnp.float32), 0)
    out_weight_grad = outer_sum(mixed_low, branch_grad)
    mixed_grad = back_product(branch_grad, back_out).astype(jnp.bfloat16)
    mixed_blocks = mixed_grad.reshape(groups, block, span, width)

    def query_back(items):
        query_blk, pair_blk, own_seg, far_seg, log_total, grad_blk = items
        scores = masked_scores(query_blk, pair_blk[..., :width], own_seg, far_seg)
        probs = jnp.exp(scores - log_total)
        probs_low = probs.astype(jnp.bfloat16)
        query_heads = query_blk.reshape(block, span, HEADS, head_dim)
        key_heads = pair_blk[..., :width].reshape(block, total_keys, HEADS, head_dim)
        value_heads = pair_blk[..., width:].reshape(block, total_keys, HEADS, head_dim)
        grad_heads = grad_blk.reshape(block, span, HEADS, head_dim)
        prob_grad = jnp.einsum(
            "bqhd,bkhd->bhqk", grad_heads, value_heads, preferred_element_type=jnp.float32
        )
        inner = jnp.sum(probs * prob_grad, -1, keepdims=True)
        score_grad = (probs * (prob_grad - inner)).astype(jnp.bfloat16)
        query_grad = (
            jnp.einsum("bhqk,bkhd->bqhd", score_grad, key_heads, preferred_element_type=jnp.float32)
            * scale
        )
        key_grad = (
            jnp.einsum(
                "bhqk,bqhd->bkhd", score_grad, query_heads, preferred_element_type=jnp.float32
            )
            * scale
        )
        value_grad = jnp.einsum(
            "bhqk,bqhd->bkhd", probs_low, grad_heads, preferred_element_type=jnp.float32
        )
        pair_grad = jnp.concatenate(
            [
                key_grad.reshape(block, total_keys, width),
                value_grad.reshape(block, total_keys, width),
            ],
            -1,
        )
        return (query_grad.reshape(block, span, width), pair_grad, inner)

    query_grads, pair_grads, unused_inner = lax.map(
        query_back,
        (query_blocks, pair_blocks, own_segments, far_segments, log_totals, mixed_blocks),
    )
    pair_grads = pair_grads.reshape(rows, total_keys, 2 * width)
    local_pair_grads = lax.psum_scatter(pair_grads, "tm", scatter_dimension=1, tiled=True).astype(
        jnp.bfloat16
    )
    query_low = query_grads.reshape(count, width).astype(jnp.bfloat16)
    local_pair_grads = local_pair_grads.reshape(count, 2 * width)
    qkv_grad = jnp.concatenate([query_low, local_pair_grads], 1)
    qkv_weight_grad = outer_sum(first_in, qkv_grad)
    qv_bias_grad = jnp.stack(
        [
            jnp.sum(query_low.astype(jnp.float32), 0),
            jnp.sum(local_pair_grads[:, width:].astype(jnp.float32), 0),
        ]
    )
    first_grad = back_product(qkv_grad, back_qkv).reshape(rows, span, width)
    norm_pull_one = jax.vjp(layer_norm, start, gains[0], shifts[0])[1]
    start_norm_grad, gain_one_grad, shift_one_grad = norm_pull_one(first_grad)
    start_grad = middle_grad + start_norm_grad
    embed_grad = jnp.sum(jnp.where(masked, start_grad, 0.0), (0, 1))
    patch_grad = jnp.where(masked, 0.0, start_grad)
    (
        embed_sum,
        gain_sum,
        shift_sum,
        qkv_sum,
        qv_sum,
        out_sum,
        branch_sum,
        up_sum,
        up_bias_sum,
        down_sum,
    ) = (
        lax.psum_scatter(embed_grad, ("batch", "tm"), scatter_dimension=0, tiled=True),
        lax.psum_scatter(
            jnp.stack([gain_one_grad, gain_two_grad]),
            ("batch", "tm"),
            scatter_dimension=1,
            tiled=True,
        ),
        lax.psum_scatter(
            jnp.stack([shift_one_grad, shift_two_grad]),
            ("batch", "tm"),
            scatter_dimension=1,
            tiled=True,
        ),
        lax.psum_scatter(qkv_weight_grad, ("batch", "tm"), scatter_dimension=0, tiled=True),
        lax.psum_scatter(qv_bias_grad, ("batch", "tm"), scatter_dimension=1, tiled=True),
        lax.psum_scatter(out_weight_grad, ("batch", "tm"), scatter_dimension=0, tiled=True),
        lax.psum_scatter(
            jnp.stack([out_bias_grad, down_bias_grad]),
            ("batch", "tm"),
            scatter_dimension=1,
            tiled=True,
        ),
        lax.psum_scatter(up_weight_grad, ("batch", "tm"), scatter_dimension=0, tiled=True),
        lax.psum_scatter(up_bias_grad, ("batch", "tm"), scatter_dimension=0, tiled=True),
        lax.psum_scatter(down_weight_grad, ("batch", "tm"), scatter_dimension=0, tiled=True),
    )
    return (
        output,
        patch_grad,
        embed_sum,
        gain_sum,
        shift_sum,
        qkv_sum,
        qv_sum,
        out_sum,
        branch_sum,
        up_sum,
        up_bias_sum,
        down_sum,
    )


def solution(mesh):
    wide, deep = mesh.shape["batch"] * mesh.shape["tm"], mesh.shape["batch"] // 2

    def on_device(patches, *rest):
        width = patches.shape[-1]
        fits = mesh.shape["tm"] == patches.shape[0] == 4 and width % (8 * wide) == 0 and patches.shape[1] == 256
        return by_rows(deep, patches, *rest) if fits else by_patches(patches, *rest)

    return jax.shard_map(
        on_device,
        mesh=mesh,
        in_specs=(
            P("batch", "tm", None),
            P("batch", "tm"),
            P("batch", "tm"),
            P("batch", "tm", None),
            P(("batch", "tm")),
            P(None, ("batch", "tm")),
            P(None, ("batch", "tm")),
            P(("batch", "tm"), None),
            P(None, ("batch", "tm")),
            P(("batch", "tm"), None),
            P(None, ("batch", "tm")),
            P(("batch", "tm"), None),
            P(("batch", "tm")),
            P(("batch", "tm"), None),
        ),
        out_specs=(
            P("batch", "tm", None),
            P("batch", "tm", None),
            P(("batch", "tm")),
            P(None, ("batch", "tm")),
            P(None, ("batch", "tm")),
            P(("batch", "tm"), None),
            P(None, ("batch", "tm")),
            P(("batch", "tm"), None),
            P(None, ("batch", "tm")),
            P(("batch", "tm"), None),
            P(("batch", "tm")),
            P(("batch", "tm"), None),
        ),
        check_vma=False,
    )
```
